128 devices in a mesh: dp: 16 (over y, z), head: 8 (over x, core).
Axes of the slice: x: 4, y: 4, z: 4, core: 2. Of those that a mesh axis runs over, the one named last changes fastest.
Arguments:
- queries: bfloat16 [768, 128, 576], P('dp', 'head'), may hold values from -48 to 48
- kv_pool: bfloat16 [2048, 64, 576], P('dp'), may hold values from -6.1 to 6.1
- page_table: int32 [256, 8], P('dp'), may hold values from 0 to 2047, as said below
- cache_len: int32 [256], P('dp'), may hold values from 1 to 509, as said below
- accepted: int32 [256], P('dp'), may hold values from 0 to 2
- w_uv: bfloat16 [128, 512, 128], P('head'), may hold values from -0.75 to 0.75
- w_o: bfloat16 [16384, 7168], P('head', 'dp'), may hold values from -0.125 to 0.125
- residual: bfloat16 [768, 7168], P('dp'), may hold values from -6 to 6
- norm_gain: float32 [7168], replicated, may hold values from 0.5 to 1.5
- expert_ids: int32 [768, 8], P('dp'), may hold values from 0 to 15, all different within a row; in each aligned block of 48 rows (0 to 47, 48 to 95, ...) at most 32 rows name the same one
- gate_weights: float32 [768, 8], P('dp'), may hold values from 0.1 to 0.5
- w_gate: bfloat16 [16, 7168, 2048], P('dp', None, 'head'), may hold values from -0.0625 to 0.0625
- w_up: bfloat16 [16, 7168, 2048], P('dp', None, 'head'), may hold values from -0.0625 to 0.0625
- w_down: bfloat16 [16, 2048, 7168], P('dp', 'head'), may hold values from -0.125 to 0.125
Outputs:
- attended: bfloat16 [768, 7168], P('dp')
- routed: bfloat16 [768, 7168], P('dp', 'head')
The draws below stay inside these ranges and needn't reach their ends.
Inputs may be any that keep to these rules, and one draw needn't show every extreme that they name: `page_table`: A global page number is a dp index times 128 plus one of that index's pages; no page serves two requests, and one request's pages lie on one dp index. On every dp index exactly 8 requests have their pages on other indices, each on a different one; among the indices that lend to index d are d + 1, d - 1 and d + 16 / 2 (modulo 16); every index lends to exactly 8 requests. cache_len + accepted is at most 509 for every request and equals it for some request in every draw. `expert_ids`: within the tokens of one dp index (aligned blocks of 48 rows) no expert is named more than 32 times.
All inputs are finite; a program needn't handle non-finite values.
Results may differ from the reference program's by a relative error of at most 0.035.
Values may be sent and summed in bfloat16 or wider, within the bound.
No kernel may reach another device: no remote copies, remote signals or barrier semaphores. Data moves between devices by JAX's collectives and lax.ppermute only.
A program may use at most 192 MiB of HBM per device.

```python
import math
import jax
import jax.numpy as jnp
import numpy as np
from jax import lax

D = 7168
H = 128
LAT = 512
VHEAD = 128
TOPK = 8
MOE_FF = 2048
PAGE = 64
R_DEV = 16
PPR = 8
MIG = 8
L = 512
P_DEV = 128
POOL = 2048
REQS = 256
ROWS_DP = 48
TOKENS = 768
KVW = 576
EXPERTS = 16
CAP = 32
N_DP = 16
N_HEAD = 8


def draw_queries(key, part):
    base = jax.random.fold_in(key, 404)
    first = jax.random.fold_in(base, 0)
    whole = jnp.clip(jax.random.normal(first, (TOKENS, H, KVW), jnp.float32), -6.0, 6.0)
    return whole.astype(jnp.bfloat16)


def draw_kv_pool(key, part):
    base = jax.random.fold_in(key, 505)
    first = jax.random.fold_in(base, 0)
    whole = jnp.clip(jax.random.normal(first, (POOL, PAGE, KVW), jnp.float32), -6.0, 6.0)
    return whole.astype(jnp.bfloat16)


def length_pair(key):
    base = jax.random.fold_in(key, 606)
    first, second, third, fourth = jax.random.split(base, 4)
    ceiling = jax.random.randint(first, (N_DP, 1), L // 4, L - 2)
    taken = jax.random.randint(second, (N_DP, R_DEV), 0, 3)
    spread = jax.random.randint(third, (N_DP, R_DEV), 0, 2 ** 30)
    committed = 1 + spread % (ceiling - taken)
    chosen = jax.random.randint(fourth, (), 0, N_DP * R_DEV)
    position = jnp.arange(N_DP * R_DEV).reshape(N_DP, R_DEV)
    taken = jnp.where(position == chosen, 2, taken)
    committed = jnp.where(position == chosen, L - 5, committed)
    return (committed.reshape(-1).astype(jnp.int32), taken.reshape(-1).astype(jnp.int32))


def draw_cache_len(key, part):
    return length_pair(key)[0]


def draw_accepted(key, part):
    return length_pair(key)[1]


def draw_page_table(key, part):
    base = jax.random.fold_in(key, 707)
    first, second, third = jax.random.split(base, 3)
    fixed = jnp.stack([jnp.int32(1), jnp.int32(N_DP - 1), jnp.int32(N_DP // 2)])
    candidates = jnp.arange(1, N_DP, dtype=jnp.int32)
    shuffled = jax.random.permutation(first, N_DP - 1).astype(jnp.int32)
    is_fixed = jnp.any(candidates[:, None] == fixed[None, :], axis=1)
    scores = jnp.where(is_fixed, N_DP + shuffled, shuffled)
    order = jnp.argsort(scores, stable=True)
    others = candidates[order][:MIG - 3]
    offsets = jnp.concatenate([fixed, others])
    slot_keys = jax.random.split(second, N_DP)
    picks = jax.vmap(lambda one: jax.random.permutation(one, R_DEV)[:MIG])(slot_keys).astype(jnp.int32)
    page_keys = jax.random.split(third, N_DP)
    page_order = jax.vmap(lambda one: jax.random.permutation(one, P_DEV))(page_keys).astype(jnp.int32)
    device = jnp.arange(N_DP, dtype=jnp.int32)[:, None]
    slot = jnp.arange(R_DEV, dtype=jnp.int32)[None, :]
    match = picks[:, :, None] == slot[:, None, :]
    is_moved = jnp.any(match, axis=1)
    which = jnp.sum(match.astype(jnp.int32) * jnp.arange(MIG, dtype=jnp.int32)[None, :, None], axis=1)
    lender = jnp.where(is_moved, (device + offsets[which]) % N_DP, device)
    group = jnp.where(is_moved, picks[lender, which], slot)
    within = group[:, :, None] * PPR + jnp.arange(PPR, dtype=jnp.int32)[None, None, :]
    local = page_order[lender[:, :, None], within]
    return (lender[:, :, None] * P_DEV + local).reshape(N_DP * R_DEV, PPR).astype(jnp.int32)


def block_levels(own_key, dims, cuts, smallest, top_value):
    gain = 1.0
    for axis_at, parts in cuts:
        heights = jax.random.uniform(jax.random.fold_in(jax.random.fold_in(own_key, 6), axis_at), (parts,), jnp.float32, smallest / len(cuts), top_value / len(cuts))
        gain = gain * jnp.repeat(jnp.exp(heights), dims[axis_at] // parts).reshape((-1,) + (1,) * (len(dims) - 1 - axis_at))
    return gain


def routed_block(own_key, own, number, rows, number_of, top, bound, lean):
    sequence = jax.random.permutation(own_key, number_of)
    packed, ordinary = shares(number_of, rows * top, bound, lean, True), shares(number_of, rows * top, bound, lean, False)
    places = jnp.arange(number_of)

    def named(sizes, offset_by):
        used = int((sizes > 0).sum())
        fixed = max(1, used // 4)
        moved = fixed + (places - fixed + offset_by * (used - fixed)) % max(1, number_of - fixed)
        return jnp.zeros((number_of,), jnp.int32).at[sequence[jnp.where(places < fixed, places, moved)]].set(jnp.asarray(sizes, jnp.int32))

    sizes = jnp.where(number % 4 == 0, named(packed, number // 4), named(ordinary, number - number // 4 - 1))
    mixed = jax.random.permutation(jax.random.fold_in(own, 3), number_of)
    donor, sink = mixed[0:number_of // 2 * 2:2], mixed[1:number_of // 2 * 2:2]
    margin = jnp.minimum(sizes[donor] - 1, bound - sizes[sink]) // 2
    margin = jnp.where((donor == sequence[0]) | (sink == sequence[0]) | (sizes[sink] == 0), 0, jnp.maximum(margin, 0))
    moved = jax.random.randint(jax.random.fold_in(own, 4), (number_of // 2,), 0, 1 << 20) % (margin + 1)
    sizes = sizes.at[donor].add(-moved).at[sink].add(moved)
    members = jnp.searchsorted(jnp.cumsum(sizes), jnp.arange(rows * top), side="right").astype(jnp.int32)
    grid = members.reshape(top, rows).T
    grid = grid[jax.random.permutation(jax.random.fold_in(own, 1), rows)]
    offset_by = jax.random.randint(jax.random.fold_in(own, 2), (rows, 1), 0, top)
    return jnp.take_along_axis(grid, (jnp.arange(top)[None, :] + offset_by) % top, axis=1)


def shares(amount, total, bound, skew, full):
    loads = [(1 << 20) // math.isqrt(rank ** skew) + 1 for rank in range(1, amount + 1)]
    largest = bound if full else min(bound, max(-(-total // amount), total * loads[0] // sum(loads)))
    least = 1 if total - largest >= amount - 1 else 0
    holding, spare = [largest] + [least] * (amount - 1), total - largest - least * (amount - 1)
    while spare > 0:
        free = [i for i in range(1, amount) if holding[i] < largest] or [i for i in range(1, amount) if holding[i] < bound]
        pool, remaining = sum([loads[i] for i in free]), spare
        for i in free:
            addition = min(bound - holding[i], max(1, remaining * loads[i] // pool), spare)
            holding[i] = holding[i] + addition
            spare = spare - addition
    return np.array(holding)


def normal_values(key, extent, scale, most, cuts=(), held_as=jnp.bfloat16):
    entries = jax.random.normal(key, extent, jnp.float32) * scale
    if len(cuts) > 0:
        entries = block_levels(key, extent, cuts, -0.22, 0.18) * entries
    return jnp.clip(entries, min=-most, max=most).astype(held_as)


def setup_inputs(seed: int = 0) -> dict:
    streams_of = jax.random.split(jax.random.key(seed), 15)
    queries = draw_queries(jax.random.fold_in(streams_of[14], 71), 0)
    kv_pool = draw_kv_pool(jax.random.fold_in(streams_of[14], 71), 0)
    page_table = draw_page_table(jax.random.fold_in(streams_of[14], 71), 0)
    cache_len = draw_cache_len(jax.random.fold_in(streams_of[14], 71), 0)
    accepted = draw_accepted(jax.random.fold_in(streams_of[14], 71), 0)
    w_uv = normal_values(streams_of[5], (H, LAT, VHEAD), (LAT // 8) ** -0.5, 0.75, ((0, 8),))
    w_o = normal_values(streams_of[6], (H * VHEAD, D), (H * VHEAD // 8) ** -0.5, 0.125, ((0, 8), (1, 16)))
    residual = normal_values(streams_of[7], (TOKENS, D), 1.0, 6.0, ((0, 16),))
    norm_gain = jnp.clip(1.0 + 0.1 * jax.random.normal(streams_of[8], (D,), jnp.float32), 0.5, 1.5)
    expert_ids_keys = jax.random.split(jax.random.fold_in(streams_of[9], 1), TOKENS // ROWS_DP)
    expert_ids_turns = jax.random.permutation(jax.random.fold_in(streams_of[9], 3), TOKENS // ROWS_DP)
    expert_ids = jax.vmap(lambda own, number: routed_block(jax.random.fold_in(streams_of[9], 2), own, number, ROWS_DP, EXPERTS, TOPK, CAP, 2))(expert_ids_keys, expert_ids_turns).reshape((TOKENS, TOPK))
    gate_weights = jnp.clip(0.1 + 0.4 * jax.random.uniform(streams_of[10], (TOKENS, TOPK), jnp.float32) ** block_levels(streams_of[10], (TOKENS, TOPK), ((0, 16),), -0.2, 0.2), 0.1, 0.5)
    w_gate = normal_values(streams_of[11], (EXPERTS, D, MOE_FF), D ** -0.5, 0.0625, ((0, 16), (2, 8)))
    w_up = normal_values(streams_of[12], (EXPERTS, D, MOE_FF), D ** -0.5, 0.0625, ((0, 16), (2, 8)))
    w_down = normal_values(streams_of[13], (EXPERTS, MOE_FF, D), MOE_FF ** -0.5, 0.125, ((0, 16), (1, 8)))
    return dict(queries=queries, kv_pool=kv_pool, page_table=page_table, cache_len=cache_len, accepted=accepted, w_uv=w_uv, w_o=w_o, residual=residual, norm_gain=norm_gain, expert_ids=expert_ids, gate_weights=gate_weights, w_gate=w_gate, w_up=w_up, w_down=w_down)


softmax_scale = 192.0 ** (-0.5)
norm_eps = 1e-06

def attend_rows(query_rows, key_rows, visible):
    scores = jnp.einsum('njhc,npc->njhp', query_rows.astype(jnp.float32), key_rows.astype(jnp.float32)) * softmax_scale
    position = jnp.arange(key_rows.shape[1], dtype=jnp.int32)
    drafts = jnp.arange(query_rows.shape[1], dtype=jnp.int32)
    allowed = position[None, None, None, :] <= visible[:, None, None, None] + drafts[None, :, None, None]
    highest = lax.optimization_barrier(jnp.max(jnp.where(allowed, scores, -1e+30), axis=-1, keepdims=True))
    weights = jnp.where(allowed, jnp.exp(jnp.where(allowed, scores - highest, 0.0)), 0.0)
    probs = (weights / lax.optimization_barrier(jnp.sum(weights, axis=-1, keepdims=True))).astype(jnp.bfloat16)
    latent = jnp.einsum('njhp,npc->njhc', probs.astype(jnp.float32), key_rows[:, :, :LAT].astype(jnp.float32))
    return latent.astype(jnp.bfloat16)

def reference(queries, kv_pool, page_table, cache_len, accepted, w_uv, w_o, residual, norm_gain, expert_ids, gate_weights, w_gate, w_up, w_down):
    query_rows = queries.reshape(REQS, 3, H, KVW)
    visible = cache_len + accepted

    def one_request(inputs):
        rows, pages, seen = inputs
        keys = kv_pool[pages].reshape(1, L, KVW)
        return attend_rows(rows[None], keys, seen[None])[0]
    latent = lax.map(one_request, (query_rows, page_table, visible)).reshape(TOKENS, H, LAT)
    values = jnp.einsum('thc,hcv->thv', latent.astype(jnp.float32), w_uv.astype(jnp.float32)).astype(jnp.bfloat16)
    attention = jnp.dot(values.reshape(TOKENS, H * VHEAD), w_o, preferred_element_type=jnp.float32)
    attended = (residual.astype(jnp.float32) + attention).astype(jnp.bfloat16)
    wide = attended.astype(jnp.float32)
    normed = (wide * lax.rsqrt(lax.optimization_barrier(jnp.mean(wide * wide, axis=-1, keepdims=True)) + norm_eps) * norm_gain).astype(jnp.bfloat16)
    flat_ids = expert_ids.reshape(N_DP, ROWS_DP * TOPK)
    member = (flat_ids[:, :, None] == jnp.arange(EXPERTS, dtype=jnp.int32)[None, None, :]).astype(jnp.int32)
    rank = lax.optimization_barrier(jnp.sum((jnp.cumsum(member, axis=1) - 1) * member, axis=2))
    blocks = jnp.arange(N_DP, dtype=jnp.int32)[:, None]
    slot_index = (flat_ids * (N_DP * CAP) + blocks * CAP + rank).reshape(-1).astype(jnp.int32)
    token_index = (blocks * ROWS_DP + jnp.arange(ROWS_DP * TOPK, dtype=jnp.int32)[None, :] // TOPK).reshape(-1).astype(jnp.int32)
    buffer = jnp.zeros((EXPERTS * N_DP * CAP, D), jnp.bfloat16).at[slot_index].set(normed[token_index])
    buffer = buffer.reshape(EXPERTS, N_DP * CAP, D)

    def expert_rows(inputs):
        rows, gate_matrix, up_matrix, down_matrix = inputs
        gate = jnp.dot(rows, gate_matrix, preferred_element_type=jnp.float32)
        up = jnp.dot(rows, up_matrix, preferred_element_type=jnp.float32)
        hidden = (jax.nn.silu(gate) * up).astype(jnp.bfloat16)
        sliced = hidden.reshape(rows.shape[0], N_HEAD, MOE_FF // N_HEAD).astype(jnp.float32)
        down_sliced = down_matrix.reshape(N_HEAD, MOE_FF // N_HEAD, D).astype(jnp.float32)
        pieces = jnp.einsum('rsf,sfd->rsd', sliced, down_sliced).astype(jnp.bfloat16)
        return lax.optimization_barrier(jnp.sum(pieces.astype(jnp.float32), axis=1))
    outputs = lax.map(expert_rows, (buffer, w_gate, w_up, w_down)).reshape(EXPERTS * N_DP * CAP, D)
    picked = outputs[slot_index].reshape(TOKENS, TOPK, D)
    routed = lax.optimization_barrier(jnp.sum(gate_weights[:, :, None] * picked, axis=1)).astype(jnp.bfloat16)
    return (attended, routed)
```

```python
import jax
import jax.numpy as jnp
from jax import lax
from jax.experimental import pallas as pl
from jax.experimental.pallas import tpu as pltpu
from jax.sharding import Mesh
from jax.sharding import PartitionSpec as P

LAT = 512
DP = ("y", "z")
HEAD = ("x", "core")
ALL = ("y", "z", "x", "core")
RING = 4
DP_N = 16
HEAD_N = 8
PAGES = 128
CAP = 32

softmax_scale = 192.0 ** (-0.5)
norm_eps = 1e-06
bf16 = jnp.bfloat16
f32 = jnp.float32
i32 = jnp.int32


def hop(array, axis, step):
    return lax.ppermute(array, axis, [((i + step) % RING, i) for i in range(RING)])


def send(array, axis, step):
    return lax.ppermute(array, axis, [(i, (i + step) % RING) for i in range(RING)])


def other_core(array):
    return lax.ppermute(array, "core", [(0, 1), (1, 0)])


def pack_kernel(pick_ref, query_ref, meta_ref, out_ref):
    width = query_ref.shape[2]

    def one(i, carry):
        out_ref[i, :, :width] = query_ref[pick_ref[i]]
        out_ref[i, :, width:] = meta_ref[i]
        return carry

    lax.fori_loop(0, out_ref.shape[0], one, 0)


def pack(pick, query_rows, meta):
    count, rows, width = query_rows.shape
    return pl.pallas_call(
        pack_kernel,
        out_shape=jax.ShapeDtypeStruct((DP_N, rows, width + meta.shape[2]), bf16),
        in_specs=[
            pl.BlockSpec(memory_space=pltpu.SMEM),
            pl.BlockSpec(memory_space=pltpu.VMEM),
            pl.BlockSpec(memory_space=pltpu.VMEM),
        ],
        out_specs=pl.BlockSpec(memory_space=pltpu.VMEM),
        compiler_params=pltpu.CompilerParams(vmem_limit_bytes=32 * 2**20),
        name="pack",
    )(pick, query_rows, meta)


def attend_kernel(pick_ref, page_ref, seen_ref, own_ref, far_ref, *refs):
    pages, out_ref = refs[:-1], refs[-1]
    step = pl.program_id(0)
    width = own_ref.shape[2]
    queries = jnp.where(step < 8, own_ref[0], far_ref[0, :, :width])
    keys = jnp.concatenate([page[0] for page in pages], axis=0)
    scores = (
        lax.dot_general(queries, keys, (((1,), (1,)), ((), ())), preferred_element_type=f32)
        * softmax_scale
    )
    position = lax.broadcasted_iota(i32, scores.shape, 1)
    draft = lax.broadcasted_iota(i32, scores.shape, 0) // (scores.shape[0] // 3)
    allowed = position <= seen_ref[step] + draft
    highest = jnp.max(jnp.where(allowed, scores, -1e30), axis=-1, keepdims=True)
    weights = jnp.where(allowed, jnp.exp(jnp.where(allowed, scores - highest, 0.0)), 0.0)
    probs = (weights / jnp.sum(weights, axis=-1, keepdims=True)).astype(bf16)
    out_ref[0] = lax.dot_general(
        probs, keys[:, :LAT], (((1,), (0,)), ((), ())), preferred_element_type=f32
    ).astype(bf16)


def attend(pick, pages, seen, own_queries, far_queries, kv_pool):
    count, rows, width = own_queries.shape
    page_rows = kv_pool.shape[1]
    per = pages.shape[1]

    def page_spec(a):
        return pl.BlockSpec(
            (1, page_rows, width), lambda i, pick, page, seen: (page[i * per + a], 0, 0)
        )

    spec = pltpu.PrefetchScalarGridSpec(
        num_scalar_prefetch=3,
        grid=(count,),
        in_specs=[
            pl.BlockSpec(
                (1, rows, width), lambda i, pick, page, seen: (pick[jnp.minimum(i, 7)], 0, 0)
            ),
            pl.BlockSpec(
                (1, rows, far_queries.shape[2]),
                lambda i, pick, page, seen: (pick[jnp.maximum(i, 8)], 0, 0),
            ),
        ]
        + [page_spec(a) for a in range(per)],
        out_specs=pl.BlockSpec((1, rows, LAT), lambda i, pick, page, seen: (i, 0, 0)),
    )
    return pl.pallas_call(
        attend_kernel,
        out_shape=jax.ShapeDtypeStruct((count, rows, LAT), bf16),
        grid_spec=spec,
        compiler_params=pltpu.CompilerParams(vmem_limit_bytes=32 * 2**20),
        cost_estimate=pl.CostEstimate(
            flops=count * rows * 512 * 1088 * 2, bytes_accessed=12_000_000, transcendentals=0
        ),
        name="attend",
    )(pick, pages.reshape(-1), seen, own_queries, far_queries, *([kv_pool] * per))


def before(count):
    at = jnp.arange(count, dtype=i32)
    return at[:, None] < at[None, :]


def shards(
    queries,
    kv_pool,
    page_table,
    cache_len,
    accepted,
    w_uv,
    w_o,
    residual,
    norm_gain,
    expert_ids,
    gate_weights,
    w_gate,
    w_up,
    w_down,
):
    at_x, at_y, at_z = lax.axis_index("x"), lax.axis_index("y"), lax.axis_index("z")
    at_core = lax.axis_index("core")
    dp_index = at_y * RING + at_z
    requests = page_table.shape[0]
    tokens, head_group, width = queries.shape
    query_rows = queries.reshape(requests, 3 * head_group, width)
    visible = cache_len + accepted
    lender = page_table[:, 0] // PAGES
    far = lender != dp_index
    dps = jnp.arange(DP_N, dtype=i32)

    lent_to = ((lender[None, :] == dps[:, None]) & far[None, :]).astype(i32)
    pick = jnp.sum(lent_to * jnp.arange(requests, dtype=i32)[None, :], axis=1)
    sent_pages = jnp.sum(lent_to[:, :, None] * (page_table - lender[:, None] * PAGES)[None], axis=1)
    sent_seen = jnp.sum(lent_to * visible[None, :], axis=1)
    sent_any = jnp.sum(lent_to, axis=1)
    line0 = jnp.concatenate(
        [
            sent_pages,
            (sent_seen // 2)[:, None],
            (sent_seen % 2)[:, None],
            sent_any[:, None],
            jnp.zeros((DP_N, 5), i32),
            jnp.broadcast_to(lender[None, :], (DP_N, requests)),
        ],
        axis=1,
    )
    ids_block = jnp.pad(expert_ids, ((0, 0), (0, 56)))
    line_block = jnp.pad(line0[:, None, :], ((0, 0), (0, tokens - 1), (8, 24)))
    meta = (ids_block[None] + line_block).astype(bf16)
    arrived = lax.all_to_all(pack(pick, query_rows, meta), DP, 0, 0, tiled=True)
    told = arrived[:, :, width:].astype(i32)
    all_ids = told[:, :, :8]
    told_pages = told[:, 0, 8:16]
    told_seen = told[:, 0, 16] * 2 + told[:, 0, 17]
    told_any = told[:, 0, 18]
    lenders = told[:, 0, 24:40]

    slots = jnp.arange(8, dtype=i32)
    own = 1 - far.astype(i32)
    own_rank = jnp.sum(before(requests) * own[:, None], axis=0)
    own_pick = ((own_rank[None, :] == slots[:, None]) & (own[None, :] > 0)).astype(i32)
    far_rank = jnp.sum(before(DP_N) * told_any[:, None], axis=0)
    far_pick = ((far_rank[None, :] == slots[:, None]) & (told_any[None, :] > 0)).astype(i32)
    which = jnp.concatenate([jnp.sum(own_pick * dps, axis=1), jnp.sum(far_pick * dps, axis=1)])
    held_pages = jnp.concatenate(
        [
            jnp.sum(own_pick[:, :, None] * (page_table - dp_index * PAGES)[None], axis=1),
            jnp.sum(far_pick[:, :, None] * told_pages[None], axis=1),
        ]
    )
    held_seen = jnp.concatenate(
        [jnp.sum(own_pick * visible, axis=1), jnp.sum(far_pick * told_seen, axis=1)]
    )
    latent = attend(which, held_pages, held_seen, query_rows, arrived, kv_pool)
    values = jnp.einsum(
        "thc,hcv->thv",
        latent.reshape(tokens, head_group, LAT),
        w_uv,
        preferred_element_type=f32,
    ).astype(bf16)
    values = values.reshape(tokens, head_group * w_uv.shape[2])

    half = values.shape[1] // 2

    def spread(block, first, second):
        line = jnp.concatenate([block] + [hop(block, first, k) for k in (1, 2, 3)], axis=0)
        return [line] + [hop(line, second, k) for k in (1, 2, 3)]

    zy = spread(values[:, :half], "z", "y")
    yz = spread(values[:, half:], "y", "z")
    part_zy = jnp.concatenate(
        [jnp.dot(a, w_o[:half], preferred_element_type=f32) for a in zy], axis=0
    )
    part_yz = jnp.concatenate(
        [jnp.dot(a, w_o[half:], preferred_element_type=f32) for a in yz], axis=0
    )
    columns = w_o.shape[1]
    part_yz = part_yz.reshape(RING, RING, tokens, columns).transpose(1, 0, 2, 3)
    projected = (part_zy + part_yz.reshape(-1, columns)).astype(bf16)

    is_own = (lenders == dps[:, None]).astype(i32)
    own_slot = jnp.sum(is_own[:, :, None] * before(requests)[None], axis=1)
    at_lender = (lenders[:, :, None] == dps[None, None, :]).astype(i32)
    away = at_lender * (dps[:, None, None] != dps[None, None, :])
    lends = jnp.sum(away, axis=1)
    lend_rank = jnp.sum(before(DP_N)[:, :, None] * lends[:, None, :], axis=0)
    far_slot = 8 + jnp.sum(at_lender * lend_rank[:, None, :], axis=2)
    slot = jnp.where(is_own > 0, own_slot, far_slot)
    turned = ((lenders // RING - at_y) % RING) * RING + (lenders % RING - at_z) % RING
    first_row = (turned * requests + slot) * 3
    source = (first_row[:, :, None] + jnp.arange(3, dtype=i32)).reshape(DP_N, RING, 2, -1)
    source = source.transpose(1, 2, 0, 3).reshape(RING, 2, -1)
    source = lax.dynamic_slice_in_dim(jnp.concatenate([source, source], 0), at_x, RING, 0)
    source = lax.dynamic_slice_in_dim(jnp.concatenate([source, source], 1), at_core, 2, 1)
    source = source.transpose(1, 0, 2).reshape(-1)
    rows_all = projected.shape[0]
    moves = (source[:, None] == jnp.arange(rows_all, dtype=i32)[None, :]).astype(bf16)
    homed = jnp.dot(moves, projected, preferred_element_type=f32)
    kept = homed[: rows_all // 2] + other_core(homed[rows_all // 2 :].astype(bf16)).astype(f32)
    kept = kept.reshape(RING, -1, columns)
    mine = kept[0]
    for k in (1, 2, 3):
        mine = mine + send(kept[k].astype(bf16), "x", k).astype(f32)
    share = tokens // HEAD_N
    mine = lax.all_to_all(
        mine.astype(bf16).reshape(DP_N, share, columns), DP, 0, 0, tiled=True
    )
    attention = mine.transpose(1, 0, 2).reshape(share, DP_N * columns)
    head_index = at_x * 2 + at_core
    near = lax.dynamic_slice_in_dim(residual, head_index * share, share, 0)
    attended_part = (near.astype(f32) + attention.astype(f32)).astype(bf16)
    wide = attended_part.astype(f32)
    normed = (
        wide * lax.rsqrt(jnp.mean(wide * wide, axis=-1, keepdims=True) + norm_eps) * norm_gain
    ).astype(bf16)
    padded = 8
    fill = ((0, padded - share), (0, 0))
    attended = lax.all_gather(jnp.pad(attended_part, fill), HEAD, axis=0, tiled=True)
    attended = attended.reshape(HEAD_N, padded, -1)[:, :share].reshape(tokens, -1)
    rows = lax.all_gather(jnp.pad(normed, fill), ALL, axis=0, tiled=True)

    gate = jnp.dot(rows, w_gate[0], preferred_element_type=f32)
    up = jnp.dot(rows, w_up[0], preferred_element_type=f32)
    hidden = (jax.nn.silu(gate) * up).astype(bf16)
    member = jnp.sum((all_ids == dp_index).astype(i32), axis=2)
    rank = jnp.sum(before(tokens)[None] * member[:, :, None], axis=1)
    place = jnp.where(member > 0, dps[:, None] * CAP + rank, -1)
    place = jnp.pad(
        place.reshape(DP_N, HEAD_N, share), ((0, 0), (0, 0), (0, padded - share)), constant_values=-1
    ).reshape(-1)
    slots_all = jnp.arange(DP_N * CAP, dtype=i32)
    placing = (slots_all[:, None] == place[None, :]).astype(bf16)
    hidden = jnp.dot(placing, hidden, preferred_element_type=f32).astype(bf16)
    width_out = w_down.shape[2] // HEAD_N
    down = w_down[0].reshape(-1, RING, 2, width_out)

    def piece(k, core):
        block = lax.dynamic_slice_in_dim(down, (at_x + k) % RING, 1, 1)
        block = lax.dynamic_slice_in_dim(block, core, 1, 2)
        return jnp.dot(hidden, block.reshape(-1, width_out), preferred_element_type=f32)

    total = None
    for k in (2, 1, 3, 0):
        there = other_core(piece(k, 1 - at_core).astype(bf16))
        both = piece(k, at_core) + there.astype(f32)
        if k:
            both = send(both.astype(bf16), "x", k).astype(f32)
        total = both if total is None else total + both
    total = total.astype(bf16).reshape(DP_N, CAP, width_out)
    returned = lax.all_to_all(total, DP, 0, 0, tiled=True).reshape(DP_N * CAP, width_out)
    chosen = (expert_ids[:, :, None] == dps[None, None, :]).astype(i32)
    named = jnp.sum(chosen, axis=1)
    weight = jnp.sum(chosen.astype(f32) * gate_weights[:, :, None], axis=1)
    my_rank = jnp.sum(before(tokens)[:, :, None] * named[:, None, :], axis=0)
    ranks = jnp.arange(CAP, dtype=i32)
    mix = jnp.where(my_rank[:, :, None] == ranks[None, None, :], weight[:, :, None], 0.0)
    mix = mix.reshape(tokens, DP_N * CAP)
    high = lax.reduce_precision(mix, 8, 7)
    both = jnp.concatenate([high.astype(bf16), (mix - high).astype(bf16)], axis=0)
    routed = jnp.dot(both, returned, preferred_element_type=f32)
    routed = (routed[:tokens] + routed[tokens:]).astype(bf16)
    return (attended, routed)


def solution(mesh):
    grid = Mesh(mesh.devices.reshape(RING, RING, RING, 2), ALL)
    return jax.shard_map(
        shards,
        mesh=grid,
        in_specs=(
            P(DP, HEAD, None),
            P(DP, None, None),
            P(DP, None),
            P(DP),
            P(DP),
            P(HEAD, None, None),
            P(HEAD, DP),
            P(DP, None),
            P(),
            P(DP, None),
            P(DP, None),
            P(DP, None, HEAD),
            P(DP, None, HEAD),
            P(DP, HEAD, None),
        ),
        out_specs=(P(DP, None), P(DP, HEAD)),
        check_vma=False,
    )
```

```python
import jax
import jax.numpy as jnp
from jax import lax
from jax.experimental import pallas as pl
from jax.experimental.pallas import tpu as pltpu
from jax.sharding import Mesh
from jax.sharding import PartitionSpec as P

LAT = 512
DP = ("y", "z")
HEAD = ("x", "core")
ALL = ("y", "z", "x", "core")
RING = 4
DP_N = 16
HEAD_N = 8
PAGES = 128
CAP = 32

softmax_scale = 192.0 ** (-0.5)
norm_eps = 1e-06
bf16 = jnp.bfloat16
f32 = jnp.float32
i32 = jnp.int32


def hop(array, axis, step):
    return lax.ppermute(array, axis, [((i + step) % RING, i) for i in range(RING)])


def send(array, axis, step):
    return lax.ppermute(array, axis, [(i, (i + step) % RING) for i in range(RING)])


def other_core(array):
    return lax.ppermute(array, "core", [(0, 1), (1, 0)])


def pack_kernel(pick_ref, query_ref, meta_ref, out_ref):
    width = query_ref.shape[2]

    def one(i, carry):
        out_ref[i, :, :width] = query_ref[pick_ref[i]]
        out_ref[i, :, width:] = meta_ref[i]
        return carry

    lax.fori_loop(0, out_ref.shape[0], one, 0)


def pack(pick, query_rows, meta):
    count, rows, width = query_rows.shape
    return pl.pallas_call(
        pack_kernel,
        out_shape=jax.ShapeDtypeStruct((DP_N, rows, width + meta.shape[2]), bf16),
        in_specs=[
            pl.BlockSpec(memory_space=pltpu.SMEM),
            pl.BlockSpec(memory_space=pltpu.VMEM),
            pl.BlockSpec(memory_space=pltpu.VMEM),
        ],
        out_specs=pl.BlockSpec(memory_space=pltpu.VMEM),
        compiler_params=pltpu.CompilerParams(vmem_limit_bytes=32 * 2**20),
        name="pack",
    )(pick, query_rows, meta)


def attend_kernel(pick_ref, page_ref, seen_ref, own_ref, far_ref, *refs):
    pages, out_ref = refs[:-1], refs[-1]
    step = pl.program_id(0)
    width = own_ref.shape[2]
    queries = jnp.where(step < 8, own_ref[0], far_ref[0, :, :width])
    keys = jnp.concatenate([page[0] for page in pages], axis=0)
    scores = (
        lax.dot_general(queries, keys, (((1,), (1,)), ((), ())), preferred_element_type=f32)
        * softmax_scale
    )
    position = lax.broadcasted_iota(i32, scores.shape, 1)
    draft = lax.broadcasted_iota(i32, scores.shape, 0) // (scores.shape[0] // 3)
    allowed = position <= seen_ref[step] + draft
    highest = jnp.max(jnp.where(allowed, scores, -1e30), axis=-1, keepdims=True)
    weights = jnp.where(allowed, jnp.exp(jnp.where(allowed, scores - highest, 0.0)), 0.0)
    probs = (weights / jnp.sum(weights, axis=-1, keepdims=True)).astype(bf16)
    out_ref[0] = lax.dot_general(
        probs, keys[:, :LAT], (((1,), (0,)), ((), ())), preferred_element_type=f32
    ).astype(bf16)


def attend(pick, pages, seen, own_queries, far_queries, kv_pool):
    count, rows, width = own_queries.shape
    page_rows = kv_pool.shape[1]
    per = pages.shape[1]

    def page_spec(a):
        return pl.BlockSpec(
            (1, page_rows, width), lambda i, pick, page, seen: (page[i * per + a], 0, 0)
        )

    spec = pltpu.PrefetchScalarGridSpec(
        num_scalar_prefetch=3,
        grid=(count,),
        in_specs=[
            pl.BlockSpec(
                (1, rows, width), lambda i, pick, page, seen: (pick[jnp.minimum(i, 7)], 0, 0)
            ),
            pl.BlockSpec(
                (1, rows, far_queries.shape[2]),
                lambda i, pick, page, seen: (pick[jnp.maximum(i, 8)], 0, 0),
            ),
        ]
        + [page_spec(a) for a in range(per)],
        out_specs=pl.BlockSpec((1, rows, LAT), lambda i, pick, page, seen: (i, 0, 0)),
    )
    return pl.pallas_call(
        attend_kernel,
        out_shape=jax.ShapeDtypeStruct((count, rows, LAT), bf16),
        grid_spec=spec,
        compiler_params=pltpu.CompilerParams(vmem_limit_bytes=32 * 2**20),
        cost_estimate=pl.CostEstimate(
            flops=count * rows * 512 * 1088 * 2, bytes_accessed=12_000_000, transcendentals=0
        ),
        name="attend",
    )(pick, pages.reshape(-1), seen, own_queries, far_queries, *([kv_pool] * per))


def before(count):
    at = jnp.arange(count, dtype=i32)
    return at[:, None] < at[None, :]


def shards(
    queries,
    kv_pool,
    page_table,
    cache_len,
    accepted,
    w_uv,
    w_o,
    residual,
    norm_gain,
    expert_ids,
    gate_weights,
    w_gate,
    w_up,
    w_down,
):
    at_x, at_y, at_z = lax.axis_index("x"), lax.axis_index("y"), lax.axis_index("z")
    at_core = lax.axis_index("core")
    dp_index = at_y * RING + at_z
    requests = page_table.shape[0]
    tokens, head_group, width = queries.shape
    query_rows = queries.reshape(requests, 3 * head_group, width)
    visible = cache_len + accepted
    lender = page_table[:, 0] // PAGES
    far = lender != dp_index
    dps = jnp.arange(DP_N, dtype=i32)

    lent_to = ((lender[None, :] == dps[:, None]) & far[None, :]).astype(i32)
    pick = jnp.sum(lent_to * jnp.arange(requests, dtype=i32)[None, :], axis=1)
    sent_pages = jnp.sum(lent_to[:, :, None] * (page_table - lender[:, None] * PAGES)[None], axis=1)
    sent_seen = jnp.sum(lent_to * visible[None, :], axis=1)
    sent_any = jnp.sum(lent_to, axis=1)
    line0 = jnp.concatenate(
        [
            sent_pages,
            (sent_seen // 2)[:, None],
            (sent_seen % 2)[:, None],
            sent_any[:, None],
            jnp.zeros((DP_N, 5), i32),
            jnp.broadcast_to(lender[None, :], (DP_N, requests)),
        ],
        axis=1,
    )
    w1 = lax.reduce_precision(gate_weights, 8, 7)
    w2 = lax.reduce_precision(gate_weights - w1, 8, 7)
    ids_block = jnp.concatenate(
        [expert_ids.astype(bf16), jnp.zeros((tokens, 32), bf16), w1.astype(bf16), w2.astype(bf16)],
        axis=1,
    )
    ids_block = jnp.pad(ids_block, ((0, 0), (0, 8)))
    line_block = jnp.pad(line0[:, None, :], ((0, 0), (0, tokens - 1), (8, 24))).astype(bf16)
    meta = ids_block[None] + line_block
    arrived = lax.all_to_all(pack(pick, query_rows, meta), DP, 0, 0, tiled=True)
    told = arrived[:, :, width:]
    all_weights = told[:, :, 40:48].astype(f32) + told[:, :, 48:56].astype(f32)
    told = told[:, :, :40].astype(i32)
    all_ids = told[:, :, :8]
    told_pages = told[:, 0, 8:16]
    told_seen = told[:, 0, 16] * 2 + told[:, 0, 17]
    told_any = told[:, 0, 18]
    lenders = told[:, 0, 24:40]

    slots = jnp.arange(8, dtype=i32)
    own = 1 - far.astype(i32)
    own_rank = jnp.sum(before(requests) * own[:, None], axis=0)
    own_pick = ((own_rank[None, :] == slots[:, None]) & (own[None, :] > 0)).astype(i32)
    far_rank = jnp.sum(before(DP_N) * told_any[:, None], axis=0)
    far_pick = ((far_rank[None, :] == slots[:, None]) & (told_any[None, :] > 0)).astype(i32)
    which = jnp.concatenate([jnp.sum(own_pick * dps, axis=1), jnp.sum(far_pick * dps, axis=1)])
    held_pages = jnp.concatenate(
        [
            jnp.sum(own_pick[:, :, None] * (page_table - dp_index * PAGES)[None], axis=1),
            jnp.sum(far_pick[:, :, None] * told_pages[None], axis=1),
        ]
    )
    held_seen = jnp.concatenate(
        [jnp.sum(own_pick * visible, axis=1), jnp.sum(far_pick * told_seen, axis=1)]
    )
    latent = attend(which, held_pages, held_seen, query_rows, arrived, kv_pool)
    values = jnp.einsum(
        "thc,hcv->thv",
        latent.reshape(tokens, head_group, LAT),
        w_uv,
        preferred_element_type=f32,
    ).astype(bf16)
    values = values.reshape(tokens, head_group * w_uv.shape[2])

    half = values.shape[1] // 2

    def spread(block, first, second):
        line = jnp.concatenate([block] + [hop(block, first, k) for k in (1, 2, 3)], axis=0)
        return [line] + [hop(line, second, k) for k in (1, 2, 3)]

    zy = spread(values[:, :half], "z", "y")
    yz = spread(values[:, half:], "y", "z")
    part_zy = jnp.concatenate(
        [jnp.dot(a, w_o[:half], preferred_element_type=f32) for a in zy], axis=0
    )
    part_yz = jnp.concatenate(
        [jnp.dot(a, w_o[half:], preferred_element_type=f32) for a in yz], axis=0
    )
    columns = w_o.shape[1]
    part_yz = part_yz.reshape(RING, RING, tokens, columns).transpose(1, 0, 2, 3)
    projected = (part_zy + part_yz.reshape(-1, columns)).astype(bf16)

    is_own = (lenders == dps[:, None]).astype(i32)
    own_slot = jnp.sum(is_own[:, :, None] * before(requests)[None], axis=1)
    at_lender = (lenders[:, :, None] == dps[None, None, :]).astype(i32)
    away = at_lender * (dps[:, None, None] != dps[None, None, :])
    lends = jnp.sum(away, axis=1)
    lend_rank = jnp.sum(before(DP_N)[:, :, None] * lends[:, None, :], axis=0)
    far_slot = 8 + jnp.sum(at_lender * lend_rank[:, None, :], axis=2)
    slot = jnp.where(is_own > 0, own_slot, far_slot)
    turned = ((lenders // RING - at_y) % RING) * RING + (lenders % RING - at_z) % RING
    first_row = (turned * requests + slot) * 3
    source = (first_row[:, :, None] + jnp.arange(3, dtype=i32)).reshape(RING, 2, 2 * tokens)
    source = lax.dynamic_slice_in_dim(jnp.concatenate([source, source], 0), at_x, RING, 0)
    source = lax.dynamic_slice_in_dim(jnp.concatenate([source, source], 1), at_core, 2, 1)
    source = source.transpose(1, 0, 2).reshape(-1)
    rows_all = projected.shape[0]
    moves = (source[:, None] == jnp.arange(rows_all, dtype=i32)[None, :]).astype(bf16)
    homed = jnp.dot(moves, projected, preferred_element_type=f32)
    kept = homed[: rows_all // 2] + other_core(homed[rows_all // 2 :].astype(bf16)).astype(f32)
    kept = kept.reshape(RING, 2 * tokens, columns)
    mine = kept[0]
    for k in (2, 1, 3):
        mine = mine + send(kept[k].astype(bf16), "x", k).astype(f32)
    mine = mine.astype(bf16)

    odd = dp_index % 2
    low, high = mine[:tokens], mine[tokens:]
    got = []
    for turn in (0, 1):
        pairs = []
        for d in range(DP_N):
            for h in range(HEAD_N):
                pairs.append((d * HEAD_N + h, (2 * h + (turn + d) % 2) * HEAD_N + d // 2))
        block = jnp.where((odd + turn) % 2 == 0, low, high)
        got.append(lax.ppermute(block, ALL, pairs))
    attention = jnp.concatenate(
        [jnp.where(odd == 0, got[0], got[1]), jnp.where(odd == 0, got[1], got[0])], axis=1
    )
    wide_piece = 2 * columns
    head_index = at_x * 2 + at_core
    near = lax.dynamic_slice_in_dim(residual, head_index * wide_piece, wide_piece, 1)
    piece = (near.astype(f32) + attention.astype(f32)).astype(bf16)

    part = tokens // 3

    def ring(block, axis, along):
        return jnp.concatenate([block] + [hop(block, axis, k) for k in (1, 2, 3)], axis=along)

    pa, pb, pc = piece[:part], piece[part : 2 * part], piece[2 * part :]
    pa, pb, pc = ring(pa, "z", 0), ring(pb, "y", 0), ring(pc, "x", 1)
    out_c = pc
    pa, pb, pc = ring(pa, "y", 0), ring(pb, "x", 1), ring(pc, "z", 0)
    out_b = pb[:part]
    pa, pb, pc = ring(pa, "x", 1), ring(pb, "z", 0), ring(pc, "y", 0)
    out_a = pa[:part]
    here = jnp.concatenate([out_a, out_b, out_c], axis=0)
    there = other_core(here)
    first = jnp.where(at_core == 0, here, there)
    second = jnp.where(at_core == 0, there, here)
    blocks = []
    for k in range(RING):
        for side in (first, second):
            blocks.append(side[:, k * wide_piece : (k + 1) * wide_piece])
    row = jnp.concatenate(blocks, axis=1)
    row = jnp.concatenate([row, row], axis=1)
    attended = lax.dynamic_slice_in_dim(
        row, (RING - at_x) % RING * 2 * wide_piece, residual.shape[1], 1
    )

    def rows_of(weights, core):
        cut = [
            lax.dynamic_slice_in_dim(
                weights, ((at_x + k) % RING * 2 + core) * wide_piece, wide_piece, 0
            )
            for k in range(RING)
        ]
        gains = [
            lax.dynamic_slice_in_dim(
                norm_gain, ((at_x + k) % RING * 2 + core) * wide_piece, wide_piece, 0
            )
            for k in range(RING)
        ]
        cut, gains = jnp.concatenate(cut, axis=0), jnp.concatenate(gains, axis=0)
        return (cut.astype(f32) * gains[:, None]).astype(bf16)

    def columns_of(weights, core):
        cut = [
            lax.dynamic_slice_in_dim(
                weights, ((at_x + k) % RING * 2 + core) * wide_piece, wide_piece, 1
            )
            for k in range(RING)
        ]
        return jnp.concatenate(cut, axis=1)

    gate_own, up_own = rows_of(w_gate[0], at_core), rows_of(w_up[0], at_core)
    gate_other = other_core(rows_of(w_gate[0], 1 - at_core))
    up_other = other_core(rows_of(w_up[0], 1 - at_core))
    units = w_gate.shape[2]
    w_in = jnp.concatenate([gate_own, up_own, gate_other, up_other], axis=1)
    w_out = jnp.concatenate(
        [columns_of(w_down[0], at_core), other_core(columns_of(w_down[0], 1 - at_core))], axis=0
    )

    weight = jnp.sum(jnp.where(all_ids == dp_index, all_weights, 0.0), axis=2)
    weight = weight.reshape(RING, RING, tokens)
    weight = lax.dynamic_slice_in_dim(jnp.concatenate([weight, weight], 0), at_y, RING, 0)
    weight = lax.dynamic_slice_in_dim(jnp.concatenate([weight, weight], 1), at_z, RING, 1)
    parts = []
    for n, block in enumerate((pa, pb, pc)):
        scale = weight[:, :, n * part : (n + 1) * part]
        scale = (scale.transpose(1, 0, 2) if n == 1 else scale).reshape(-1, 1)
        wide = block.astype(f32)
        squares = jnp.sum(wide * wide, axis=1, keepdims=True)
        sums = jnp.dot(block, w_in, preferred_element_type=f32)
        squares = squares + other_core(squares)
        swapped = other_core(sums.astype(bf16)).astype(f32)
        root = lax.rsqrt(squares / residual.shape[1] + norm_eps)
        own_sum = (sums[:, : 2 * units] + swapped[:, 2 * units :]) * root
        other_sum = (sums[:, 2 * units :] + swapped[:, : 2 * units]) * root
        hidden = [jax.nn.silu(a[:, :units]) * a[:, units:] * scale for a in (own_sum, other_sum)]
        hidden = jnp.concatenate(hidden, axis=1).astype(bf16)
        parts.append(jnp.dot(hidden, w_out, preferred_element_type=f32))

    def gather_sum(block, axis, along):
        size = block.shape[along] // RING
        cuts = [lax.slice_in_dim(block, k * size, (k + 1) * size, axis=along) for k in range(RING)]
        total = cuts[0]
        for k in (2, 1, 3):
            total = total + send(cuts[k].astype(bf16), axis, k).astype(f32)
        return total

    ra, rb, rc = parts
    ra, rb, rc = gather_sum(ra, "x", 1), gather_sum(rb, "z", 0), gather_sum(rc, "y", 0)
    ra, rb, rc = gather_sum(ra, "y", 0), gather_sum(rb, "x", 1), gather_sum(rc, "z", 0)
    ra, rb, rc = gather_sum(ra, "z", 0), gather_sum(rb, "y", 0), gather_sum(rc, "x", 1)
    routed = jnp.concatenate([ra, rb, rc], axis=0).astype(bf16)
    return (attended, routed)


def solution(mesh):
    grid = Mesh(mesh.devices.reshape(RING, RING, RING, 2), ALL)
    return jax.shard_map(
        shards,
        mesh=grid,
        in_specs=(
            P(DP, HEAD, None),
            P(DP, None, None),
            P(DP, None),
            P(DP),
            P(DP),
            P(HEAD, None, None),
            P(HEAD, DP),
            P(DP, None),
            P(),
            P(DP, None),
            P(DP, None),
            P(DP, None, HEAD),
            P(DP, None, HEAD),
            P(DP, HEAD, None),
        ),
        out_specs=(P(DP, None), P(DP, HEAD)),
        check_vma=False,
    )
```

```python
import jax
import jax.numpy as jnp
from jax import lax
from jax.experimental import pallas as pl
from jax.experimental.pallas import tpu as pltpu
from jax.sharding import Mesh
from jax.sharding import PartitionSpec as P

LAT = 512
DP = ("y", "z")
HEAD = ("x", "core")
ALL = ("y", "z", "x", "core")
RING = 4
DP_N = 16
HEAD_N = 8
PAGES = 128
CAP = 32

softmax_scale = 192.0 ** (-0.5)
norm_eps = 1e-06
bf16 = jnp.bfloat16
f32 = jnp.float32
i32 = jnp.int32


def hop(array, axis, step):
    return lax.ppermute(array, axis, [((i + step) % RING, i) for i in range(RING)])


def send(array, axis, step):
    return lax.ppermute(array, axis, [(i, (i + step) % RING) for i in range(RING)])


def other_core(array):
    return lax.ppermute(array, "core", [(0, 1), (1, 0)])


def pack_kernel(me_ref, page_ref, held_ref, taken_ref, query_ref, ids_ref, gate_ref, out_ref, who_ref):
    me = me_ref[0]
    width = query_ref.shape[2]
    requests, per = page_ref.shape
    rows = ids_ref.shape[0]
    lanes = out_ref.shape[2] - width

    def put(block, first):
        row = lax.broadcasted_iota(i32, (block.shape[1], lanes), 0)
        lane = lax.broadcasted_iota(i32, (block.shape[1], lanes), 1)
        spot = jnp.where(lane == row + first, 1.0, 0.0).astype(bf16)
        return jnp.dot(block.astype(bf16), spot, preferred_element_type=f32)

    gates = gate_ref[...]
    coarse = gates.astype(bf16).astype(f32)
    base = put(ids_ref[...].astype(f32), 0) + put(coarse, 40) + put(gates - coarse, 48)
    row = lax.broadcasted_iota(i32, (rows, lanes), 0)
    lane = lax.broadcasted_iota(i32, (rows, lanes), 1)

    def clear(i, carry):
        who_ref[i] = -1
        return carry

    lax.fori_loop(0, DP_N, clear, 0)
    lane = jnp.where(row == 0, lane, -1)
    for r in range(requests):
        lender = page_ref[r, 0] // PAGES
        base = jnp.where(lane == 24 + r, lender.astype(f32), base)

        @pl.when(lender != me)
        def _():
            who_ref[lender] = r

    def one(i, carry):
        found = who_ref[i]
        r = jnp.maximum(found, 0)
        seen = held_ref[r] + taken_ref[r]
        told = [page_ref[r, k] - page_ref[r, 0] // PAGES * PAGES for k in range(per)]
        told += [seen // 2, seen % 2, jnp.where(found >= 0, 1, 0)]
        line = base
        for k, value in enumerate(told):
            line = jnp.where(lane == 8 + k, value.astype(f32), line)
        out_ref[i, :, :width] = query_ref[r]
        out_ref[i, :, width:] = line.astype(bf16)
        return carry

    lax.fori_loop(0, DP_N, one, 0)


def pack(me, page_table, cache_len, accepted, query_rows, expert_ids, gate_weights):
    count, rows, width = query_rows.shape
    scalar, vector = (pl.BlockSpec(memory_space=m) for m in (pltpu.SMEM, pltpu.VMEM))
    return pl.pallas_call(
        pack_kernel,
        out_shape=jax.ShapeDtypeStruct((DP_N, rows, width + 64), bf16),
        in_specs=[scalar] * 4 + [vector] * 3,
        out_specs=vector,
        scratch_shapes=[pltpu.SMEM((DP_N,), i32)],
        compiler_params=pltpu.CompilerParams(vmem_limit_bytes=32 * 2**20),
        name="pack",
    )(me, page_table, cache_len, accepted, query_rows, expert_ids, gate_weights)


def attend_kernel(
    me_ref, page_ref, held_ref, taken_ref, told_ref, own_ref, far_ref, pool_ref, out_ref,
    which_ref, list_ref, seen_ref, keys_ref, sems,
):
    me = me_ref[0]
    count, rows, width = own_ref.shape
    per = page_ref.shape[1]
    page_rows = pool_ref.shape[1]
    pair = keys_ref.shape[1]

    def plan(r, found):
        own_at, far_at = found
        mine = page_ref[r, 0] // PAGES == me
        lent = told_ref[r, 10] > 0

        @pl.when(mine)
        def _():
            at = jnp.minimum(own_at, 7)
            which_ref[at] = r
            seen_ref[at] = held_ref[r] + taken_ref[r]
            for k in range(per):
                list_ref[at * per + k] = page_ref[r, k] - me * PAGES

        @pl.when(lent)
        def _():
            at = 8 + jnp.minimum(far_at, 7)
            which_ref[at] = r
            seen_ref[at] = told_ref[r, 8] * 2 + told_ref[r, 9]
            for k in range(per):
                list_ref[at * per + k] = told_ref[r, k]

        return own_at + mine.astype(i32), far_at + lent.astype(i32)

    lax.fori_loop(0, count, plan, (jnp.int32(0), jnp.int32(0)))

    def copies(turn, slot):
        made = []
        for n in range(pair):
            for k in range(per):
                page = list_ref[(turn * pair + n) * per + k]
                made.append(
                    pltpu.make_async_copy(
                        pool_ref.at[page],
                        keys_ref.at[slot, n, pl.ds(k * page_rows, page_rows)],
                        sems.at[slot, n, k],
                    )
                )
        return made

    for copy in copies(0, 0):
        copy.start()
    position = lax.broadcasted_iota(i32, (rows, per * page_rows), 1)
    draft = lax.broadcasted_iota(i32, (rows, per * page_rows), 0) // (rows // 3)
    turns = count // pair

    def turn_step(turn, carry):
        slot = lax.rem(turn, 2)

        @pl.when(turn + 1 < turns)
        def _():
            for copy in copies(turn + 1, 1 - slot):
                copy.start()

        for copy in copies(turn, slot):
            copy.wait()
        for n in range(pair):
            at = turn * pair + n
            which = which_ref[at]
            queries = jnp.where(at < 8, own_ref[which], far_ref[which, :, :width])
            keys = keys_ref[slot, n]
            scores = (
                lax.dot_general(queries, keys, (((1,), (1,)), ((), ())), preferred_element_type=f32)
                * softmax_scale
            )
            allowed = position <= seen_ref[at] + draft
            highest = jnp.max(jnp.where(allowed, scores, -1e30), axis=-1, keepdims=True)
            weights = jnp.where(allowed, jnp.exp(jnp.where(allowed, scores - highest, 0.0)), 0.0)
            probs = (weights / jnp.sum(weights, axis=-1, keepdims=True)).astype(bf16)
            out_ref[at] = lax.dot_general(
                probs, keys[:, :LAT], (((1,), (0,)), ((), ())), preferred_element_type=f32
            ).astype(bf16)
        return carry

    lax.fori_loop(0, turns, turn_step, 0)


def attend(me, page_table, cache_len, accepted, told, own_queries, far_queries, kv_pool):
    count, rows, width = own_queries.shape
    per, page_rows = page_table.shape[1], kv_pool.shape[1]
    pair = 2
    scalar, vector = (pl.BlockSpec(memory_space=m) for m in (pltpu.SMEM, pltpu.VMEM))
    return pl.pallas_call(
        attend_kernel,
        out_shape=jax.ShapeDtypeStruct((count, rows, LAT), bf16),
        in_specs=[scalar] * 5 + [vector] * 2 + [pl.BlockSpec(memory_space=pl.ANY)],
        out_specs=vector,
        scratch_shapes=[
            pltpu.SMEM((count,), i32),
            pltpu.SMEM((count * per,), i32),
            pltpu.SMEM((count,), i32),
            pltpu.VMEM((2, pair, per * page_rows, width), bf16),
            pltpu.SemaphoreType.DMA((2, pair, per)),
        ],
        compiler_params=pltpu.CompilerParams(vmem_limit_bytes=32 * 2**20),
        cost_estimate=pl.CostEstimate(
            flops=count * rows * 512 * 1088 * 2, bytes_accessed=12_000_000, transcendentals=0
        ),
        name="attend",
    )(me, page_table, cache_len, accepted, told, own_queries, far_queries, kv_pool)


def sort_kernel(spot_ref, gate_ref, up_ref, down_ref, own_ref, other_ref, down_own_ref, down_other_ref, sems):
    wide = down_own_ref.shape[1] // RING
    units = gate_ref.shape[2]
    made = []
    for side, (rows_ref, cols_ref) in enumerate(
        ((own_ref, down_own_ref), (other_ref, down_other_ref))
    ):
        for k in range(RING):
            start = pl.multiple_of(spot_ref[side * RING + k] * wide, 128)
            there = pl.ds(start, wide)
            here = pl.ds(k * wide, wide)
            made.append(
                (gate_ref.at[0, there], rows_ref.at[here, pl.ds(0, units)], sems.at[side, k, 0])
            )
            made.append(
                (up_ref.at[0, there], rows_ref.at[here, pl.ds(units, units)], sems.at[side, k, 1])
            )
            made.append((down_ref.at[0, :, there], cols_ref.at[:, here], sems.at[side, k, 2]))
    made = [pltpu.make_async_copy(*one) for one in made]
    for copy in made:
        copy.start()
    for copy in made:
        copy.wait()


def sort_weights(spots, w_gate, w_up, w_down):
    units, model = w_down.shape[1:]
    anywhere = pl.BlockSpec(memory_space=pl.ANY)
    return pl.pallas_call(
        sort_kernel,
        out_shape=[jax.ShapeDtypeStruct((model // 2, 2 * units), bf16)] * 2
        + [jax.ShapeDtypeStruct((units, model // 2), bf16)] * 2,
        in_specs=[pl.BlockSpec(memory_space=pltpu.SMEM)] + [anywhere] * 3,
        out_specs=[anywhere] * 4,
        scratch_shapes=[pltpu.SemaphoreType.DMA((2, RING, 3))],
        cost_estimate=pl.CostEstimate(flops=0, bytes_accessed=22_000_000, transcendentals=0),
        name="sort_weights",
    )(spots, w_gate, w_up, w_down)


def before(count):
    at = jnp.arange(count, dtype=i32)
    return at[:, None] < at[None, :]


def shards(
    queries,
    kv_pool,
    page_table,
    cache_len,
    accepted,
    w_uv,
    w_o,
    residual,
    norm_gain,
    expert_ids,
    gate_weights,
    w_gate,
    w_up,
    w_down,
):
    at_x, at_y, at_z = lax.axis_index("x"), lax.axis_index("y"), lax.axis_index("z")
    at_core = lax.axis_index("core")
    dp_index = at_y * RING + at_z
    requests = page_table.shape[0]
    tokens, head_group, width = queries.shape
    query_rows = queries.reshape(requests, 3 * head_group, width)
    dps = jnp.arange(DP_N, dtype=i32)
    me = dp_index.astype(i32)[None]

    packed = pack(me, page_table, cache_len, accepted, query_rows, expert_ids, gate_weights)
    arrived = lax.all_to_all(packed, DP, 0, 0, tiled=True)

    _, w_gate, w_up, w_down = lax.optimization_barrier((packed, w_gate, w_up, w_down))
    ring_at = (at_x + jnp.arange(RING, dtype=i32)) % RING * 2
    spots = jnp.concatenate([ring_at + at_core, ring_at + 1 - at_core])
    in_own, in_give, out_own, out_give = sort_weights(spots, w_gate, w_up, w_down)
    in_other, out_other = other_core(in_give), other_core(out_give)

    told = arrived[:, :, width:]
    all_ids = told[:, :, :8].astype(i32)
    all_weights = told[:, :, 40:48].astype(f32) + told[:, :, 48:56].astype(f32)
    lenders = told[:, 0, 24:40].astype(i32)
    line = told[:, 0, 8:24].astype(i32)
    latent = attend(me, page_table, cache_len, accepted, line, query_rows, arrived, kv_pool)
    values = jnp.einsum(
        "thc,hcv->thv",
        latent.reshape(tokens, head_group, LAT),
        w_uv,
        preferred_element_type=f32,
    ).astype(bf16)
    values = values.reshape(tokens, head_group * w_uv.shape[2])

    values, in_own, in_other, out_own, out_other = lax.optimization_barrier(
        (values, in_own, in_other, out_own, out_other)
    )

    half = values.shape[1] // 2

    def spread(block, first, second):
        line = jnp.concatenate([block] + [hop(block, first, k) for k in (1, 2, 3)], axis=0)
        return [line] + [hop(line, second, k) for k in (1, 2, 3)]

    zy = spread(values[:, :half], "z", "y")
    yz = spread(values[:, half:], "y", "z")
    part_zy = jnp.concatenate(
        [jnp.dot(a, w_o[:half], preferred_element_type=f32) for a in zy], axis=0
    )
    part_yz = jnp.concatenate(
        [jnp.dot(a, w_o[half:], preferred_element_type=f32) for a in yz], axis=0
    )
    columns = w_o.shape[1]
    part_yz = part_yz.reshape(RING, RING, tokens, columns).transpose(1, 0, 2, 3)
    projected = (part_zy + part_yz.reshape(-1, columns)).astype(bf16)

    is_own = (lenders == dps[:, None]).astype(i32)
    own_slot = jnp.sum(is_own[:, :, None] * before(requests)[None], axis=1)
    at_lender = (lenders[:, :, None] == dps[None, None, :]).astype(i32)
    away = at_lender * (dps[:, None, None] != dps[None, None, :])
    lends = jnp.sum(away, axis=1)
    lend_rank = jnp.sum(before(DP_N)[:, :, None] * lends[:, None, :], axis=0)
    far_slot = 8 + jnp.sum(at_lender * lend_rank[:, None, :], axis=2)
    slot = jnp.where(is_own > 0, own_slot, far_slot)
    turned = ((lenders // RING - at_y) % RING) * RING + (lenders % RING - at_z) % RING
    first_row = (turned * requests + slot) * 3
    source = (first_row[:, :, None] + jnp.arange(3, dtype=i32)).reshape(RING, 2, 2 * tokens)
    source = lax.dynamic_slice_in_dim(jnp.concatenate([source, source], 0), at_x, RING, 0)
    source = lax.dynamic_slice_in_dim(jnp.concatenate([source, source], 1), at_core, 2, 1)
    source = source.transpose(1, 0, 2).reshape(-1)
    rows_all = projected.shape[0]
    moves = (source[:, None] == jnp.arange(rows_all, dtype=i32)[None, :]).astype(bf16)
    homed = jnp.dot(moves, projected, preferred_element_type=f32)
    kept = homed[: rows_all // 2] + other_core(homed[rows_all // 2 :].astype(bf16)).astype(f32)
    kept = kept.reshape(RING, 2 * tokens, columns)
    mine = kept[0]
    for k in (2, 1, 3):
        mine = mine + send(kept[k].astype(bf16), "x", k).astype(f32)
    mine = mine.astype(bf16)

    odd = dp_index % 2
    low, high = mine[:tokens], mine[tokens:]
    got = []
    for turn in (0, 1):
        pairs = []
        for d in range(DP_N):
            for h in range(HEAD_N):
                pairs.append((d * HEAD_N + h, (2 * h + (turn + d) % 2) * HEAD_N + d // 2))
        block = jnp.where((odd + turn) % 2 == 0, low, high)
        got.append(lax.ppermute(block, ALL, pairs))
    attention = jnp.concatenate(
        [jnp.where(odd == 0, got[0], got[1]), jnp.where(odd == 0, got[1], got[0])], axis=1
    )
    wide_piece = 2 * columns
    head_index = at_x * 2 + at_core
    near = lax.dynamic_slice_in_dim(residual, head_index * wide_piece, wide_piece, 1)
    piece = (near.astype(f32) + attention.astype(f32)).astype(bf16)

    part = tokens // 3

    def ring(block, axis, along):
        return jnp.concatenate([block] + [hop(block, axis, k) for k in (1, 2, 3)], axis=along)

    pa, pb, pc = piece[:part], piece[part : 2 * part], piece[2 * part :]
    pa, pb, pc = ring(pa, "z", 0), ring(pb, "y", 0), ring(pc, "x", 1)
    out_c = pc
    pa, pb, pc = ring(pa, "y", 0), ring(pb, "x", 1), ring(pc, "z", 0)
    out_b = pb[:part]
    pa, pb, pc = ring(pa, "x", 1), ring(pb, "z", 0), ring(pc, "y", 0)
    out_a = pa[:part]
    here = jnp.concatenate([out_a, out_b, out_c], axis=0)
    there = other_core(here)
    first = jnp.where(at_core == 0, here, there)
    second = jnp.where(at_core == 0, there, here)
    blocks = []
    for k in range(RING):
        for side in (first, second):
            blocks.append(side[:, k * wide_piece : (k + 1) * wide_piece])
    row = jnp.concatenate(blocks, axis=1)
    row = jnp.concatenate([row, row], axis=1)
    attended = lax.dynamic_slice_in_dim(
        row, (RING - at_x) % RING * 2 * wide_piece, residual.shape[1], 1
    )

    units = w_gate.shape[2]
    gains = jnp.concatenate([norm_gain, norm_gain]).reshape(2 * RING, 2, wide_piece)
    gains = lax.dynamic_slice(gains, (at_x, at_core, 0), (RING, 1, wide_piece)).reshape(1, -1)

    weight = jnp.sum(jnp.where(all_ids == dp_index, all_weights, 0.0), axis=2)
    weight = weight.reshape(RING, RING, tokens)
    weight = lax.dynamic_slice_in_dim(jnp.concatenate([weight, weight], 0), at_y, RING, 0)
    weight = lax.dynamic_slice_in_dim(jnp.concatenate([weight, weight], 1), at_z, RING, 1)
    parts = []
    for n, block in enumerate((pa, pb, pc)):
        scale = weight[:, :, n * part : (n + 1) * part]
        scale = (scale.transpose(1, 0, 2) if n == 1 else scale).reshape(-1, 1)
        wide = block.astype(f32)
        squares = jnp.sum(wide * wide, axis=1, keepdims=True)
        gained = lax.optimization_barrier((wide * gains).astype(bf16))
        sums = jnp.dot(gained, in_own, preferred_element_type=f32)
        give = jnp.dot(gained, in_other, preferred_element_type=f32)
        swapped = other_core(jnp.concatenate([give, sums], axis=1).astype(bf16)).astype(f32)
        squares = squares + other_core(squares)
        root = lax.rsqrt(squares / residual.shape[1] + norm_eps)
        own_sum = (sums + swapped[:, : 2 * units]) * root
        other_sum = (give + swapped[:, 2 * units :]) * root
        hidden = [jax.nn.silu(a[:, :units]) * a[:, units:] * scale for a in (own_sum, other_sum)]
        hidden = lax.optimization_barrier([a.astype(bf16) for a in hidden])
        parts.append(
            (
                jnp.dot(hidden[0], out_own, preferred_element_type=f32)
                + jnp.dot(hidden[1], out_other, preferred_element_type=f32)
            ).astype(bf16)
        )

    def gather_sum(block, axis, along):
        size = block.shape[along] // RING
        cuts = [lax.slice_in_dim(block, k * size, (k + 1) * size, axis=along) for k in range(RING)]
        total = cuts[0].astype(f32)
        for k in (2, 1, 3):
            total = total + send(cuts[k].astype(bf16), axis, k).astype(f32)
        return total

    ra, rb, rc = parts
    ra, rb, rc = gather_sum(ra, "x", 1), gather_sum(rb, "z", 0), gather_sum(rc, "y", 0)
    ra, rb, rc = gather_sum(ra, "y", 0), gather_sum(rb, "x", 1), gather_sum(rc, "z", 0)
    ra, rb, rc = gather_sum(ra, "z", 0), gather_sum(rb, "y", 0), gather_sum(rc, "x", 1)
    routed = jnp.concatenate([ra, rb, rc], axis=0).astype(bf16)
    return (attended, routed)


def solution(mesh):
    grid = Mesh(mesh.devices.reshape(RING, RING, RING, 2), ALL)
    return jax.shard_map(
        shards,
        mesh=grid,
        in_specs=(
            P(DP, HEAD, None),
            P(DP, None, None),
            P(DP, None),
            P(DP),
            P(DP),
            P(HEAD, None, None),
            P(HEAD, DP),
            P(DP, None),
            P(),
            P(DP, None),
            P(DP, None),
            P(DP, None, HEAD),
            P(DP, None, HEAD),
            P(DP, HEAD, None),
        ),
        out_specs=(P(DP, None), P(DP, HEAD)),
        check_vma=False,
    )
```

```python
import jax
import jax.numpy as jnp
from jax import lax
from jax.experimental import pallas as pl
from jax.experimental.pallas import tpu as pltpu
from jax.sharding import Mesh
from jax.sharding import PartitionSpec as P

LAT = 512
DP = ("y", "z")
HEAD = ("x", "core")
ALL = ("y", "z", "x", "core")
RING = 4
DP_N = 16
HEAD_N = 8
PAGES = 128
CAP = 32

softmax_scale = 192.0 ** (-0.5)
norm_eps = 1e-06
bf16 = jnp.bfloat16
f32 = jnp.float32
i32 = jnp.int32


def hop(array, axis, step):
    return lax.ppermute(array, axis, [((i + step) % RING, i) for i in range(RING)])


def send(array, axis, step):
    return lax.ppermute(array, axis, [(i, (i + step) % RING) for i in range(RING)])


def other_core(array):
    return lax.ppermute(array, "core", [(0, 1), (1, 0)])


def pack_kernel(me_ref, page_ref, held_ref, taken_ref, query_ref, out_ref, who_ref):
    me = me_ref[0]
    width = query_ref.shape[2]
    requests, per = page_ref.shape
    rows = out_ref.shape[1]
    lanes = out_ref.shape[2] - width

    row = lax.broadcasted_iota(i32, (rows, lanes), 0)
    lane = lax.broadcasted_iota(i32, (rows, lanes), 1)

    def clear(i, carry):
        who_ref[i] = -1
        return carry

    lax.fori_loop(0, DP_N, clear, 0)
    lane = jnp.where(row == 0, lane, -1)
    base = jnp.zeros((rows, lanes), f32)
    for r in range(requests):
        lender = page_ref[r, 0] // PAGES
        base = jnp.where(lane == 24 + r, lender.astype(f32), base)

        @pl.when(lender != me)
        def _():
            who_ref[lender] = r

    def one(i, carry):
        found = who_ref[i]
        r = jnp.maximum(found, 0)
        seen = held_ref[r] + taken_ref[r]
        told = [page_ref[r, k] - page_ref[r, 0] // PAGES * PAGES for k in range(per)]
        told += [seen // 2, seen % 2, jnp.where(found >= 0, 1, 0)]
        line = base
        for k, value in enumerate(told):
            line = jnp.where(lane == 8 + k, value.astype(f32), line)
        out_ref[i, :, :width] = query_ref[r]
        out_ref[i, :, width:] = line.astype(bf16)
        return carry

    lax.fori_loop(0, DP_N, one, 0)


def pack(me, page_table, cache_len, accepted, query_rows):
    count, rows, width = query_rows.shape
    scalar, vector = (pl.BlockSpec(memory_space=m) for m in (pltpu.SMEM, pltpu.VMEM))
    return pl.pallas_call(
        pack_kernel,
        out_shape=jax.ShapeDtypeStruct((DP_N, rows, width + 64), bf16),
        in_specs=[scalar] * 4 + [vector],
        out_specs=vector,
        scratch_shapes=[pltpu.SMEM((DP_N,), i32)],
        compiler_params=pltpu.CompilerParams(vmem_limit_bytes=32 * 2**20),
        name="pack",
    )(me, page_table, cache_len, accepted, query_rows)


def plan_kernel(
    me_ref, page_ref, held_ref, taken_ref, told_ref, which_ref, list_ref, seen_ref
):
    me = me_ref[0]
    count, per = page_ref.shape

    def plan(r, found):
        own_at, far_at = found
        mine = page_ref[r, 0] // PAGES == me
        lent = told_ref[r, 10] > 0

        @pl.when(mine)
        def _():
            at = jnp.minimum(own_at, 7)
            which_ref[at] = r
            seen_ref[at] = held_ref[r] + taken_ref[r]
            for k in range(per):
                list_ref[at * per + k] = page_ref[r, k] - me * PAGES

        @pl.when(lent)
        def _():
            at = 8 + jnp.minimum(far_at, 7)
            which_ref[at] = r
            seen_ref[at] = told_ref[r, 8] * 2 + told_ref[r, 9]
            for k in range(per):
                list_ref[at * per + k] = told_ref[r, k]

        return own_at + mine.astype(i32), far_at + lent.astype(i32)

    lax.fori_loop(0, count, plan, (jnp.int32(0), jnp.int32(0)))


def plan(me, page_table, cache_len, accepted, told):
    count, per = page_table.shape
    scalar = pl.BlockSpec(memory_space=pltpu.SMEM)
    return pl.pallas_call(
        plan_kernel,
        out_shape=[
            jax.ShapeDtypeStruct((count,), i32),
            jax.ShapeDtypeStruct((count * per,), i32),
            jax.ShapeDtypeStruct((count,), i32),
        ],
        in_specs=[scalar] * 5,
        out_specs=[scalar] * 3,
        name="plan",
    )(me, page_table, cache_len, accepted, told)


def attend_kernel(pick_ref, page_ref, seen_ref, *refs):
    out_ref = refs[-1]
    step = pl.program_id(0)
    per = (len(refs) - 1) // 2
    for n in range(2):
        own_ref, far_ref, *pages = refs[n * per : (n + 1) * per]
        at = step * 2 + n
        width = own_ref.shape[2]
        queries = jnp.where(at < 8, own_ref[0], far_ref[0, :, :width])
        keys = jnp.concatenate([page[0] for page in pages], axis=0)
        scores = (
            lax.dot_general(queries, keys, (((1,), (1,)), ((), ())), preferred_element_type=f32)
            * softmax_scale
        )
        position = lax.broadcasted_iota(i32, scores.shape, 1)
        draft = lax.broadcasted_iota(i32, scores.shape, 0) // (scores.shape[0] // 3)
        allowed = position <= seen_ref[at] + draft
        highest = jnp.max(jnp.where(allowed, scores, -1e30), axis=-1, keepdims=True)
        weights = jnp.where(allowed, jnp.exp(jnp.where(allowed, scores - highest, 0.0)), 0.0)
        probs = (weights / jnp.sum(weights, axis=-1, keepdims=True)).astype(bf16)
        out_ref[n] = lax.dot_general(
            probs, keys[:, :LAT], (((1,), (0,)), ((), ())), preferred_element_type=f32
        ).astype(bf16)


def attend(pick, pages, seen, own_queries, far_queries, kv_pool):
    count, rows, width = own_queries.shape
    page_rows = kv_pool.shape[1]
    per = pages.shape[0] // count

    def specs(n):
        def own(i, pick, page, seen):
            return (pick[jnp.minimum(i * 2 + n, 6 + n)], 0, 0)

        def far(i, pick, page, seen):
            return (pick[jnp.maximum(i * 2 + n, 8 + n)], 0, 0)

        def page_spec(a):
            return pl.BlockSpec(
                (1, page_rows, width),
                lambda i, pick, page, seen: (page[(i * 2 + n) * per + a], 0, 0),
            )

        return [
            pl.BlockSpec((1, rows, width), own),
            pl.BlockSpec((1, rows, far_queries.shape[2]), far),
        ] + [page_spec(a) for a in range(per)]

    spec = pltpu.PrefetchScalarGridSpec(
        num_scalar_prefetch=3,
        grid=(count // 2,),
        in_specs=specs(0) + specs(1),
        out_specs=pl.BlockSpec((2, rows, LAT), lambda i, pick, page, seen: (i, 0, 0)),
    )
    group = [own_queries, far_queries] + [kv_pool] * per
    return pl.pallas_call(
        attend_kernel,
        out_shape=jax.ShapeDtypeStruct((count, rows, LAT), bf16),
        grid_spec=spec,
        compiler_params=pltpu.CompilerParams(vmem_limit_bytes=32 * 2**20),
        cost_estimate=pl.CostEstimate(
            flops=count * rows * 512 * 1088 * 2, bytes_accessed=12_000_000, transcendentals=0
        ),
        name="attend",
    )(pick, pages, seen, *group, *group)


def cut_kernel(spot_ref, gate_ref, up_ref, down_ref, rows_ref, cols_ref):
    units = gate_ref.shape[2]
    rows_ref[:, :units] = gate_ref[0]
    rows_ref[:, units:] = up_ref[0]
    cols_ref[...] = down_ref[0]


def cut_weights(spots, w_gate, w_up, w_down):
    units, model = w_down.shape[1:]
    wide = model // HEAD_N
    rows = pl.BlockSpec((1, wide, units), lambda i, spot: (0, spot[i], 0))
    spec = pltpu.PrefetchScalarGridSpec(
        num_scalar_prefetch=1,
        grid=(RING,),
        in_specs=[rows, rows, pl.BlockSpec((1, units, wide), lambda i, spot: (0, 0, spot[i]))],
        out_specs=[
            pl.BlockSpec((wide, 2 * units), lambda i, spot: (i, 0)),
            pl.BlockSpec((units, wide), lambda i, spot: (0, i)),
        ],
    )
    return pl.pallas_call(
        cut_kernel,
        out_shape=[
            jax.ShapeDtypeStruct((model // 2, 2 * units), bf16),
            jax.ShapeDtypeStruct((units, model // 2), bf16),
        ],
        grid_spec=spec,
        compiler_params=pltpu.CompilerParams(vmem_limit_bytes=32 * 2**20),
        cost_estimate=pl.CostEstimate(flops=0, bytes_accessed=11_000_000, transcendentals=0),
        name="cut_weights",
    )(spots, w_gate, w_up, w_down)


def before(count):
    at = jnp.arange(count, dtype=i32)
    return at[:, None] < at[None, :]


def shards(
    queries,
    kv_pool,
    page_table,
    cache_len,
    accepted,
    w_uv,
    w_o,
    residual,
    norm_gain,
    expert_ids,
    gate_weights,
    w_gate,
    w_up,
    w_down,
):
    at_x, at_y, at_z = lax.axis_index("x"), lax.axis_index("y"), lax.axis_index("z")
    at_core = lax.axis_index("core")
    dp_index = at_y * RING + at_z
    requests = page_table.shape[0]
    tokens, head_group, width = queries.shape
    query_rows = queries.reshape(requests, 3 * head_group, width)
    dps = jnp.arange(DP_N, dtype=i32)
    me = dp_index.astype(i32)[None]

    packed = pack(me, page_table, cache_len, accepted, query_rows)
    arrived = lax.all_to_all(packed, DP, 0, 0, tiled=True)
    told = arrived[:, 0, width:]
    lenders = told[:, 24:40].astype(i32)
    line = told[:, 8:24].astype(i32)
    latent = attend(
        *plan(me, page_table, cache_len, accepted, line), query_rows, arrived, kv_pool
    )
    values = jnp.einsum(
        "thc,hcv->thv",
        latent.reshape(tokens, head_group, LAT),
        w_uv,
        preferred_element_type=f32,
    ).astype(bf16)
    values = values.reshape(tokens, head_group * w_uv.shape[2])

    values, w_gate, w_up, w_down = lax.optimization_barrier((values, w_gate, w_up, w_down))
    ring_at = (at_x + jnp.arange(RING, dtype=i32)) % RING * 2
    in_give, out_give = cut_weights(ring_at + 1 - at_core, w_gate, w_up, w_down)
    in_own, out_own = cut_weights(ring_at + at_core, w_gate, w_up, w_down)
    in_other, out_other = other_core(in_give), other_core(out_give)

    half = values.shape[1] // 2

    def spread(block, first, second):
        line = jnp.concatenate([block] + [hop(block, first, k) for k in (1, 2, 3)], axis=0)
        return [line] + [hop(line, second, k) for k in (1, 2, 3)]

    zy = spread(values[:, :half], "z", "y")
    yz = spread(values[:, half:], "y", "z")
    part_zy = jnp.concatenate(
        [jnp.dot(a, w_o[:half], preferred_element_type=f32) for a in zy], axis=0
    )
    part_yz = jnp.concatenate(
        [jnp.dot(a, w_o[half:], preferred_element_type=f32) for a in yz], axis=0
    )
    columns = w_o.shape[1]
    part_yz = part_yz.reshape(RING, RING, tokens, columns).transpose(1, 0, 2, 3)
    projected = (part_zy + part_yz.reshape(-1, columns)).astype(bf16)

    is_own = (lenders == dps[:, None]).astype(i32)
    own_slot = jnp.sum(is_own[:, :, None] * before(requests)[None], axis=1)
    at_lender = (lenders[:, :, None] == dps[None, None, :]).astype(i32)
    away = at_lender * (dps[:, None, None] != dps[None, None, :])
    lends = jnp.sum(away, axis=1)
    lend_rank = jnp.sum(before(DP_N)[:, :, None] * lends[:, None, :], axis=0)
    far_slot = 8 + jnp.sum(at_lender * lend_rank[:, None, :], axis=2)
    slot = jnp.where(is_own > 0, own_slot, far_slot)
    turned = ((lenders // RING - at_y) % RING) * RING + (lenders % RING - at_z) % RING
    first_row = (turned * requests + slot) * 3
    source = (first_row[:, :, None] + jnp.arange(3, dtype=i32)).reshape(RING, 2, 2 * tokens)
    source = lax.dynamic_slice_in_dim(jnp.concatenate([source, source], 0), at_x, RING, 0)
    source = lax.dynamic_slice_in_dim(jnp.concatenate([source, source], 1), at_core, 2, 1)
    source = source.transpose(1, 0, 2).reshape(-1)
    rows_all = projected.shape[0]
    moves = (source[:, None] == jnp.arange(rows_all, dtype=i32)[None, :]).astype(bf16)
    homed = jnp.dot(moves, projected, preferred_element_type=f32)
    kept = homed[: rows_all // 2] + other_core(homed[rows_all // 2 :].astype(bf16)).astype(f32)
    kept = kept.reshape(RING, 2 * tokens, columns)
    mine = kept[0]
    for k in (2, 1, 3):
        mine = mine + send(kept[k].astype(bf16), "x", k).astype(f32)
    mine = mine.astype(bf16)

    odd = dp_index % 2
    low, high = mine[:tokens], mine[tokens:]
    got = []
    for turn in (0, 1):
        pairs = []
        for d in range(DP_N):
            for h in range(HEAD_N):
                pairs.append((d * HEAD_N + h, (2 * h + (turn + d) % 2) * HEAD_N + d // 2))
        block = jnp.where((odd + turn) % 2 == 0, low, high)
        got.append(lax.ppermute(block, ALL, pairs))
    attention = jnp.concatenate(
        [jnp.where(odd == 0, got[0], got[1]), jnp.where(odd == 0, got[1], got[0])], axis=1
    )
    wide_piece = 2 * columns
    head_index = at_x * 2 + at_core
    near = lax.dynamic_slice_in_dim(residual, head_index * wide_piece, wide_piece, 1)
    piece = (near.astype(f32) + attention.astype(f32)).astype(bf16)
    piece, in_own, in_other, out_own, out_other = lax.optimization_barrier(
        (piece, in_own, in_other, out_own, out_other)
    )

    here = jnp.concatenate([piece] + [hop(piece, "x", k) for k in (1, 2, 3)], axis=1)
    there = other_core(here)
    wide, wide_there = here.astype(f32), there.astype(f32)
    squares = jnp.sum(wide * wide, axis=1, keepdims=True) + jnp.sum(
        wide_there * wide_there, axis=1, keepdims=True
    )
    gains = jnp.concatenate([norm_gain, norm_gain]).reshape(2 * RING, 2, wide_piece)
    gains = lax.dynamic_slice(gains, (at_x, at_core, 0), (RING, 1, wide_piece)).reshape(1, -1)
    model = residual.shape[1]
    normed = (wide * lax.rsqrt(squares / model + norm_eps) * gains).astype(bf16)
    first = jnp.where(at_core == 0, here, there)
    second = jnp.where(at_core == 0, there, here)
    blocks = []
    for k in range(RING):
        for side in (first, second):
            blocks.append(side[:, k * wide_piece : (k + 1) * wide_piece])
    row = jnp.concatenate(blocks + blocks, axis=1)
    attended = lax.dynamic_slice_in_dim(row, (RING - at_x) % RING * 2 * wide_piece, model, 1)

    chosen = (expert_ids[:, :, None] == dps[None, None, :]).astype(i32)
    named = jnp.sum(chosen, axis=1)
    weight = jnp.sum(chosen.astype(f32) * gate_weights[:, :, None], axis=1)
    rank = jnp.sum(before(tokens)[:, :, None] * named[:, None, :], axis=0)
    rank = jnp.where(named > 0, rank, -1)
    ranks = jnp.arange(CAP, dtype=i32)
    placing = (rank.T[:, None, :] == ranks[None, :, None]).astype(bf16)
    placing = placing.reshape(DP_N * CAP, tokens)
    outgoing = jnp.dot(placing, normed, preferred_element_type=f32).astype(bf16)
    rows = lax.all_to_all(outgoing.reshape(DP_N, CAP, -1), DP, 0, 0, tiled=True)
    rows = rows.reshape(DP_N * CAP, -1)

    units = w_gate.shape[2]
    sums = jnp.dot(rows, in_own, preferred_element_type=f32)
    give = jnp.dot(rows, in_other, preferred_element_type=f32)
    swapped = other_core(jnp.concatenate([give, sums], axis=1).astype(bf16)).astype(f32)
    own_sum = sums + swapped[:, : 2 * units]
    other_sum = give + swapped[:, 2 * units :]
    hidden = [jax.nn.silu(a[:, :units]) * a[:, units:] for a in (own_sum, other_sum)]
    hidden = lax.optimization_barrier([a.astype(bf16) for a in hidden])
    output = jnp.dot(hidden[0], out_own, preferred_element_type=f32) + jnp.dot(
        hidden[1], out_other, preferred_element_type=f32
    )
    output = output.astype(bf16).reshape(DP_N, CAP, -1)
    returned = lax.all_to_all(output, DP, 0, 0, tiled=True).reshape(DP_N * CAP, -1)

    mix = jnp.where(rank[:, :, None] == ranks[None, None, :], weight[:, :, None], 0.0)
    mix = mix.reshape(tokens, DP_N * CAP)
    coarse = lax.reduce_precision(mix, 8, 7)
    both = jnp.concatenate([coarse.astype(bf16), (mix - coarse).astype(bf16)], axis=0)
    both = jnp.dot(both, returned, preferred_element_type=f32)
    mixed = both[:tokens] + both[tokens:]
    routed = mixed[:, :wide_piece]
    for k in (2, 1, 3):
        block = mixed[:, k * wide_piece : (k + 1) * wide_piece].astype(bf16)
        routed = routed + send(block, "x", k).astype(f32)
    return (attended, routed.astype(bf16))


def solution(mesh):
    grid = Mesh(mesh.devices.reshape(RING, RING, RING, 2), ALL)
    return jax.shard_map(
        shards,
        mesh=grid,
        in_specs=(
            P(DP, HEAD, None),
            P(DP, None, None),
            P(DP, None),
            P(DP),
            P(DP),
            P(HEAD, None, None),
            P(HEAD, DP),
            P(DP, None),
            P(),
            P(DP, None),
            P(DP, None),
            P(DP, None, HEAD),
            P(DP, None, HEAD),
            P(DP, HEAD, None),
        ),
        out_specs=(P(DP, None), P(DP, HEAD)),
        check_vma=False,
    )
```

```python
import jax
import jax.numpy as jnp
from jax import lax
from jax.experimental import pallas as pl
from jax.experimental.pallas import tpu as pltpu
from jax.sharding import Mesh
from jax.sharding import PartitionSpec as P

LAT = 512
DP = ("y", "z")
HEAD = ("x", "core")
ALL = ("y", "z", "x", "core")
RING = 4
DP_N = 16
HEAD_N = 8
PAGES = 128
CAP = 32

softmax_scale = 192.0 ** (-0.5)
norm_eps = 1e-06
bf16 = jnp.bfloat16
f32 = jnp.float32
i32 = jnp.int32


def hop(array, axis, step):
    return lax.ppermute(array, axis, [((i + step) % RING, i) for i in range(RING)])


def send(array, axis, step):
    return lax.ppermute(array, axis, [(i, (i + step) % RING) for i in range(RING)])


def other_core(array):
    return lax.ppermute(array, "core", [(0, 1), (1, 0)])


def pack_kernel(me_ref, page_ref, held_ref, taken_ref, query_ref, out_ref, who_ref):
    me = me_ref[0]
    width = query_ref.shape[2]
    requests, per = page_ref.shape
    rows = out_ref.shape[1]
    lanes = out_ref.shape[2] - width

    row = lax.broadcasted_iota(i32, (rows, lanes), 0)
    lane = lax.broadcasted_iota(i32, (rows, lanes), 1)

    def clear(i, carry):
        who_ref[i] = -1
        return carry

    lax.fori_loop(0, DP_N, clear, 0)
    lane = jnp.where(row == 0, lane, -1)
    base = jnp.zeros((rows, lanes), f32)
    for r in range(requests):
        lender = page_ref[r, 0] // PAGES
        base = jnp.where(lane == 24 + r, lender.astype(f32), base)

        @pl.when(lender != me)
        def _():
            who_ref[lender] = r

    def one(i, carry):
        found = who_ref[i]
        r = jnp.maximum(found, 0)
        seen = held_ref[r] + taken_ref[r]
        told = [page_ref[r, k] - page_ref[r, 0] // PAGES * PAGES for k in range(per)]
        told += [seen // 2, seen % 2, jnp.where(found >= 0, 1, 0)]
        line = base
        for k, value in enumerate(told):
            line = jnp.where(lane == 8 + k, value.astype(f32), line)
        out_ref[i, :, :width] = query_ref[r]
        out_ref[i, :, width:] = line.astype(bf16)
        return carry

    lax.fori_loop(0, DP_N, one, 0)


def pack(me, page_table, cache_len, accepted, query_rows):
    count, rows, width = query_rows.shape
    scalar, vector = (pl.BlockSpec(memory_space=m) for m in (pltpu.SMEM, pltpu.VMEM))
    return pl.pallas_call(
        pack_kernel,
        out_shape=jax.ShapeDtypeStruct((DP_N, rows, width + 64), bf16),
        in_specs=[scalar] * 4 + [vector],
        out_specs=vector,
        scratch_shapes=[pltpu.SMEM((DP_N,), i32)],
        compiler_params=pltpu.CompilerParams(vmem_limit_bytes=32 * 2**20),
        name="pack",
    )(me, page_table, cache_len, accepted, query_rows)


def plan_kernel(
    me_ref, page_ref, held_ref, taken_ref, told_ref, which_ref, list_ref, seen_ref
):
    me = me_ref[0]
    count, per = page_ref.shape

    def plan(r, found):
        own_at, far_at = found
        mine = page_ref[r, 0] // PAGES == me
        lent = told_ref[r, 10] > 0

        @pl.when(mine)
        def _():
            at = jnp.minimum(own_at, 7)
            which_ref[at] = r
            seen_ref[at] = held_ref[r] + taken_ref[r]
            for k in range(per):
                list_ref[at * per + k] = page_ref[r, k] - me * PAGES

        @pl.when(lent)
        def _():
            at = 8 + jnp.minimum(far_at, 7)
            which_ref[at] = r
            seen_ref[at] = told_ref[r, 8] * 2 + told_ref[r, 9]
            for k in range(per):
                list_ref[at * per + k] = told_ref[r, k]

        return own_at + mine.astype(i32), far_at + lent.astype(i32)

    lax.fori_loop(0, count, plan, (jnp.int32(0), jnp.int32(0)))


def plan(me, page_table, cache_len, accepted, told):
    count, per = page_table.shape
    scalar = pl.BlockSpec(memory_space=pltpu.SMEM)
    return pl.pallas_call(
        plan_kernel,
        out_shape=[
            jax.ShapeDtypeStruct((count,), i32),
            jax.ShapeDtypeStruct((count * per,), i32),
            jax.ShapeDtypeStruct((count,), i32),
        ],
        in_specs=[scalar] * 5,
        out_specs=[scalar] * 3,
        name="plan",
    )(me, page_table, cache_len, accepted, told)


def attend_kernel(pick_ref, page_ref, seen_ref, *refs):
    out_ref = refs[-1]
    step = pl.program_id(0)
    per = (len(refs) - 1) // 2
    for n in range(2):
        own_ref, far_ref, *pages = refs[n * per : (n + 1) * per]
        at = step * 2 + n
        width = own_ref.shape[2]
        queries = jnp.where(at < 8, own_ref[0], far_ref[0, :, :width])
        keys = jnp.concatenate([page[0] for page in pages], axis=0)
        scores = (
            lax.dot_general(queries, keys, (((1,), (1,)), ((), ())), preferred_element_type=f32)
            * softmax_scale
        )
        position = lax.broadcasted_iota(i32, scores.shape, 1)
        draft = lax.broadcasted_iota(i32, scores.shape, 0) // (scores.shape[0] // 3)
        allowed = position <= seen_ref[at] + draft
        highest = jnp.max(jnp.where(allowed, scores, -1e30), axis=-1, keepdims=True)
        weights = jnp.where(allowed, jnp.exp(jnp.where(allowed, scores - highest, 0.0)), 0.0)
        probs = (weights / jnp.sum(weights, axis=-1, keepdims=True)).astype(bf16)
        out_ref[n] = lax.dot_general(
            probs, keys[:, :LAT], (((1,), (0,)), ((), ())), preferred_element_type=f32
        ).astype(bf16)


def attend(pick, pages, seen, own_queries, far_queries, kv_pool):
    count, rows, width = own_queries.shape
    page_rows = kv_pool.shape[1]
    per = pages.shape[0] // count

    def specs(n):
        def own(i, pick, page, seen):
            return (pick[jnp.minimum(i * 2 + n, 6 + n)], 0, 0)

        def far(i, pick, page, seen):
            return (pick[jnp.maximum(i * 2 + n, 8 + n)], 0, 0)

        def page_spec(a):
            return pl.BlockSpec(
                (1, page_rows, width),
                lambda i, pick, page, seen: (page[(i * 2 + n) * per + a], 0, 0),
            )

        return [
            pl.BlockSpec((1, rows, width), own),
            pl.BlockSpec((1, rows, far_queries.shape[2]), far),
        ] + [page_spec(a) for a in range(per)]

    spec = pltpu.PrefetchScalarGridSpec(
        num_scalar_prefetch=3,
        grid=(count // 2,),
        in_specs=specs(0) + specs(1),
        out_specs=pl.BlockSpec((2, rows, LAT), lambda i, pick, page, seen: (i, 0, 0)),
    )
    group = [own_queries, far_queries] + [kv_pool] * per
    return pl.pallas_call(
        attend_kernel,
        out_shape=jax.ShapeDtypeStruct((count, rows, LAT), bf16),
        grid_spec=spec,
        compiler_params=pltpu.CompilerParams(vmem_limit_bytes=32 * 2**20),
        cost_estimate=pl.CostEstimate(
            flops=count * rows * 512 * 1088 * 2, bytes_accessed=12_000_000, transcendentals=0
        ),
        name="attend",
    )(pick, pages, seen, *group, *group)


def before(count):
    at = jnp.arange(count, dtype=i32)
    return at[:, None] < at[None, :]


def shards(
    queries,
    kv_pool,
    page_table,
    cache_len,
    accepted,
    w_uv,
    w_o,
    residual,
    norm_gain,
    expert_ids,
    gate_weights,
    w_gate,
    w_up,
    w_down,
):
    at_x, at_y, at_z = lax.axis_index("x"), lax.axis_index("y"), lax.axis_index("z")
    at_core = lax.axis_index("core")
    dp_index = at_y * RING + at_z
    requests = page_table.shape[0]
    tokens, head_group, width = queries.shape
    query_rows = queries.reshape(requests, 3 * head_group, width)
    dps = jnp.arange(DP_N, dtype=i32)
    me = dp_index.astype(i32)[None]

    packed = pack(me, page_table, cache_len, accepted, query_rows)
    arrived = lax.all_to_all(packed, DP, 0, 0, tiled=True)
    told = arrived[:, 0, width:]
    lenders = told[:, 24:40].astype(i32)
    line = told[:, 8:24].astype(i32)
    latent = attend(
        *plan(me, page_table, cache_len, accepted, line), query_rows, arrived, kv_pool
    )
    values = jnp.einsum(
        "thc,hcv->thv",
        latent.reshape(tokens, head_group, LAT),
        w_uv,
        preferred_element_type=f32,
    ).astype(bf16)
    values = values.reshape(tokens, head_group * w_uv.shape[2])

    half = values.shape[1] // 2

    def spread(block, first, second):
        line = jnp.concatenate([block] + [hop(block, first, k) for k in (1, 2, 3)], axis=0)
        return [line] + [hop(line, second, k) for k in (1, 2, 3)]

    zy = spread(values[:, :half], "z", "y")
    yz = spread(values[:, half:], "y", "z")
    part_zy = jnp.concatenate(
        [jnp.dot(a, w_o[:half], preferred_element_type=f32) for a in zy], axis=0
    )
    part_yz = jnp.concatenate(
        [jnp.dot(a, w_o[half:], preferred_element_type=f32) for a in yz], axis=0
    )
    columns = w_o.shape[1]
    part_yz = part_yz.reshape(RING, RING, tokens, columns).transpose(1, 0, 2, 3)
    projected = (part_zy + part_yz.reshape(-1, columns)).astype(bf16)

    is_own = (lenders == dps[:, None]).astype(i32)
    own_slot = jnp.sum(is_own[:, :, None] * before(requests)[None], axis=1)
    at_lender = (lenders[:, :, None] == dps[None, None, :]).astype(i32)
    away = at_lender * (dps[:, None, None] != dps[None, None, :])
    lends = jnp.sum(away, axis=1)
    lend_rank = jnp.sum(before(DP_N)[:, :, None] * lends[:, None, :], axis=0)
    far_slot = 8 + jnp.sum(at_lender * lend_rank[:, None, :], axis=2)
    slot = jnp.where(is_own > 0, own_slot, far_slot)
    turned = ((lenders // RING - at_y) % RING) * RING + (lenders % RING - at_z) % RING
    first_row = (turned * requests + slot) * 3
    source = (first_row[:, :, None] + jnp.arange(3, dtype=i32)).reshape(RING, 2, 2 * tokens)
    source = lax.dynamic_slice_in_dim(jnp.concatenate([source, source], 0), at_x, RING, 0)
    source = lax.dynamic_slice_in_dim(jnp.concatenate([source, source], 1), at_core, 2, 1)
    source = source.transpose(1, 0, 2).reshape(-1)
    rows_all = projected.shape[0]
    moves = (source[:, None] == jnp.arange(rows_all, dtype=i32)[None, :]).astype(bf16)
    homed = jnp.dot(moves, projected, preferred_element_type=f32)
    kept = homed[: rows_all // 2] + other_core(homed[rows_all // 2 :].astype(bf16)).astype(f32)
    kept = kept.reshape(RING, 2 * tokens, columns)
    mine = kept[0]
    for k in (2, 1, 3):
        mine = mine + send(kept[k].astype(bf16), "x", k).astype(f32)
    mine = mine.astype(bf16)

    odd = dp_index % 2
    low, high = mine[:tokens], mine[tokens:]
    got = []
    for turn in (0, 1):
        pairs = []
        for d in range(DP_N):
            for h in range(HEAD_N):
                pairs.append((d * HEAD_N + h, (2 * h + (turn + d) % 2) * HEAD_N + d // 2))
        block = jnp.where((odd + turn) % 2 == 0, low, high)
        got.append(lax.ppermute(block, ALL, pairs))
    attention = jnp.concatenate(
        [jnp.where(odd == 0, got[0], got[1]), jnp.where(odd == 0, got[1], got[0])], axis=1
    )
    wide_piece = 2 * columns
    head_index = at_x * 2 + at_core
    near = lax.dynamic_slice_in_dim(residual, head_index * wide_piece, wide_piece, 1)
    piece = (near.astype(f32) + attention.astype(f32)).astype(bf16)

    here = jnp.concatenate([piece] + [hop(piece, "x", k) for k in (1, 2, 3)], axis=1)
    there = other_core(here)
    wide, wide_there = here.astype(f32), there.astype(f32)
    squares = jnp.sum(wide * wide, axis=1, keepdims=True) + jnp.sum(
        wide_there * wide_there, axis=1, keepdims=True
    )
    gains = jnp.concatenate([norm_gain, norm_gain]).reshape(2 * RING, 2, wide_piece)
    gains = lax.dynamic_slice(gains, (at_x, at_core, 0), (RING, 1, wide_piece)).reshape(1, -1)
    model = residual.shape[1]
    normed = (wide * lax.rsqrt(squares / model + norm_eps) * gains).astype(bf16)
    first = jnp.where(at_core == 0, here, there)
    second = jnp.where(at_core == 0, there, here)
    blocks = []
    for k in range(RING):
        for side in (first, second):
            blocks.append(side[:, k * wide_piece : (k + 1) * wide_piece])
    row = jnp.concatenate(blocks + blocks, axis=1)
    attended = lax.dynamic_slice_in_dim(row, (RING - at_x) % RING * 2 * wide_piece, model, 1)

    chosen = (expert_ids[:, :, None] == dps[None, None, :]).astype(i32)
    named = jnp.sum(chosen, axis=1)
    weight = jnp.sum(chosen.astype(f32) * gate_weights[:, :, None], axis=1)
    rank = jnp.sum(before(tokens)[:, :, None] * named[:, None, :], axis=0)
    rank = jnp.where(named > 0, rank, -1)
    ranks = jnp.arange(CAP, dtype=i32)
    placing = (rank.T[:, None, :] == ranks[None, :, None]).astype(bf16)
    placing = placing.reshape(DP_N * CAP, tokens)

    cut = 3 * wide_piece // 7
    early = normed[:, :cut]
    doubled = [normed[:, k * wide_piece + cut : (k + 1) * wide_piece] for k in range(RING)]
    rest = wide_piece - cut
    back = (RING - at_x) % RING
    late = lax.dynamic_slice_in_dim(
        jnp.concatenate(doubled + doubled, axis=1), back * rest, RING * rest, 1
    )

    def to_experts(block):
        block = jnp.dot(placing, block, preferred_element_type=f32).astype(bf16)
        block = lax.all_to_all(block.reshape(DP_N, CAP, -1), DP, 0, 0, tiled=True)
        return block.reshape(DP_N * CAP, -1)

    early = to_experts(early)
    early, late = lax.optimization_barrier((early, late))
    late = to_experts(late)
    early = [early] + [hop(early, "x", k) for k in (1, 2, 3)]
    early = lax.dynamic_slice_in_dim(
        jnp.concatenate(early + early, axis=1), back * cut, RING * cut, 1
    )

    def in_rows(core, low, high):
        blocks = []
        for weights in (w_gate, w_up):
            view = weights[0].reshape(RING, 2, wide_piece, -1)
            view = lax.dynamic_slice_in_dim(view, core, 1, 1)[:, 0, low:high]
            blocks.append(view.reshape(RING * (high - low), -1))
        return jnp.concatenate(blocks, axis=1)

    def out_columns(core, low, high):
        return jnp.concatenate(
            [
                lax.dynamic_slice_in_dim(
                    w_down[0], (2 * k + core) * wide_piece + low, high - low, 1
                )
                for k in range(RING)
            ],
            axis=1,
        )

    units = w_gate.shape[2]
    away = 1 - at_core
    sums = (
        jnp.dot(early, in_rows(at_core, 0, cut), preferred_element_type=f32)
        + jnp.dot(other_core(early), in_rows(away, 0, cut), preferred_element_type=f32)
        + jnp.dot(late, in_rows(at_core, cut, wide_piece), preferred_element_type=f32)
        + jnp.dot(other_core(late), in_rows(away, cut, wide_piece), preferred_element_type=f32)
    )
    hidden = (jax.nn.silu(sums[:, :units]) * sums[:, units:]).astype(bf16)
    hidden = lax.optimization_barrier(hidden)

    def output(low, high):
        give = jnp.dot(hidden, out_columns(away, low, high), preferred_element_type=f32)
        keep = jnp.dot(hidden, out_columns(at_core, low, high), preferred_element_type=f32)
        return keep + other_core(give.astype(bf16)).astype(f32)

    def to_home(block):
        block = lax.all_to_all(block.reshape(DP_N, CAP, -1), DP, 0, 0, tiled=True)
        return block.reshape(DP_N * CAP, -1)

    def ring_sum(block, size):
        block = jnp.concatenate([block, block], axis=1)
        block = lax.dynamic_slice_in_dim(block, at_x * size, RING * size, 1)
        total = block[:, :size].astype(f32)
        for k in (2, 1, 3):
            total = total + send(block[:, k * size : (k + 1) * size], "x", k).astype(f32)
        return total

    late = output(cut, wide_piece).astype(bf16)
    early, late = lax.optimization_barrier((output(0, cut).astype(bf16), late))
    late = to_home(late)
    early, late = lax.optimization_barrier((ring_sum(early, cut).astype(bf16), late))
    early = to_home(early)

    mix = jnp.where(rank[:, :, None] == ranks[None, None, :], weight[:, :, None], 0.0)
    mix = mix.reshape(tokens, DP_N * CAP)
    coarse = lax.reduce_precision(mix, 8, 7)
    both = jnp.concatenate([coarse.astype(bf16), (mix - coarse).astype(bf16)], axis=0)

    def mixed(block):
        block = jnp.dot(both, block, preferred_element_type=f32)
        return block[:tokens] + block[tokens:]

    late = ring_sum(mixed(late).astype(bf16), rest)
    routed = jnp.concatenate([mixed(early), late], axis=1).astype(bf16)
    return (attended, routed)


def solution(mesh):
    grid = Mesh(mesh.devices.reshape(RING, RING, RING, 2), ALL)
    return jax.shard_map(
        shards,
        mesh=grid,
        in_specs=(
            P(DP, HEAD, None),
            P(DP, None, None),
            P(DP, None),
            P(DP),
            P(DP),
            P(HEAD, None, None),
            P(HEAD, DP),
            P(DP, None),
            P(),
            P(DP, None),
            P(DP, None),
            P(DP, None, HEAD),
            P(DP, None, HEAD),
            P(DP, HEAD, None),
        ),
        out_specs=(P(DP, None), P(DP, HEAD)),
        check_vma=False,
    )
```

```python
import jax
import jax.numpy as jnp
from jax import lax
from jax.experimental import pallas as pl
from jax.experimental.pallas import tpu as pltpu
from jax.sharding import Mesh
from jax.sharding import PartitionSpec as P

LAT = 512
DP = ("y", "z")
HEAD = ("x", "core")
ALL = ("y", "z", "x", "core")
RING = 4
DP_N = 16
HEAD_N = 8
PAGES = 128
CAP = 32

softmax_scale = 192.0 ** (-0.5)
norm_eps = 1e-06
bf16 = jnp.bfloat16
f32 = jnp.float32
i32 = jnp.int32


def hop(array, axis, step):
    return lax.ppermute(array, axis, [((i + step) % RING, i) for i in range(RING)])


def send(array, axis, step):
    return lax.ppermute(array, axis, [(i, (i + step) % RING) for i in range(RING)])


def other_core(array):
    return lax.ppermute(array, "core", [(0, 1), (1, 0)])


def pack_kernel(me_ref, page_ref, held_ref, taken_ref, query_ref, out_ref, who_ref):
    me = me_ref[0]
    width = query_ref.shape[2]
    requests, per = page_ref.shape
    rows = out_ref.shape[1]
    lanes = out_ref.shape[2] - width

    row = lax.broadcasted_iota(i32, (rows, lanes), 0)
    lane = lax.broadcasted_iota(i32, (rows, lanes), 1)

    def clear(i, carry):
        who_ref[i] = -1
        return carry

    lax.fori_loop(0, DP_N, clear, 0)
    lane = jnp.where(row == 0, lane, -1)
    base = jnp.zeros((rows, lanes), f32)
    for r in range(requests):
        lender = page_ref[r, 0] // PAGES
        base = jnp.where(lane == 24 + r, lender.astype(f32), base)

        @pl.when(lender != me)
        def _():
            who_ref[lender] = r

    def one(i, carry):
        found = who_ref[i]
        r = jnp.maximum(found, 0)
        seen = held_ref[r] + taken_ref[r]
        told = [page_ref[r, k] - page_ref[r, 0] // PAGES * PAGES for k in range(per)]
        told += [seen // 2, seen % 2, jnp.where(found >= 0, 1, 0)]
        line = base
        for k, value in enumerate(told):
            line = jnp.where(lane == 8 + k, value.astype(f32), line)
        out_ref[i, :, :width] = query_ref[r]
        out_ref[i, :, width:] = line.astype(bf16)
        return carry

    lax.fori_loop(0, DP_N, one, 0)


def pack(me, page_table, cache_len, accepted, query_rows):
    count, rows, width = query_rows.shape
    scalar, vector = (pl.BlockSpec(memory_space=m) for m in (pltpu.SMEM, pltpu.VMEM))
    return pl.pallas_call(
        pack_kernel,
        out_shape=jax.ShapeDtypeStruct((DP_N, rows, width + 64), bf16),
        in_specs=[scalar] * 4 + [vector],
        out_specs=vector,
        scratch_shapes=[pltpu.SMEM((DP_N,), i32)],
        compiler_params=pltpu.CompilerParams(vmem_limit_bytes=32 * 2**20),
        name="pack",
    )(me, page_table, cache_len, accepted, query_rows)


def attend_kernel(
    me_ref, page_ref, held_ref, taken_ref, told_ref, own_ref, far_ref, pool_ref, out_ref,
    which_ref, list_ref, seen_ref,
):
    me = me_ref[0]
    count, rows, width = own_ref.shape
    per = page_ref.shape[1]

    def plan(r, found):
        own_at, far_at = found
        mine = page_ref[r, 0] // PAGES == me
        lent = told_ref[r, 10] > 0

        @pl.when(mine)
        def _():
            at = jnp.minimum(own_at, 7)
            which_ref[at] = r
            seen_ref[at] = held_ref[r] + taken_ref[r]
            for k in range(per):
                list_ref[at * per + k] = page_ref[r, k] - me * PAGES

        @pl.when(lent)
        def _():
            at = 8 + jnp.minimum(far_at, 7)
            which_ref[at] = r
            seen_ref[at] = told_ref[r, 8] * 2 + told_ref[r, 9]
            for k in range(per):
                list_ref[at * per + k] = told_ref[r, k]

        return own_at + mine.astype(i32), far_at + lent.astype(i32)

    lax.fori_loop(0, count, plan, (jnp.int32(0), jnp.int32(0)))

    def one(at, source):
        queries = source[which_ref[at], :, :width]
        keys = jnp.concatenate([pool_ref[list_ref[at * per + k]] for k in range(per)], axis=0)
        scores = (
            lax.dot_general(queries, keys, (((1,), (1,)), ((), ())), preferred_element_type=f32)
            * softmax_scale
        )
        position = lax.broadcasted_iota(i32, scores.shape, 1)
        draft = lax.broadcasted_iota(i32, scores.shape, 0) // (scores.shape[0] // 3)
        allowed = position <= seen_ref[at] + draft
        highest = jnp.max(jnp.where(allowed, scores, -1e30), axis=-1, keepdims=True)
        weights = jnp.where(allowed, jnp.exp(jnp.where(allowed, scores - highest, 0.0)), 0.0)
        probs = (weights / jnp.sum(weights, axis=-1, keepdims=True)).astype(bf16)
        out_ref[at] = lax.dot_general(
            probs, keys[:, :LAT], (((1,), (0,)), ((), ())), preferred_element_type=f32
        ).astype(bf16)

    def turn(i, carry):
        one(i, own_ref)
        one(8 + i, far_ref)
        return carry

    lax.fori_loop(0, 8, turn, 0)


def attend(me, page_table, cache_len, accepted, told, own_queries, far_queries, kv_pool):
    count, rows, width = own_queries.shape
    per = page_table.shape[1]
    scalar, vector = (pl.BlockSpec(memory_space=m) for m in (pltpu.SMEM, pltpu.VMEM))
    return pl.pallas_call(
        attend_kernel,
        out_shape=jax.ShapeDtypeStruct((count, rows, LAT), bf16),
        in_specs=[scalar] * 5 + [vector] * 3,
        out_specs=vector,
        scratch_shapes=[
            pltpu.SMEM((count,), i32),
            pltpu.SMEM((count * per,), i32),
            pltpu.SMEM((count,), i32),
        ],
        compiler_params=pltpu.CompilerParams(vmem_limit_bytes=40 * 2**20),
        cost_estimate=pl.CostEstimate(
            flops=count * rows * 512 * 1088 * 2, bytes_accessed=12_000_000, transcendentals=0
        ),
        name="attend",
    )(me, page_table, cache_len, accepted, told, own_queries, far_queries, kv_pool)


def before(count):
    at = jnp.arange(count, dtype=i32)
    return at[:, None] < at[None, :]


def shards(
    queries,
    kv_pool,
    page_table,
    cache_len,
    accepted,
    w_uv,
    w_o,
    residual,
    norm_gain,
    expert_ids,
    gate_weights,
    w_gate,
    w_up,
    w_down,
):
    at_x, at_y, at_z = lax.axis_index("x"), lax.axis_index("y"), lax.axis_index("z")
    at_core = lax.axis_index("core")
    dp_index = at_y * RING + at_z
    requests = page_table.shape[0]
    tokens, head_group, width = queries.shape
    query_rows = queries.reshape(requests, 3 * head_group, width)
    dps = jnp.arange(DP_N, dtype=i32)
    me = dp_index.astype(i32)[None]

    packed = pack(me, page_table, cache_len, accepted, query_rows)
    arrived = lax.all_to_all(packed, DP, 0, 0, tiled=True)
    told = arrived[:, 0, width:]
    lenders = told[:, 24:40].astype(i32)
    line = told[:, 8:24].astype(i32)
    latent = attend(me, page_table, cache_len, accepted, line, query_rows, arrived, kv_pool)
    values = jnp.einsum(
        "thc,hcv->thv",
        latent.reshape(tokens, head_group, LAT),
        w_uv,
        preferred_element_type=f32,
    ).astype(bf16)
    values = values.reshape(tokens, head_group * w_uv.shape[2])

    half = values.shape[1] // 2

    def spread(block, first, second):
        line = jnp.concatenate([block] + [hop(block, first, k) for k in (1, 2, 3)], axis=0)
        return [line] + [hop(line, second, k) for k in (1, 2, 3)]

    zy = spread(values[:, :half], "z", "y")
    yz = spread(values[:, half:], "y", "z")
    part_zy = jnp.concatenate(
        [jnp.dot(a, w_o[:half], preferred_element_type=f32) for a in zy], axis=0
    )
    part_yz = jnp.concatenate(
        [jnp.dot(a, w_o[half:], preferred_element_type=f32) for a in yz], axis=0
    )
    columns = w_o.shape[1]
    part_yz = part_yz.reshape(RING, RING, tokens, columns).transpose(1, 0, 2, 3)
    projected = (part_zy + part_yz.reshape(-1, columns)).astype(bf16)

    is_own = (lenders == dps[:, None]).astype(i32)
    own_slot = jnp.sum(is_own[:, :, None] * before(requests)[None], axis=1)
    at_lender = (lenders[:, :, None] == dps[None, None, :]).astype(i32)
    away = at_lender * (dps[:, None, None] != dps[None, None, :])
    lends = jnp.sum(away, axis=1)
    lend_rank = jnp.sum(before(DP_N)[:, :, None] * lends[:, None, :], axis=0)
    far_slot = 8 + jnp.sum(at_lender * lend_rank[:, None, :], axis=2)
    slot = jnp.where(is_own > 0, own_slot, far_slot)
    turned = ((lenders // RING - at_y) % RING) * RING + (lenders % RING - at_z) % RING
    first_row = (turned * requests + slot) * 3
    source = (first_row[:, :, None] + jnp.arange(3, dtype=i32)).reshape(-1)
    rows_all = projected.shape[0]
    moves = (source[:, None] == jnp.arange(rows_all, dtype=i32)[None, :]).astype(bf16)
    homed = jnp.dot(moves, projected, preferred_element_type=f32).astype(bf16)
    homed = lax.all_to_all(homed.reshape(DP_N, tokens, columns), DP, 0, 0, tiled=True)

    wide_piece = DP_N * columns // HEAD_N
    homed = homed.reshape(RING, 2, 2, tokens, columns)
    homed = lax.dynamic_slice_in_dim(jnp.concatenate([homed, homed], 0), at_x, RING, 0)
    keep = lax.dynamic_slice_in_dim(homed, at_core, 1, 1)[:, 0]
    give = lax.dynamic_slice_in_dim(homed, 1 - at_core, 1, 1)[:, 0]
    kept = keep.astype(f32) + other_core(give).astype(f32)
    attention = kept[0]
    for k in (2, 1, 3):
        attention = attention + send(kept[k].astype(bf16), "x", k).astype(f32)
    attention = jnp.concatenate([attention[0], attention[1]], axis=1)
    head_index = at_x * 2 + at_core
    near = lax.dynamic_slice_in_dim(residual, head_index * wide_piece, wide_piece, 1)
    piece = (near.astype(f32) + attention).astype(bf16)

    here = jnp.concatenate([piece] + [hop(piece, "x", k) for k in (1, 2, 3)], axis=1)
    there = other_core(here)
    wide, wide_there = here.astype(f32), there.astype(f32)
    squares = jnp.sum(wide * wide, axis=1, keepdims=True) + jnp.sum(
        wide_there * wide_there, axis=1, keepdims=True
    )
    gains = jnp.concatenate([norm_gain, norm_gain]).reshape(2 * RING, 2, wide_piece)
    gains = lax.dynamic_slice(gains, (at_x, at_core, 0), (RING, 1, wide_piece)).reshape(1, -1)
    model = residual.shape[1]
    normed = (wide * lax.rsqrt(squares / model + norm_eps) * gains).astype(bf16)
    first = jnp.where(at_core == 0, here, there)
    second = jnp.where(at_core == 0, there, here)
    blocks = []
    for k in range(RING):
        for side in (first, second):
            blocks.append(side[:, k * wide_piece : (k + 1) * wide_piece])
    row = jnp.concatenate(blocks + blocks, axis=1)
    attended = lax.dynamic_slice_in_dim(row, (RING - at_x) % RING * 2 * wide_piece, model, 1)

    chosen = (expert_ids[:, :, None] == dps[None, None, :]).astype(i32)
    named = jnp.sum(chosen, axis=1)
    weight = jnp.sum(chosen.astype(f32) * gate_weights[:, :, None], axis=1)
    rank = jnp.sum(before(tokens)[:, :, None] * named[:, None, :], axis=0)
    rank = jnp.where(named > 0, rank, -1)
    ranks = jnp.arange(CAP, dtype=i32)
    placing = (rank.T[:, None, :] == ranks[None, :, None]).astype(bf16)
    placing = placing.reshape(DP_N * CAP, tokens)

    cut = 3 * wide_piece // 7
    early = normed[:, :cut]
    doubled = [normed[:, k * wide_piece + cut : (k + 1) * wide_piece] for k in range(RING)]
    rest = wide_piece - cut
    back = (RING - at_x) % RING
    late = lax.dynamic_slice_in_dim(
        jnp.concatenate(doubled + doubled, axis=1), back * rest, RING * rest, 1
    )

    def to_experts(block):
        block = jnp.dot(placing, block, preferred_element_type=f32).astype(bf16)
        block = lax.all_to_all(block.reshape(DP_N, CAP, -1), DP, 0, 0, tiled=True)
        return block.reshape(DP_N * CAP, -1)

    early = to_experts(early)
    early, late = lax.optimization_barrier((early, late))
    late = to_experts(late)
    early = [early] + [hop(early, "x", k) for k in (1, 2, 3)]
    early = lax.dynamic_slice_in_dim(
        jnp.concatenate(early + early, axis=1), back * cut, RING * cut, 1
    )

    def in_rows(core, low, high):
        blocks = []
        for weights in (w_gate, w_up):
            view = weights[0].reshape(RING, 2, wide_piece, -1)
            view = lax.dynamic_slice_in_dim(view, core, 1, 1)[:, 0, low:high]
            blocks.append(view.reshape(RING * (high - low), -1))
        return jnp.concatenate(blocks, axis=1)

    def out_columns(core, low, high):
        return jnp.concatenate(
            [
                lax.dynamic_slice_in_dim(
                    w_down[0], (2 * k + core) * wide_piece + low, high - low, 1
                )
                for k in range(RING)
            ],
            axis=1,
        )

    units = w_gate.shape[2]
    away = 1 - at_core
    sums = (
        jnp.dot(early, in_rows(at_core, 0, cut), preferred_element_type=f32)
        + jnp.dot(other_core(early), in_rows(away, 0, cut), preferred_element_type=f32)
        + jnp.dot(late, in_rows(at_core, cut, wide_piece), preferred_element_type=f32)
        + jnp.dot(other_core(late), in_rows(away, cut, wide_piece), preferred_element_type=f32)
    )
    hidden = (jax.nn.silu(sums[:, :units]) * sums[:, units:]).astype(bf16)
    hidden = lax.optimization_barrier(hidden)

    def output(low, high):
        give = jnp.dot(hidden, out_columns(away, low, high), preferred_element_type=f32)
        keep = jnp.dot(hidden, out_columns(at_core, low, high), preferred_element_type=f32)
        return keep + other_core(give.astype(bf16)).astype(f32)

    def to_home(block):
        block = lax.all_to_all(block.reshape(DP_N, CAP, -1), DP, 0, 0, tiled=True)
        return block.reshape(DP_N * CAP, -1)

    def ring_sum(block, size):
        block = jnp.concatenate([block, block], axis=1)
        block = lax.dynamic_slice_in_dim(block, at_x * size, RING * size, 1)
        total = block[:, :size].astype(f32)
        for k in (2, 1, 3):
            total = total + send(block[:, k * size : (k + 1) * size], "x", k).astype(f32)
        return total

    late = output(cut, wide_piece).astype(bf16)
    early, late = lax.optimization_barrier((output(0, cut).astype(bf16), late))
    late = to_home(late)
    early, late = lax.optimization_barrier((ring_sum(early, cut).astype(bf16), late))
    early = to_home(early)

    mix = jnp.where(rank[:, :, None] == ranks[None, None, :], weight[:, :, None], 0.0)
    mix = mix.reshape(tokens, DP_N * CAP)
    coarse = lax.reduce_precision(mix, 8, 7)
    both = jnp.concatenate([coarse.astype(bf16), (mix - coarse).astype(bf16)], axis=0)

    def mixed(block):
        block = jnp.dot(both, block, preferred_element_type=f32)
        return block[:tokens] + block[tokens:]

    late = ring_sum(mixed(late).astype(bf16), rest)
    routed = jnp.concatenate([mixed(early), late], axis=1).astype(bf16)
    return (attended, routed)


def solution(mesh):
    grid = Mesh(mesh.devices.reshape(RING, RING, RING, 2), ALL)
    return jax.shard_map(
        shards,
        mesh=grid,
        in_specs=(
            P(DP, HEAD, None),
            P(DP, None, None),
            P(DP, None),
            P(DP),
            P(DP),
            P(HEAD, None, None),
            P(HEAD, DP),
            P(DP, None),
            P(),
            P(DP, None),
            P(DP, None),
            P(DP, None, HEAD),
            P(DP, None, HEAD),
            P(DP, HEAD, None),
        ),
        out_specs=(P(DP, None), P(DP, HEAD)),
        check_vma=False,
    )
```

```python
import functools

import jax
import jax.numpy as jnp
from jax import lax
from jax.experimental import pallas as pl
from jax.experimental.pallas import tpu as pltpu
from jax.sharding import Mesh
from jax.sharding import PartitionSpec as P

LAT = 512
DP = ("y", "z")
HEAD = ("x", "core")
ALL = ("y", "z", "x", "core")
RING = 4
DP_N = 16
HEAD_N = 8
PAGES = 128
CAP = 32

softmax_scale = 192.0 ** (-0.5)
norm_eps = 1e-06
bf16 = jnp.bfloat16
f32 = jnp.float32
i32 = jnp.int32


def hop(array, axis, step):
    return lax.ppermute(array, axis, [((i + step) % RING, i) for i in range(RING)])


def send(array, axis, step):
    return lax.ppermute(array, axis, [(i, (i + step) % RING) for i in range(RING)])


def other_core(array):
    return lax.ppermute(array, "core", [(0, 1), (1, 0)])


def pack_kernel(me_ref, page_ref, held_ref, taken_ref, query_ref, out_ref, who_ref):
    me = me_ref[0]
    width = query_ref.shape[2]
    requests, per = page_ref.shape
    rows = out_ref.shape[1]
    lanes = out_ref.shape[2] - width

    row = lax.broadcasted_iota(i32, (rows, lanes), 0)
    lane = lax.broadcasted_iota(i32, (rows, lanes), 1)

    def clear(i, carry):
        who_ref[i] = -1
        return carry

    lax.fori_loop(0, DP_N, clear, 0)
    lane = jnp.where(row == 0, lane, -1)
    base = jnp.zeros((rows, lanes), f32)
    for r in range(requests):
        lender = page_ref[r, 0] // PAGES
        base = jnp.where(lane == 24 + r, lender.astype(f32), base)

        @pl.when(lender != me)
        def _():
            who_ref[lender] = r

    def one(i, carry):
        found = who_ref[i]
        r = jnp.maximum(found, 0)
        seen = held_ref[r] + taken_ref[r]
        told = [page_ref[r, k] - page_ref[r, 0] // PAGES * PAGES for k in range(per)]
        told += [seen // 2, seen % 2, jnp.where(found >= 0, 1, 0)]
        line = base
        for k, value in enumerate(told):
            line = jnp.where(lane == 8 + k, value.astype(f32), line)
        out_ref[i, :, :width] = query_ref[r]
        out_ref[i, :, width:] = line.astype(bf16)
        return carry

    lax.fori_loop(0, DP_N, one, 0)


def pack(me, page_table, cache_len, accepted, query_rows):
    count, rows, width = query_rows.shape
    scalar, vector = (pl.BlockSpec(memory_space=m) for m in (pltpu.SMEM, pltpu.VMEM))
    return pl.pallas_call(
        pack_kernel,
        out_shape=jax.ShapeDtypeStruct((DP_N, rows, width + 64), bf16),
        in_specs=[scalar] * 4 + [vector],
        out_specs=vector,
        scratch_shapes=[pltpu.SMEM((DP_N,), i32)],
        compiler_params=pltpu.CompilerParams(vmem_limit_bytes=32 * 2**20),
        name="pack",
    )(me, page_table, cache_len, accepted, query_rows)


def attend_kernel(
    me_ref, page_ref, held_ref, taken_ref, told_ref, query_ref, pool_ref, out_ref,
    which_ref, list_ref, seen_ref, keys_ref, held_pool_ref, sems, own,
):
    me = me_ref[0]
    count, rows, _ = query_ref.shape
    page_rows, width, pages = pool_ref.shape
    chunks = sems.shape[0]
    size = page_rows // chunks
    copies = [
        pltpu.make_async_copy(
            pool_ref.at[pl.ds(n * size, size)], held_pool_ref.at[pl.ds(n * size, size)], sems.at[n]
        )
        for n in range(chunks)
    ]
    for copy in copies:
        copy.start()
    per = page_ref.shape[1]
    slots = count // 2

    def plan(r, at):
        found = page_ref[r, 0] // PAGES == me if own else told_ref[r, 10] > 0
        spot = jnp.minimum(at, slots - 1)

        @pl.when(found)
        def _():
            which_ref[spot] = r
            if own:
                seen_ref[spot] = held_ref[r] + taken_ref[r]
            else:
                seen_ref[spot] = told_ref[r, 8] * 2 + told_ref[r, 9]
            for k in range(per):
                list_ref[spot * per + k] = page_ref[r, k] - me * PAGES if own else told_ref[r, k]

        return at + found.astype(i32)

    lax.fori_loop(0, count, plan, jnp.int32(0))
    row = lax.broadcasted_iota(i32, (slots * per, pages), 0)
    lane = lax.broadcasted_iota(i32, (slots * per, pages), 1)
    wanted = jnp.zeros((slots * per, pages), i32)
    for n in range(slots * per):
        wanted = jnp.where(row == n, list_ref[n], wanted)
    order = jnp.where(wanted == lane, 1.0, 0.0).astype(bf16)

    def sort(i, carry):
        sorted_rows = lax.dot_general(
            order, held_pool_ref[i], (((1,), (1,)), ((), ())), preferred_element_type=f32
        ).astype(bf16)
        for pair in range(slots // 2):
            keys_ref[pair, pl.ds(pl.multiple_of(i * 16, 16), 16), :] = sorted_rows[
                pair * 16 : (pair + 1) * 16
            ]
        return carry

    for n in range(chunks):
        copies[n].wait()
        lax.fori_loop(n * size, (n + 1) * size, sort, 0, unroll=True)
    keys_at = lax.broadcasted_iota(i32, (2 * rows, page_rows * 16), 1)
    query_at = lax.broadcasted_iota(i32, (2 * rows, page_rows * 16), 0)
    position = keys_at % 8 * page_rows + keys_at // 16
    second = query_at >= rows
    same = (keys_at // 8 % 2 == 1) == second
    draft = jnp.where(second, query_at - rows, query_at) // (rows // 3)
    offset = jnp.where(same, position - draft, 1 << 20)
    for pair in range(slots // 2):
        queries = jnp.concatenate(
            [query_ref[which_ref[2 * pair + n], :, :width] for n in range(2)], axis=0
        )
        keys = keys_ref[pair]
        scores = (
            lax.dot_general(queries, keys, (((1,), (1,)), ((), ())), preferred_element_type=f32)
            * softmax_scale
        )
        allowed = offset <= jnp.where(second, seen_ref[2 * pair + 1], seen_ref[2 * pair])
        highest = jnp.max(jnp.where(allowed, scores, -1e30), axis=-1, keepdims=True)
        weights = jnp.where(allowed, jnp.exp(jnp.where(allowed, scores - highest, 0.0)), 0.0)
        probs = (weights / jnp.sum(weights, axis=-1, keepdims=True)).astype(bf16)
        latent = lax.dot_general(
            probs, keys[:, :LAT], (((1,), (0,)), ((), ())), preferred_element_type=f32
        ).astype(bf16)
        out_ref[2 * pair] = latent[:rows]
        out_ref[2 * pair + 1] = latent[rows:]


def attend(own, me, page_table, cache_len, accepted, told, queries, pool):
    count, rows, _ = queries.shape
    page_rows, width, pages = pool.shape
    per, slots = page_table.shape[1], count // 2
    scalar, vector = (pl.BlockSpec(memory_space=m) for m in (pltpu.SMEM, pltpu.VMEM))
    return pl.pallas_call(
        functools.partial(attend_kernel, own=own),
        out_shape=jax.ShapeDtypeStruct((slots, rows, LAT), bf16),
        in_specs=[scalar] * 5 + [vector, pl.BlockSpec(memory_space=pl.ANY)],
        out_specs=vector,
        scratch_shapes=[
            pltpu.SMEM((slots,), i32),
            pltpu.SMEM((slots * per,), i32),
            pltpu.SMEM((slots,), i32),
            pltpu.VMEM((slots // 2, page_rows * 16, width), bf16),
            pltpu.VMEM((page_rows, width, pages), bf16),
            pltpu.SemaphoreType.DMA((4,)),
        ],
        compiler_params=pltpu.CompilerParams(vmem_limit_bytes=56 * 2**20),
        cost_estimate=pl.CostEstimate(
            flops=4_000_000_000, bytes_accessed=12_000_000, transcendentals=0
        ),
        name="attend_own" if own else "attend_far",
    )(me, page_table, cache_len, accepted, told, queries, pool)


def home_kernel(
    spot_ref, here_ref, there_ref, gain_ref, placing_ref, attended_ref, early_ref, late_ref
):
    wide = here_ref.shape[1] // RING
    cut, rest = early_ref.shape[1], late_ref.shape[1] // RING
    here, there = here_ref[...], there_ref[...]
    for k in range(RING):
        for side, block in enumerate((here, there)):
            start = pl.multiple_of(spot_ref[side * RING + k] * wide, 128)
            attended_ref[:, pl.ds(start, wide)] = block[:, k * wide : (k + 1) * wide]
    rows, rows_there = here.astype(f32), there.astype(f32)
    squares = jnp.sum(rows * rows, axis=1, keepdims=True) + jnp.sum(
        rows_there * rows_there, axis=1, keepdims=True
    )
    root = lax.rsqrt(squares / attended_ref.shape[1] + norm_eps)
    normed = (rows * root * gain_ref[...]).astype(bf16)
    placing = placing_ref[...]
    early_ref[...] = jnp.dot(placing, normed[:, :cut], preferred_element_type=f32).astype(bf16)
    for k in range(RING):
        late_ref[:, k * rest : (k + 1) * rest] = jnp.dot(
            placing, normed[:, k * wide + cut : (k + 1) * wide], preferred_element_type=f32
        ).astype(bf16)


def home_rows(spots, here, there, gains, placing, cut):
    tokens, half = here.shape
    slots = placing.shape[0]
    vector = pl.BlockSpec(memory_space=pltpu.VMEM)
    return pl.pallas_call(
        home_kernel,
        out_shape=[
            jax.ShapeDtypeStruct((tokens, 2 * half), bf16),
            jax.ShapeDtypeStruct((slots, cut), bf16),
            jax.ShapeDtypeStruct((slots, half - RING * cut), bf16),
        ],
        in_specs=[pl.BlockSpec(memory_space=pltpu.SMEM)] + [vector] * 4,
        out_specs=[vector] * 3,
        compiler_params=pltpu.CompilerParams(vmem_limit_bytes=32 * 2**20),
        name="home_rows",
    )(spots, here, there, gains, placing)


def enter_kernel(spot_ref, early_ref, late_ref, gate_ref, up_ref, *refs):
    out_ref, sum_ref = refs[-2:]
    units = gate_ref.shape[2]
    cut = early_ref.shape[1]

    @pl.when(pl.program_id(0) == 0)
    def _():
        sum_ref[...] = refs[0][...] if len(refs) == 3 else jnp.zeros_like(sum_ref)

    for n, weights in enumerate((gate_ref, up_ref)):
        sum_ref[:, n * units : (n + 1) * units] += jnp.dot(
            early_ref[...], weights[0, :cut], preferred_element_type=f32
        ) + jnp.dot(late_ref[...], weights[0, cut:], preferred_element_type=f32)

    @pl.when(pl.program_id(0) == RING - 1)
    def _():
        if len(refs) == 3:
            gate = sum_ref[:, :units]
            out_ref[...] = (gate / (1.0 + jnp.exp(-gate)) * sum_ref[:, units:]).astype(bf16)
        else:
            out_ref[...] = sum_ref[...]


def enter(spots, early, late, w_gate, w_up, so_far=None):
    slots = early.shape[0]
    cut, rest = early.shape[1] // RING, late.shape[1] // RING
    units = w_gate.shape[2]
    weights = pl.BlockSpec((1, cut + rest, units), lambda i, spot: (0, spot[i], 0))
    more = [] if so_far is None else [so_far]
    whole = pl.BlockSpec((slots, 2 * units), lambda i, spot: (0, 0))
    spec = pltpu.PrefetchScalarGridSpec(
        num_scalar_prefetch=1,
        grid=(RING,),
        in_specs=[
            pl.BlockSpec((slots, cut), lambda i, spot: (0, i)),
            pl.BlockSpec((slots, rest), lambda i, spot: (0, i)),
            weights,
            weights,
        ]
        + [whole] * len(more),
        out_specs=pl.BlockSpec((slots, units if more else 2 * units), lambda i, spot: (0, 0)),
        scratch_shapes=[pltpu.VMEM((slots, 2 * units), f32)],
    )
    return pl.pallas_call(
        enter_kernel,
        out_shape=jax.ShapeDtypeStruct(
            (slots, units if more else 2 * units), bf16 if more else f32
        ),
        grid_spec=spec,
        compiler_params=pltpu.CompilerParams(vmem_limit_bytes=56 * 2**20),
        cost_estimate=pl.CostEstimate(
            flops=4 * slots * units * RING * (cut + rest), bytes_accessed=8_000_000, transcendentals=0
        ),
        name="enter_last" if more else "enter_first",
    )(spots, early, late, w_gate, w_up, *more)


def leave_kernel(spot_ref, hidden_ref, down_ref, *refs):
    early_ref, late_ref = refs[-2:]
    cut = early_ref.shape[1]
    rows = jnp.dot(hidden_ref[...], down_ref[0], preferred_element_type=f32)
    early, late = rows[:, :cut], rows[:, cut:]
    if len(refs) == 4:
        early, late = early + refs[0][...].astype(f32), late + refs[1][...].astype(f32)
    early_ref[...] = early.astype(bf16)
    late_ref[...] = late.astype(bf16)


def leave(spots, hidden, w_down, cut, *more):
    slots, units = hidden.shape
    rest = w_down.shape[2] // HEAD_N - cut
    sides = [
        pl.BlockSpec((slots, cut), lambda i, spot: (0, i)),
        pl.BlockSpec((slots, rest), lambda i, spot: (0, i)),
    ]
    spec = pltpu.PrefetchScalarGridSpec(
        num_scalar_prefetch=1,
        grid=(RING,),
        in_specs=[
            pl.BlockSpec((slots, units), lambda i, spot: (0, 0)),
            pl.BlockSpec((1, units, cut + rest), lambda i, spot: (0, 0, spot[i])),
        ]
        + sides[: len(more)],
        out_specs=sides,
    )
    return pl.pallas_call(
        leave_kernel,
        out_shape=[
            jax.ShapeDtypeStruct((slots, RING * cut), bf16),
            jax.ShapeDtypeStruct((slots, RING * rest), bf16),
        ],
        grid_spec=spec,
        compiler_params=pltpu.CompilerParams(vmem_limit_bytes=56 * 2**20),
        cost_estimate=pl.CostEstimate(
            flops=2 * slots * units * RING * (cut + rest), bytes_accessed=8_000_000, transcendentals=0
        ),
        name="leave_last" if more else "leave_first",
    )(spots, hidden, w_down, *more)


def before(count):
    at = jnp.arange(count, dtype=i32)
    return at[:, None] < at[None, :]


def shards(
    queries,
    kv_pool,
    page_table,
    cache_len,
    accepted,
    w_uv,
    w_o,
    residual,
    norm_gain,
    expert_ids,
    gate_weights,
    w_gate,
    w_up,
    w_down,
):
    at_x, at_y, at_z = lax.axis_index("x"), lax.axis_index("y"), lax.axis_index("z")
    at_core = lax.axis_index("core")
    dp_index = at_y * RING + at_z
    requests = page_table.shape[0]
    tokens, head_group, width = queries.shape
    query_rows = queries.reshape(requests, 3 * head_group, width)
    dps = jnp.arange(DP_N, dtype=i32)
    me = dp_index.astype(i32)[None]

    packed = pack(me, page_table, cache_len, accepted, query_rows)
    arrived = lax.all_to_all(packed, DP, 0, 0, tiled=True)
    told = arrived[:, 0, width:]
    lenders = told[:, 24:40].astype(i32)
    line = told[:, 8:24].astype(i32)
    pool = kv_pool.transpose(1, 2, 0)
    tables = (me, page_table, cache_len, accepted)
    latent = jnp.concatenate(
        [
            attend(True, *tables, jnp.zeros((DP_N, 16), i32), query_rows, pool),
            attend(False, *tables, line, arrived, pool),
        ]
    )
    values = jnp.einsum(
        "thc,hcv->thv",
        latent.reshape(tokens, head_group, LAT),
        w_uv,
        preferred_element_type=f32,
    ).astype(bf16)
    values = values.reshape(tokens, head_group * w_uv.shape[2])

    half = values.shape[1] // 2

    def spread(block, first, second):
        line = jnp.concatenate([block] + [hop(block, first, k) for k in (1, 2, 3)], axis=0)
        return [line] + [hop(line, second, k) for k in (1, 2, 3)]

    zy = spread(values[:, :half], "z", "y")
    yz = spread(values[:, half:], "y", "z")
    part_zy = jnp.concatenate(
        [jnp.dot(a, w_o[:half], preferred_element_type=f32) for a in zy], axis=0
    )
    part_yz = jnp.concatenate(
        [jnp.dot(a, w_o[half:], preferred_element_type=f32) for a in yz], axis=0
    )
    columns = w_o.shape[1]
    part_yz = part_yz.reshape(RING, RING, tokens, columns).transpose(1, 0, 2, 3)
    projected = (part_zy + part_yz.reshape(-1, columns)).astype(bf16)

    is_own = (lenders == dps[:, None]).astype(i32)
    own_slot = jnp.sum(is_own[:, :, None] * before(requests)[None], axis=1)
    at_lender = (lenders[:, :, None] == dps[None, None, :]).astype(i32)
    away = at_lender * (dps[:, None, None] != dps[None, None, :])
    lends = jnp.sum(away, axis=1)
    lend_rank = jnp.sum(before(DP_N)[:, :, None] * lends[:, None, :], axis=0)
    far_slot = 8 + jnp.sum(at_lender * lend_rank[:, None, :], axis=2)
    slot = jnp.where(is_own > 0, own_slot, far_slot)
    turned = ((lenders // RING - at_y) % RING) * RING + (lenders % RING - at_z) % RING
    first_row = (turned * requests + slot) * 3
    source = (first_row[:, :, None] + jnp.arange(3, dtype=i32)).reshape(-1)
    rows_all = projected.shape[0]
    moves = (source[:, None] == jnp.arange(rows_all, dtype=i32)[None, :]).astype(bf16)
    homed = jnp.dot(moves, projected, preferred_element_type=f32).astype(bf16)
    homed = lax.all_to_all(homed.reshape(DP_N, tokens, columns), DP, 0, 0, tiled=True)

    wide_piece = DP_N * columns // HEAD_N
    homed = homed.reshape(RING, 2, 2, tokens, columns)
    homed = lax.dynamic_slice_in_dim(jnp.concatenate([homed, homed], 0), at_x, RING, 0)
    keep = lax.dynamic_slice_in_dim(homed, at_core, 1, 1)[:, 0]
    give = lax.dynamic_slice_in_dim(homed, 1 - at_core, 1, 1)[:, 0]
    kept = keep.astype(f32) + other_core(give).astype(f32)
    attention = kept[0]
    for k in (2, 1, 3):
        attention = attention + send(kept[k].astype(bf16), "x", k).astype(f32)
    attention = jnp.concatenate([attention[0], attention[1]], axis=1)
    head_index = at_x * 2 + at_core
    near = lax.dynamic_slice_in_dim(residual, head_index * wide_piece, wide_piece, 1)
    piece = (near.astype(f32) + attention).astype(bf16)

    here = jnp.concatenate([piece] + [hop(piece, "x", k) for k in (1, 2, 3)], axis=1)
    there = other_core(here)
    ring_at = (at_x + jnp.arange(RING, dtype=i32)) % RING * 2
    spots_here, spots_there = ring_at + at_core, ring_at + 1 - at_core
    gains = jnp.concatenate([norm_gain, norm_gain]).reshape(2 * RING, 2, wide_piece)
    gains = lax.dynamic_slice(gains, (at_x, at_core, 0), (RING, 1, wide_piece)).reshape(1, -1)

    chosen = (expert_ids[:, :, None] == dps[None, None, :]).astype(i32)
    named = jnp.sum(chosen, axis=1)
    weight = jnp.sum(chosen.astype(f32) * gate_weights[:, :, None], axis=1)
    rank = jnp.sum(before(tokens)[:, :, None] * named[:, None, :], axis=0)
    rank = jnp.where(named > 0, rank, -1)
    ranks = jnp.arange(CAP, dtype=i32)
    placing = (rank.T[:, None, :] == ranks[None, :, None]).astype(bf16)
    placing = placing.reshape(DP_N * CAP, tokens)

    cut = 3 * wide_piece // 7
    rest = wide_piece - cut
    attended, early, late = home_rows(
        jnp.concatenate([spots_here, spots_there]), here, there, gains, placing, cut
    )

    def exchange(block):
        block = lax.all_to_all(block.reshape(DP_N, CAP, -1), DP, 0, 0, tiled=True)
        return block.reshape(DP_N * CAP, -1)

    early = exchange(early)
    early, late = lax.optimization_barrier((early, late))
    late = exchange(late)
    early = jnp.concatenate([early] + [hop(early, "x", k) for k in (1, 2, 3)], axis=1)

    sums = enter(spots_here, early, late, w_gate, w_up)
    hidden = enter(spots_there, other_core(early), other_core(late), w_gate, w_up, sums)
    give = leave(spots_there, hidden, w_down, cut)
    early, late = leave(spots_here, hidden, w_down, cut, *[other_core(a) for a in give])

    def ring_sum(block, size):
        total = block[:, :size].astype(f32)
        for k in (2, 1, 3):
            total = total + send(block[:, k * size : (k + 1) * size], "x", k).astype(f32)
        return total

    late = exchange(late)
    early, late = lax.optimization_barrier((ring_sum(early, cut).astype(bf16), late))
    early = exchange(early)

    mix = jnp.where(rank[:, :, None] == ranks[None, None, :], weight[:, :, None], 0.0)
    mix = mix.reshape(tokens, DP_N * CAP)
    coarse = lax.reduce_precision(mix, 8, 7)
    both = jnp.concatenate([coarse.astype(bf16), (mix - coarse).astype(bf16)], axis=0)

    def mixed(block):
        block = jnp.dot(both, block, preferred_element_type=f32)
        return block[:tokens] + block[tokens:]

    late = ring_sum(mixed(late).astype(bf16), rest)
    routed = jnp.concatenate([mixed(early), late], axis=1).astype(bf16)
    return (attended, routed)


def solution(mesh):
    grid = Mesh(mesh.devices.reshape(RING, RING, RING, 2), ALL)
    return jax.shard_map(
        shards,
        mesh=grid,
        in_specs=(
            P(DP, HEAD, None),
            P(DP, None, None),
            P(DP, None),
            P(DP),
            P(DP),
            P(HEAD, None, None),
            P(HEAD, DP),
            P(DP, None),
            P(),
            P(DP, None),
            P(DP, None),
            P(DP, None, HEAD),
            P(DP, None, HEAD),
            P(DP, HEAD, None),
        ),
        out_specs=(P(DP, None), P(DP, HEAD)),
        check_vma=False,
    )
```

```python
import functools

import jax
import jax.numpy as jnp
from jax import lax
from jax.experimental import pallas as pl
from jax.experimental.pallas import tpu as pltpu
from jax.sharding import Mesh
from jax.sharding import PartitionSpec as P

LAT = 512
DP = ("y", "z")
HEAD = ("x", "core")
ALL = ("y", "z", "x", "core")
RING = 4
DP_N = 16
HEAD_N = 8
PAGES = 128
CAP = 32

softmax_scale = 192.0 ** (-0.5)
norm_eps = 1e-06
bf16 = jnp.bfloat16
f32 = jnp.float32
i32 = jnp.int32


def hop(array, axis, step):
    return lax.ppermute(array, axis, [((i + step) % RING, i) for i in range(RING)])


def send(array, axis, step):
    return lax.ppermute(array, axis, [(i, (i + step) % RING) for i in range(RING)])


def other_core(array):
    return lax.ppermute(array, "core", [(0, 1), (1, 0)])


def pack_kernel(me_ref, page_ref, held_ref, taken_ref, query_ref, out_ref, who_ref):
    me = me_ref[0]
    width = query_ref.shape[2]
    requests, per = page_ref.shape
    rows = out_ref.shape[1]
    lanes = out_ref.shape[2] - width

    row = lax.broadcasted_iota(i32, (rows, lanes), 0)
    lane = lax.broadcasted_iota(i32, (rows, lanes), 1)

    def clear(i, carry):
        who_ref[i] = -1
        return carry

    lax.fori_loop(0, DP_N, clear, 0)
    lane = jnp.where(row == 0, lane, -1)
    base = jnp.zeros((rows, lanes), f32)
    for r in range(requests):
        lender = page_ref[r, 0] // PAGES
        base = jnp.where(lane == 24 + r, lender.astype(f32), base)

        @pl.when(lender != me)
        def _():
            who_ref[lender] = r

    def one(i, carry):
        found = who_ref[i]
        r = jnp.maximum(found, 0)
        seen = held_ref[r] + taken_ref[r]
        told = [page_ref[r, k] - page_ref[r, 0] // PAGES * PAGES for k in range(per)]
        told += [seen // 2, seen % 2, jnp.where(found >= 0, 1, 0)]
        line = base
        for k, value in enumerate(told):
            line = jnp.where(lane == 8 + k, value.astype(f32), line)
        out_ref[i, :, :width] = query_ref[r]
        out_ref[i, :, width:] = line.astype(bf16)
        return carry

    lax.fori_loop(0, DP_N, one, 0)


def pack(me, page_table, cache_len, accepted, query_rows):
    count, rows, width = query_rows.shape
    scalar, vector = (pl.BlockSpec(memory_space=m) for m in (pltpu.SMEM, pltpu.VMEM))
    return pl.pallas_call(
        pack_kernel,
        out_shape=jax.ShapeDtypeStruct((DP_N, rows, width + 64), bf16),
        in_specs=[scalar] * 4 + [vector],
        out_specs=vector,
        scratch_shapes=[pltpu.SMEM((DP_N,), i32)],
        compiler_params=pltpu.CompilerParams(vmem_limit_bytes=32 * 2**20),
        name="pack",
    )(me, page_table, cache_len, accepted, query_rows)


def attend_kernel(
    me_ref, page_ref, held_ref, taken_ref, told_ref, query_ref, pool_ref, out_ref,
    which_ref, list_ref, seen_ref, keys_ref, held_pool_ref, sems, own,
):
    me = me_ref[0]
    count, rows, _ = query_ref.shape
    page_rows, width, pages = pool_ref.shape
    chunks = sems.shape[0]
    size = page_rows // chunks
    copies = [
        pltpu.make_async_copy(
            pool_ref.at[pl.ds(n * size, size)], held_pool_ref.at[pl.ds(n * size, size)], sems.at[n]
        )
        for n in range(chunks)
    ]
    for copy in copies:
        copy.start()
    per = page_ref.shape[1]
    slots = count // 2

    def plan(r, at):
        found = page_ref[r, 0] // PAGES == me if own else told_ref[r, 10] > 0
        spot = jnp.minimum(at, slots - 1)

        @pl.when(found)
        def _():
            which_ref[spot] = r
            if own:
                seen_ref[spot] = held_ref[r] + taken_ref[r]
            else:
                seen_ref[spot] = told_ref[r, 8] * 2 + told_ref[r, 9]
            for k in range(per):
                list_ref[spot * per + k] = page_ref[r, k] - me * PAGES if own else told_ref[r, k]

        return at + found.astype(i32)

    lax.fori_loop(0, count, plan, jnp.int32(0))
    row = lax.broadcasted_iota(i32, (slots * per, pages), 0)
    lane = lax.broadcasted_iota(i32, (slots * per, pages), 1)
    wanted = jnp.zeros((slots * per, pages), i32)
    for n in range(slots * per):
        wanted = jnp.where(row == n, list_ref[n], wanted)
    order = jnp.where(wanted == lane, 1.0, 0.0).astype(bf16)

    def sort(i, carry):
        sorted_rows = lax.dot_general(
            order, held_pool_ref[i], (((1,), (1,)), ((), ())), preferred_element_type=f32
        ).astype(bf16)
        for pair in range(slots // 2):
            keys_ref[pair, pl.ds(pl.multiple_of(i * 16, 16), 16), :] = sorted_rows[
                pair * 16 : (pair + 1) * 16
            ]
        return carry

    for n in range(chunks):
        copies[n].wait()
        lax.fori_loop(n * size, (n + 1) * size, sort, 0, unroll=True)
    keys_at = lax.broadcasted_iota(i32, (2 * rows, page_rows * 16), 1)
    query_at = lax.broadcasted_iota(i32, (2 * rows, page_rows * 16), 0)
    position = keys_at % 8 * page_rows + keys_at // 16
    second = query_at >= rows
    same = (keys_at // 8 % 2 == 1) == second
    draft = jnp.where(second, query_at - rows, query_at) // (rows // 3)
    offset = jnp.where(same, position - draft, 1 << 20)
    for pair in range(slots // 2):
        queries = jnp.concatenate(
            [query_ref[which_ref[2 * pair + n], :, :width] for n in range(2)], axis=0
        )
        keys = keys_ref[pair]
        scores = (
            lax.dot_general(queries, keys, (((1,), (1,)), ((), ())), preferred_element_type=f32)
            * softmax_scale
        )
        allowed = offset <= jnp.where(second, seen_ref[2 * pair + 1], seen_ref[2 * pair])
        highest = jnp.max(jnp.where(allowed, scores, -1e30), axis=-1, keepdims=True)
        weights = jnp.where(allowed, jnp.exp(jnp.where(allowed, scores - highest, 0.0)), 0.0)
        probs = (weights / jnp.sum(weights, axis=-1, keepdims=True)).astype(bf16)
        latent = lax.dot_general(
            probs, keys[:, :LAT], (((1,), (0,)), ((), ())), preferred_element_type=f32
        ).astype(bf16)
        out_ref[2 * pair] = latent[:rows]
        out_ref[2 * pair + 1] = latent[rows:]


def attend(own, me, page_table, cache_len, accepted, told, queries, pool):
    count, rows, _ = queries.shape
    page_rows, width, pages = pool.shape
    per, slots = page_table.shape[1], count // 2
    scalar, vector = (pl.BlockSpec(memory_space=m) for m in (pltpu.SMEM, pltpu.VMEM))
    return pl.pallas_call(
        functools.partial(attend_kernel, own=own),
        out_shape=jax.ShapeDtypeStruct((slots, rows, LAT), bf16),
        in_specs=[scalar] * 5 + [vector, pl.BlockSpec(memory_space=pl.ANY)],
        out_specs=vector,
        scratch_shapes=[
            pltpu.SMEM((slots,), i32),
            pltpu.SMEM((slots * per,), i32),
            pltpu.SMEM((slots,), i32),
            pltpu.VMEM((slots // 2, page_rows * 16, width), bf16),
            pltpu.VMEM((page_rows, width, pages), bf16),
            pltpu.SemaphoreType.DMA((4,)),
        ],
        compiler_params=pltpu.CompilerParams(vmem_limit_bytes=56 * 2**20),
        cost_estimate=pl.CostEstimate(
            flops=4_000_000_000, bytes_accessed=12_000_000, transcendentals=0
        ),
        name="attend_own" if own else "attend_far",
    )(me, page_table, cache_len, accepted, told, queries, pool)


def home_kernel(
    spot_ref, here_ref, there_ref, gain_ref, placing_ref, attended_ref, early_ref, late_ref
):
    wide = here_ref.shape[1] // RING
    cut, rest = early_ref.shape[1], late_ref.shape[1] // RING
    here, there = here_ref[...], there_ref[...]
    for k in range(RING):
        for side, block in enumerate((here, there)):
            start = pl.multiple_of(spot_ref[side * RING + k] * wide, 128)
            attended_ref[:, pl.ds(start, wide)] = block[:, k * wide : (k + 1) * wide]
    rows, rows_there = here.astype(f32), there.astype(f32)
    squares = jnp.sum(rows * rows, axis=1, keepdims=True) + jnp.sum(
        rows_there * rows_there, axis=1, keepdims=True
    )
    root = lax.rsqrt(squares / attended_ref.shape[1] + norm_eps)
    normed = (rows * root * gain_ref[...]).astype(bf16)
    placing = placing_ref[...]
    early_ref[...] = jnp.dot(placing, normed[:, :cut], preferred_element_type=f32).astype(bf16)
    for k in range(RING):
        start = pl.multiple_of(spot_ref[k] // 2 * rest, 128)
        late_ref[:, pl.ds(start, rest)] = jnp.dot(
            placing, normed[:, k * wide + cut : (k + 1) * wide], preferred_element_type=f32
        ).astype(bf16)


def home_rows(spots, here, there, gains, placing, cut):
    tokens, half = here.shape
    slots = placing.shape[0]
    vector = pl.BlockSpec(memory_space=pltpu.VMEM)
    return pl.pallas_call(
        home_kernel,
        out_shape=[
            jax.ShapeDtypeStruct((tokens, 2 * half), bf16),
            jax.ShapeDtypeStruct((slots, cut), bf16),
            jax.ShapeDtypeStruct((slots, half - RING * cut), bf16),
        ],
        in_specs=[pl.BlockSpec(memory_space=pltpu.SMEM)] + [vector] * 4,
        out_specs=[vector] * 3,
        compiler_params=pltpu.CompilerParams(vmem_limit_bytes=32 * 2**20),
        name="home_rows",
    )(spots, here, there, gains, placing)


def before(count):
    at = jnp.arange(count, dtype=i32)
    return at[:, None] < at[None, :]


def shards(
    queries,
    kv_pool,
    page_table,
    cache_len,
    accepted,
    w_uv,
    w_o,
    residual,
    norm_gain,
    expert_ids,
    gate_weights,
    w_gate,
    w_up,
    w_down,
):
    at_x, at_y, at_z = lax.axis_index("x"), lax.axis_index("y"), lax.axis_index("z")
    at_core = lax.axis_index("core")
    dp_index = at_y * RING + at_z
    requests = page_table.shape[0]
    tokens, head_group, width = queries.shape
    query_rows = queries.reshape(requests, 3 * head_group, width)
    dps = jnp.arange(DP_N, dtype=i32)
    me = dp_index.astype(i32)[None]

    packed = pack(me, page_table, cache_len, accepted, query_rows)
    arrived = lax.all_to_all(packed, DP, 0, 0, tiled=True)
    told = arrived[:, 0, width:]
    lenders = told[:, 24:40].astype(i32)
    line = told[:, 8:24].astype(i32)
    pool = kv_pool.transpose(1, 2, 0)
    tables = (me, page_table, cache_len, accepted)
    latent = jnp.concatenate(
        [
            attend(True, *tables, jnp.zeros((DP_N, 16), i32), query_rows, pool),
            attend(False, *tables, line, arrived, pool),
        ]
    )
    values = jnp.einsum(
        "thc,hcv->thv",
        latent.reshape(tokens, head_group, LAT),
        w_uv,
        preferred_element_type=f32,
    ).astype(bf16)
    values = values.reshape(tokens, head_group * w_uv.shape[2])

    half = values.shape[1] // 2

    def spread(block, first, second):
        line = jnp.concatenate([block] + [hop(block, first, k) for k in (1, 2, 3)], axis=0)
        return [line] + [hop(line, second, k) for k in (1, 2, 3)]

    zy = spread(values[:, :half], "z", "y")
    yz = spread(values[:, half:], "y", "z")
    part_zy = jnp.concatenate(
        [jnp.dot(a, w_o[:half], preferred_element_type=f32) for a in zy], axis=0
    )
    part_yz = jnp.concatenate(
        [jnp.dot(a, w_o[half:], preferred_element_type=f32) for a in yz], axis=0
    )
    columns = w_o.shape[1]
    part_yz = part_yz.reshape(RING, RING, tokens, columns).transpose(1, 0, 2, 3)
    projected = (part_zy + part_yz.reshape(-1, columns)).astype(bf16)

    is_own = (lenders == dps[:, None]).astype(i32)
    own_slot = jnp.sum(is_own[:, :, None] * before(requests)[None], axis=1)
    at_lender = (lenders[:, :, None] == dps[None, None, :]).astype(i32)
    away = at_lender * (dps[:, None, None] != dps[None, None, :])
    lends = jnp.sum(away, axis=1)
    lend_rank = jnp.sum(before(DP_N)[:, :, None] * lends[:, None, :], axis=0)
    far_slot = 8 + jnp.sum(at_lender * lend_rank[:, None, :], axis=2)
    slot = jnp.where(is_own > 0, own_slot, far_slot)
    turned = ((lenders // RING - at_y) % RING) * RING + (lenders % RING - at_z) % RING
    first_row = (turned * requests + slot) * 3
    source = (first_row[:, :, None] + jnp.arange(3, dtype=i32)).reshape(-1)
    rows_all = projected.shape[0]
    moves = (source[:, None] == jnp.arange(rows_all, dtype=i32)[None, :]).astype(bf16)
    homed = jnp.dot(moves, projected, preferred_element_type=f32).astype(bf16)
    wide_piece = w_down.shape[2] // HEAD_N
    cut = 3 * wide_piece // 7
    rest = wide_piece - cut
    away = 1 - at_core
    homed, w_gate, w_up, w_down = lax.optimization_barrier((homed, w_gate, w_up, w_down))

    def spot(k, core):
        return ((at_x + k) % RING * 2 + core) * wide_piece

    def in_first(core):
        return [
            jnp.concatenate(
                [lax.dynamic_slice_in_dim(w[0], spot(k, core), cut, 0) for k in range(RING)], axis=0
            )
            for w in (w_gate, w_up)
        ]

    def in_last(core):
        views = [w[0].reshape(RING, 2, wide_piece, -1) for w in (w_gate, w_up)]
        return [
            lax.dynamic_slice_in_dim(v, core, 1, 1)[:, 0, cut:].reshape(RING * rest, -1)
            for v in views
        ]

    def out_first(core):
        cuts = [lax.dynamic_slice_in_dim(w_down[0], spot(k, core), cut, 1) for k in range(RING)]
        return jnp.concatenate(cuts, axis=1)

    def out_last(core):
        starts = [(2 * k + core) * wide_piece + cut for k in range(RING)]
        cuts = [lax.dynamic_slice_in_dim(w_down[0], start, rest, 1) for start in starts]
        return jnp.concatenate(cuts, axis=1)

    weights = [
        in_first(at_core), in_first(away), in_last(at_core), in_last(away),
        out_first(at_core), out_first(away), out_last(at_core), out_last(away),
    ]
    homed = lax.all_to_all(homed.reshape(DP_N, tokens, columns), DP, 0, 0, tiled=True)
    homed, weights = lax.optimization_barrier((homed, weights))

    homed = homed.reshape(RING, 2, 2, tokens, columns)
    homed = lax.dynamic_slice_in_dim(jnp.concatenate([homed, homed], 0), at_x, RING, 0)
    keep = lax.dynamic_slice_in_dim(homed, at_core, 1, 1)[:, 0]
    give = lax.dynamic_slice_in_dim(homed, 1 - at_core, 1, 1)[:, 0]
    kept = keep.astype(f32) + other_core(give).astype(f32)
    attention = kept[0]
    for k in (2, 1, 3):
        attention = attention + send(kept[k].astype(bf16), "x", k).astype(f32)
    attention = jnp.concatenate([attention[0], attention[1]], axis=1)
    head_index = at_x * 2 + at_core
    near = lax.dynamic_slice_in_dim(residual, head_index * wide_piece, wide_piece, 1)
    piece = (near.astype(f32) + attention).astype(bf16)

    here = jnp.concatenate([piece] + [hop(piece, "x", k) for k in (1, 2, 3)], axis=1)
    there = other_core(here)
    ring_at = (at_x + jnp.arange(RING, dtype=i32)) % RING * 2
    spots_here, spots_there = ring_at + at_core, ring_at + 1 - at_core
    gains = jnp.concatenate([norm_gain, norm_gain]).reshape(2 * RING, 2, wide_piece)
    gains = lax.dynamic_slice(gains, (at_x, at_core, 0), (RING, 1, wide_piece)).reshape(1, -1)

    chosen = (expert_ids[:, :, None] == dps[None, None, :]).astype(i32)
    named = jnp.sum(chosen, axis=1)
    weight = jnp.sum(chosen.astype(f32) * gate_weights[:, :, None], axis=1)
    rank = jnp.sum(before(tokens)[:, :, None] * named[:, None, :], axis=0)
    rank = jnp.where(named > 0, rank, -1)
    ranks = jnp.arange(CAP, dtype=i32)
    placing = (rank.T[:, None, :] == ranks[None, :, None]).astype(bf16)
    placing = placing.reshape(DP_N * CAP, tokens)

    attended, early, late = home_rows(
        jnp.concatenate([spots_here, spots_there]), here, there, gains, placing, cut
    )

    def exchange(block):
        block = lax.all_to_all(block.reshape(DP_N, CAP, -1), DP, 0, 0, tiled=True)
        return block.reshape(DP_N * CAP, -1)

    early = exchange(early)
    early, late = lax.optimization_barrier((early, late))
    late = exchange(late)
    hops = [hop(early, "x", k) for k in (1, 2, 3)]
    late, hops = lax.optimization_barrier((late, hops))
    early = jnp.concatenate([early] + hops, axis=1)

    early_own, early_away, late_own, late_away, out_early, give_early, out_late, give_late = weights

    def product(rows, pair):
        return [jnp.dot(rows, w, preferred_element_type=f32) for w in pair]

    early_there, late_there = other_core(early), other_core(late)
    sums = [
        sum(terms)
        for terms in zip(
            product(early, early_own),
            product(late, late_own),
            product(early_there, early_away),
            product(late_there, late_away),
        )
    ]
    hidden = lax.optimization_barrier((jax.nn.silu(sums[0]) * sums[1]).astype(bf16))

    def output(keep, give):
        give = jnp.dot(hidden, give, preferred_element_type=f32).astype(bf16)
        return (jnp.dot(hidden, keep, preferred_element_type=f32) + other_core(give).astype(f32)).astype(bf16)

    late, early = output(out_late, give_late), output(out_early, give_early)
    early, late = lax.optimization_barrier((early, late))

    def ring_sum(block, size):
        total = block[:, :size].astype(f32)
        for k in (2, 1, 3):
            total = total + send(block[:, k * size : (k + 1) * size], "x", k).astype(f32)
        return total

    late = exchange(late)
    early, late = lax.optimization_barrier((ring_sum(early, cut).astype(bf16), late))
    early = exchange(early)

    mix = jnp.where(rank[:, :, None] == ranks[None, None, :], weight[:, :, None], 0.0)
    mix = mix.reshape(tokens, DP_N * CAP)
    coarse = lax.reduce_precision(mix, 8, 7)
    both = jnp.concatenate([coarse.astype(bf16), (mix - coarse).astype(bf16)], axis=0)

    def mixed(block):
        block = jnp.dot(both, block, preferred_element_type=f32)
        return block[:tokens] + block[tokens:]

    late = mixed(late).astype(bf16)
    late = lax.dynamic_slice_in_dim(
        jnp.concatenate([late, late], axis=1), at_x * rest, RING * rest, 1
    )
    late = ring_sum(late, rest)
    routed = jnp.concatenate([mixed(early), late], axis=1).astype(bf16)
    return (attended, routed)


def solution(mesh):
    grid = Mesh(mesh.devices.reshape(RING, RING, RING, 2), ALL)
    return jax.shard_map(
        shards,
        mesh=grid,
        in_specs=(
            P(DP, HEAD, None),
            P(DP, None, None),
            P(DP, None),
            P(DP),
            P(DP),
            P(HEAD, None, None),
            P(HEAD, DP),
            P(DP, None),
            P(),
            P(DP, None),
            P(DP, None),
            P(DP, None, HEAD),
            P(DP, None, HEAD),
            P(DP, HEAD, None),
        ),
        out_specs=(P(DP, None), P(DP, HEAD)),
        check_vma=False,
    )
```

```python
import functools

import jax
import jax.numpy as jnp
from jax import lax
from jax.experimental import pallas as pl
from jax.experimental.pallas import tpu as pltpu
from jax.sharding import Mesh
from jax.sharding import PartitionSpec as P

LAT = 512
DP = ("y", "z")
HEAD = ("x", "core")
ALL = ("y", "z", "x", "core")
RING = 4
DP_N = 16
HEAD_N = 8
PAGES = 128
CAP = 32

softmax_scale = 192.0 ** (-0.5)
norm_eps = 1e-06
bf16 = jnp.bfloat16
f32 = jnp.float32
i32 = jnp.int32


def hop(array, axis, step):
    return lax.ppermute(array, axis, [((i + step) % RING, i) for i in range(RING)])


def send(array, axis, step):
    return lax.ppermute(array, axis, [(i, (i + step) % RING) for i in range(RING)])


def other_core(array):
    return lax.ppermute(array, "core", [(0, 1), (1, 0)])


def pack_kernel(me_ref, page_ref, query_ref, out_ref, who_ref):
    me = me_ref[0]
    width = query_ref.shape[2]
    requests, per = page_ref.shape[0], page_ref.shape[1] - 1
    rows = out_ref.shape[1]
    lanes = out_ref.shape[2] - width

    row = lax.broadcasted_iota(i32, (rows, lanes), 0)
    lane = lax.broadcasted_iota(i32, (rows, lanes), 1)

    def clear(i, carry):
        who_ref[i] = -1
        return carry

    lax.fori_loop(0, DP_N, clear, 0)
    lane = jnp.where(row == 0, lane, -1)
    base = jnp.zeros((rows, lanes), f32)
    for r in range(requests):
        lender = page_ref[r, 0] // PAGES
        base = jnp.where(lane == 24 + r, lender.astype(f32), base)

        @pl.when(lender != me)
        def _():
            who_ref[lender] = r

    def one(i, carry):
        found = who_ref[i]
        r = jnp.maximum(found, 0)
        seen = page_ref[r, per]
        told = [page_ref[r, k] - page_ref[r, 0] // PAGES * PAGES for k in range(per)]
        told += [seen // 2, seen % 2, jnp.where(found >= 0, 1, 0)]
        line = base
        for k, value in enumerate(told):
            line = jnp.where(lane == 8 + k, value.astype(f32), line)
        out_ref[i, :, :width] = query_ref[r]
        out_ref[i, :, width:] = line.astype(bf16)
        return carry

    lax.fori_loop(0, DP_N, one, 0)


def pack(me, table, query_rows):
    count, rows, width = query_rows.shape
    scalar, vector = (pl.BlockSpec(memory_space=m) for m in (pltpu.SMEM, pltpu.VMEM))
    return pl.pallas_call(
        pack_kernel,
        out_shape=jax.ShapeDtypeStruct((DP_N, rows, width + 64), bf16),
        in_specs=[scalar] * 2 + [vector],
        out_specs=vector,
        scratch_shapes=[pltpu.SMEM((DP_N,), i32)],
        compiler_params=pltpu.CompilerParams(vmem_limit_bytes=32 * 2**20),
        name="pack",
    )(me, table, query_rows)


def attend_kernel(
    me_ref, page_ref, told_ref, query_ref, pool_ref, out_ref,
    which_ref, list_ref, seen_ref, keys_ref, held_pool_ref, sems, own,
):
    me = me_ref[0]
    count, rows, _ = query_ref.shape
    page_rows, width, pages = pool_ref.shape
    chunks = sems.shape[0]
    size = page_rows // chunks
    copies = [
        pltpu.make_async_copy(
            pool_ref.at[pl.ds(n * size, size)], held_pool_ref.at[pl.ds(n * size, size)], sems.at[n]
        )
        for n in range(chunks)
    ]
    for copy in copies:
        copy.start()
    per = page_ref.shape[1] - 1
    slots = count // 2

    def plan(r, at):
        found = page_ref[r, 0] // PAGES == me if own else told_ref[r, 10] > 0
        spot = jnp.minimum(at, slots - 1)

        @pl.when(found)
        def _():
            which_ref[spot] = r
            if own:
                seen_ref[spot] = page_ref[r, per]
            else:
                seen_ref[spot] = told_ref[r, 8] * 2 + told_ref[r, 9]
            for k in range(per):
                list_ref[spot * per + k] = page_ref[r, k] - me * PAGES if own else told_ref[r, k]

        return at + found.astype(i32)

    lax.fori_loop(0, count, plan, jnp.int32(0))
    row = lax.broadcasted_iota(i32, (slots * per, pages), 0)
    lane = lax.broadcasted_iota(i32, (slots * per, pages), 1)
    wanted = jnp.zeros((slots * per, pages), i32)
    for n in range(slots * per):
        wanted = jnp.where(row == n, list_ref[n], wanted)
    order = jnp.where(wanted == lane, 1.0, 0.0).astype(bf16)

    def sort(i, carry):
        sorted_rows = lax.dot_general(
            order, held_pool_ref[i], (((1,), (1,)), ((), ())), preferred_element_type=f32
        ).astype(bf16)
        for pair in range(slots // 2):
            keys_ref[pair, pl.ds(pl.multiple_of(i * 16, 16), 16), :] = sorted_rows[
                pair * 16 : (pair + 1) * 16
            ]
        return carry

    for n in range(chunks):
        copies[n].wait()
        lax.fori_loop(n * size, (n + 1) * size, sort, 0, unroll=True)
    keys_at = lax.broadcasted_iota(i32, (2 * rows, page_rows * 16), 1)
    query_at = lax.broadcasted_iota(i32, (2 * rows, page_rows * 16), 0)
    position = keys_at % 8 * page_rows + keys_at // 16
    second = query_at >= rows
    same = (keys_at // 8 % 2 == 1) == second
    draft = jnp.where(second, query_at - rows, query_at) // (rows // 3)
    offset = jnp.where(same, position - draft, 1 << 20)
    for pair in range(slots // 2):
        queries = jnp.concatenate(
            [query_ref[which_ref[2 * pair + n], :, :width] for n in range(2)], axis=0
        )
        keys = keys_ref[pair]
        scores = (
            lax.dot_general(queries, keys, (((1,), (1,)), ((), ())), preferred_element_type=f32)
            * softmax_scale
        )
        allowed = offset <= jnp.where(second, seen_ref[2 * pair + 1], seen_ref[2 * pair])
        highest = jnp.max(jnp.where(allowed, scores, -1e30), axis=-1, keepdims=True)
        weights = jnp.where(allowed, jnp.exp(jnp.where(allowed, scores - highest, 0.0)), 0.0)
        probs = (weights / jnp.sum(weights, axis=-1, keepdims=True)).astype(bf16)
        latent = lax.dot_general(
            probs, keys[:, :LAT], (((1,), (0,)), ((), ())), preferred_element_type=f32
        ).astype(bf16)
        out_ref[2 * pair] = latent[:rows]
        out_ref[2 * pair + 1] = latent[rows:]


def attend(own, me, table, told, queries, pool):
    count, rows, _ = queries.shape
    page_rows, width, pages = pool.shape
    per, slots = table.shape[1] - 1, count // 2
    scalar, vector = (pl.BlockSpec(memory_space=m) for m in (pltpu.SMEM, pltpu.VMEM))
    return pl.pallas_call(
        functools.partial(attend_kernel, own=own),
        out_shape=jax.ShapeDtypeStruct((slots, rows, LAT), bf16),
        in_specs=[scalar] * 3 + [vector, pl.BlockSpec(memory_space=pl.ANY)],
        out_specs=vector,
        scratch_shapes=[
            pltpu.SMEM((slots,), i32),
            pltpu.SMEM((slots * per,), i32),
            pltpu.SMEM((slots,), i32),
            pltpu.VMEM((slots // 2, page_rows * 16, width), bf16),
            pltpu.VMEM((page_rows, width, pages), bf16),
            pltpu.SemaphoreType.DMA((4,)),
        ],
        compiler_params=pltpu.CompilerParams(vmem_limit_bytes=56 * 2**20),
        cost_estimate=pl.CostEstimate(
            flops=4_000_000_000, bytes_accessed=12_000_000, transcendentals=0
        ),
        name="attend_own" if own else "attend_far",
    )(me, table, told, queries, pool)


def home_kernel(
    spot_ref, here_ref, there_ref, gain_ref, placing_ref, attended_ref, early_ref, late_ref
):
    wide = here_ref.shape[1] // RING
    cut, rest = early_ref.shape[1], late_ref.shape[1] // RING
    here, there = here_ref[...], there_ref[...]
    for k in range(RING):
        for side, block in enumerate((here, there)):
            start = pl.multiple_of(spot_ref[side * RING + k] * wide, 128)
            attended_ref[:, pl.ds(start, wide)] = block[:, k * wide : (k + 1) * wide]
    rows, rows_there = here.astype(f32), there.astype(f32)
    squares = jnp.sum(rows * rows, axis=1, keepdims=True) + jnp.sum(
        rows_there * rows_there, axis=1, keepdims=True
    )
    root = lax.rsqrt(squares / attended_ref.shape[1] + norm_eps)
    normed = (rows * root * gain_ref[...]).astype(bf16)
    placing = placing_ref[...]
    early_ref[...] = jnp.dot(placing, normed[:, :cut], preferred_element_type=f32).astype(bf16)
    for k in range(RING):
        start = pl.multiple_of(spot_ref[k] // 2 * rest, 128)
        late_ref[:, pl.ds(start, rest)] = jnp.dot(
            placing, normed[:, k * wide + cut : (k + 1) * wide], preferred_element_type=f32
        ).astype(bf16)


def home_rows(spots, here, there, gains, placing, cut):
    tokens, half = here.shape
    slots = placing.shape[0]
    vector = pl.BlockSpec(memory_space=pltpu.VMEM)
    return pl.pallas_call(
        home_kernel,
        out_shape=[
            jax.ShapeDtypeStruct((tokens, 2 * half), bf16),
            jax.ShapeDtypeStruct((slots, cut), bf16),
            jax.ShapeDtypeStruct((slots, half - RING * cut), bf16),
        ],
        in_specs=[pl.BlockSpec(memory_space=pltpu.SMEM)] + [vector] * 4,
        out_specs=[vector] * 3,
        compiler_params=pltpu.CompilerParams(vmem_limit_bytes=32 * 2**20),
        name="home_rows",
    )(spots, here, there, gains, placing)


def before(count):
    at = jnp.arange(count, dtype=i32)
    return at[:, None] < at[None, :]


def shards(
    queries,
    kv_pool,
    page_table,
    cache_len,
    accepted,
    w_uv,
    w_o,
    residual,
    norm_gain,
    expert_ids,
    gate_weights,
    w_gate,
    w_up,
    w_down,
):
    at_x, at_y, at_z = lax.axis_index("x"), lax.axis_index("y"), lax.axis_index("z")
    at_core = lax.axis_index("core")
    dp_index = at_y * RING + at_z
    requests = page_table.shape[0]
    tokens, head_group, width = queries.shape
    query_rows = queries.reshape(requests, 3 * head_group, width)
    dps = jnp.arange(DP_N, dtype=i32)
    me = dp_index.astype(i32)[None]

    table = jnp.concatenate([page_table, (cache_len + accepted)[:, None]], axis=1)
    packed = pack(me, table, query_rows)
    arrived = lax.all_to_all(packed, DP, 0, 0, tiled=True)
    told = arrived[:, 0, width:]
    lenders = told[:, 24:40].astype(i32)
    line = told[:, 8:24].astype(i32)
    pool = kv_pool.transpose(1, 2, 0)

    def values_of(own, told, rows):
        latent = attend(own, me, table, told, rows, pool)
        values = jnp.einsum(
            "thc,hcv->thv",
            latent.reshape(tokens // 2, head_group, LAT),
            w_uv,
            preferred_element_type=f32,
        ).astype(bf16)
        return values.reshape(tokens // 2, head_group * w_uv.shape[2])

    values = jnp.concatenate(
        [values_of(True, table, query_rows), values_of(False, line, arrived)], axis=0
    )

    half = values.shape[1] // 2

    def spread(block, first, second):
        line = jnp.concatenate([block] + [hop(block, first, k) for k in (1, 2, 3)], axis=0)
        return [line] + [hop(line, second, k) for k in (1, 2, 3)]

    zy = spread(values[:, :half], "z", "y")
    yz = spread(values[:, half:], "y", "z")
    part_zy = jnp.concatenate(
        [jnp.dot(a, w_o[:half], preferred_element_type=f32) for a in zy], axis=0
    )
    part_yz = jnp.concatenate(
        [jnp.dot(a, w_o[half:], preferred_element_type=f32) for a in yz], axis=0
    )
    columns = w_o.shape[1]
    part_yz = part_yz.reshape(RING, RING, tokens, columns).transpose(1, 0, 2, 3)
    projected = (part_zy + part_yz.reshape(-1, columns)).astype(bf16)

    is_own = (lenders == dps[:, None]).astype(i32)
    own_slot = jnp.sum(is_own[:, :, None] * before(requests)[None], axis=1)
    at_lender = (lenders[:, :, None] == dps[None, None, :]).astype(i32)
    away = at_lender * (dps[:, None, None] != dps[None, None, :])
    lends = jnp.sum(away, axis=1)
    lend_rank = jnp.sum(before(DP_N)[:, :, None] * lends[:, None, :], axis=0)
    far_slot = 8 + jnp.sum(at_lender * lend_rank[:, None, :], axis=2)
    slot = jnp.where(is_own > 0, own_slot, far_slot)
    turned = ((lenders // RING - at_y) % RING) * RING + (lenders % RING - at_z) % RING
    first_row = (turned * requests + slot) * 3
    source = (first_row[:, :, None] + jnp.arange(3, dtype=i32)).reshape(-1)
    rows_all = projected.shape[0]
    moves = (source[:, None] == jnp.arange(rows_all, dtype=i32)[None, :]).astype(bf16)
    homed = jnp.dot(moves, projected, preferred_element_type=f32).astype(bf16)
    wide_piece = w_down.shape[2] // HEAD_N
    cut = 3 * wide_piece // 7
    rest = wide_piece - cut
    away = 1 - at_core
    homed, w_gate, w_up, w_down = lax.optimization_barrier((homed, w_gate, w_up, w_down))

    def spot(k, core):
        return ((at_x + k) % RING * 2 + core) * wide_piece

    def in_first(core):
        return [
            jnp.concatenate(
                [lax.dynamic_slice_in_dim(w[0], spot(k, core), cut, 0) for k in range(RING)], axis=0
            )
            for w in (w_gate, w_up)
        ]

    def in_last(core):
        views = [w[0].reshape(RING, 2, wide_piece, -1) for w in (w_gate, w_up)]
        return [
            lax.dynamic_slice_in_dim(v, core, 1, 1)[:, 0, cut:].reshape(RING * rest, -1)
            for v in views
        ]

    def out_first(core):
        cuts = [lax.dynamic_slice_in_dim(w_down[0], spot(k, core), cut, 1) for k in range(RING)]
        return jnp.concatenate(cuts, axis=1)

    def out_last(core):
        starts = [(2 * k + core) * wide_piece + cut for k in range(RING)]
        cuts = [lax.dynamic_slice_in_dim(w_down[0], start, rest, 1) for start in starts]
        return jnp.concatenate(cuts, axis=1)

    weights = [
        in_first(at_core), in_first(away), in_last(at_core), in_last(away),
        out_first(at_core), out_first(away), out_last(at_core), out_last(away),
    ]
    homed = lax.all_to_all(homed.reshape(DP_N, tokens, columns), DP, 0, 0, tiled=True)
    homed, weights = lax.optimization_barrier((homed, weights))

    homed = homed.reshape(RING, 2, 2, tokens, columns)
    homed = lax.dynamic_slice_in_dim(jnp.concatenate([homed, homed], 0), at_x, RING, 0)
    keep = lax.dynamic_slice_in_dim(homed, at_core, 1, 1)[:, 0]
    give = lax.dynamic_slice_in_dim(homed, 1 - at_core, 1, 1)[:, 0]
    kept = keep.astype(f32) + other_core(give).astype(f32)
    attention = kept[0]
    for k in (2, 1, 3):
        attention = attention + send(kept[k].astype(bf16), "x", k).astype(f32)
    attention = jnp.concatenate([attention[0], attention[1]], axis=1)
    head_index = at_x * 2 + at_core
    near = lax.dynamic_slice_in_dim(residual, head_index * wide_piece, wide_piece, 1)
    piece = (near.astype(f32) + attention).astype(bf16)

    here = jnp.concatenate([piece] + [hop(piece, "x", k) for k in (1, 2, 3)], axis=1)
    there = other_core(here)
    ring_at = (at_x + jnp.arange(RING, dtype=i32)) % RING * 2
    spots_here, spots_there = ring_at + at_core, ring_at + 1 - at_core
    gains = jnp.concatenate([norm_gain, norm_gain]).reshape(2 * RING, 2, wide_piece)
    gains = lax.dynamic_slice(gains, (at_x, at_core, 0), (RING, 1, wide_piece)).reshape(1, -1)

    chosen = (expert_ids[:, :, None] == dps[None, None, :]).astype(i32)
    named = jnp.sum(chosen, axis=1)
    weight = jnp.sum(chosen.astype(f32) * gate_weights[:, :, None], axis=1)
    rank = jnp.sum(before(tokens)[:, :, None] * named[:, None, :], axis=0)
    rank = jnp.where(named > 0, rank, -1)
    ranks = jnp.arange(CAP, dtype=i32)
    placing = (rank.T[:, None, :] == ranks[None, :, None]).astype(bf16)
    placing = placing.reshape(DP_N * CAP, tokens)

    attended, early, late = home_rows(
        jnp.concatenate([spots_here, spots_there]), here, there, gains, placing, cut
    )

    def exchange(block):
        block = lax.all_to_all(block.reshape(DP_N, CAP, -1), DP, 0, 0, tiled=True)
        return block.reshape(DP_N * CAP, -1)

    early = exchange(early)
    early, late = lax.optimization_barrier((early, late))
    late = exchange(late)
    hops = [hop(early, "x", k) for k in (1, 2, 3)]
    late = lax.optimization_barrier((late, hops))[0]
    early = jnp.concatenate([early] + hops, axis=1)

    early_own, early_away, late_own, late_away, out_early, give_early, out_late, give_late = weights

    def product(rows, pair):
        return [jnp.dot(rows, w, preferred_element_type=f32) for w in pair]

    early_there, late_there = other_core(early), other_core(late)
    sums = [
        sum(terms)
        for terms in zip(
            product(early, early_own),
            product(late, late_own),
            product(early_there, early_away),
            product(late_there, late_away),
        )
    ]
    hidden = lax.optimization_barrier((jax.nn.silu(sums[0]) * sums[1]).astype(bf16))

    def output(keep, give):
        give = jnp.dot(hidden, give, preferred_element_type=f32).astype(bf16)
        return (jnp.dot(hidden, keep, preferred_element_type=f32) + other_core(give).astype(f32)).astype(bf16)

    late = output(out_late, give_late)
    hidden = lax.optimization_barrier((hidden, late))[0]
    early = output(out_early, give_early)

    def ring_sum(block, size):
        total = block[:, :size].astype(f32)
        for k in (2, 1, 3):
            total = total + send(block[:, k * size : (k + 1) * size], "x", k).astype(f32)
        return total

    late = exchange(late)
    early, late = lax.optimization_barrier((ring_sum(early, cut).astype(bf16), late))
    early = exchange(early)

    mix = jnp.where(rank[:, :, None] == ranks[None, None, :], weight[:, :, None], 0.0)
    mix = mix.reshape(tokens, DP_N * CAP)
    coarse = lax.reduce_precision(mix, 8, 7)
    both = jnp.concatenate([coarse.astype(bf16), (mix - coarse).astype(bf16)], axis=0)

    def mixed(block):
        block = jnp.dot(both, block, preferred_element_type=f32)
        return block[:tokens] + block[tokens:]

    late = mixed(late).astype(bf16)
    late = lax.dynamic_slice_in_dim(
        jnp.concatenate([late, late], axis=1), at_x * rest, RING * rest, 1
    )
    late = ring_sum(late, rest)
    routed = jnp.concatenate([mixed(early), late], axis=1).astype(bf16)
    return (attended, routed)


def solution(mesh):
    grid = Mesh(mesh.devices.reshape(RING, RING, RING, 2), ALL)
    return jax.shard_map(
        shards,
        mesh=grid,
        in_specs=(
            P(DP, HEAD, None),
            P(DP, None, None),
            P(DP, None),
            P(DP),
            P(DP),
            P(HEAD, None, None),
            P(HEAD, DP),
            P(DP, None),
            P(),
            P(DP, None),
            P(DP, None),
            P(DP, None, HEAD),
            P(DP, None, HEAD),
            P(DP, HEAD, None),
        ),
        out_specs=(P(DP, None), P(DP, HEAD)),
        check_vma=False,
    )
```

```python
import functools

import jax
import jax.numpy as jnp
from jax import lax
from jax.experimental import pallas as pl
from jax.experimental.pallas import tpu as pltpu
from jax.sharding import Mesh
from jax.sharding import PartitionSpec as P

LAT = 512
DP = ("y", "z")
HEAD = ("x", "core")
ALL = ("y", "z", "x", "core")
RING = 4
DP_N = 16
HEAD_N = 8
PAGES = 128
CAP = 32

softmax_scale = 192.0 ** (-0.5)
norm_eps = 1e-06
bf16 = jnp.bfloat16
f32 = jnp.float32
i32 = jnp.int32


def hop(array, axis, step):
    return lax.ppermute(array, axis, [((i + step) % RING, i) for i in range(RING)])


def send(array, axis, step):
    return lax.ppermute(array, axis, [(i, (i + step) % RING) for i in range(RING)])


def other_core(array):
    return lax.ppermute(array, "core", [(0, 1), (1, 0)])


def pack_kernel(me_ref, page_ref, query_ref, out_ref, who_ref):
    me = me_ref[0]
    width = query_ref.shape[2]
    requests, per = page_ref.shape[0], page_ref.shape[1] - 1
    rows = 16
    lanes = out_ref.shape[2] - width

    row = lax.broadcasted_iota(i32, (rows, lanes), 0)
    lane = lax.broadcasted_iota(i32, (rows, lanes), 1)

    def clear(i, carry):
        who_ref[i] = -1
        return carry

    lax.fori_loop(0, DP_N, clear, 0)
    lane = jnp.where(row == 0, lane, -1)
    base = jnp.zeros((rows, lanes), f32)
    for r in range(requests):
        lender = page_ref[r, 0] // PAGES
        base = jnp.where(lane == 24 + r, lender.astype(f32), base)

        @pl.when(lender != me)
        def _():
            who_ref[lender] = r

    def one(i, carry):
        found = who_ref[i]
        r = jnp.maximum(found, 0)
        seen = page_ref[r, per]
        told = [page_ref[r, k] - page_ref[r, 0] // PAGES * PAGES for k in range(per)]
        told += [seen // 2, seen % 2, jnp.where(found >= 0, 1, 0)]
        line = base
        for k, value in enumerate(told):
            line = jnp.where(lane == 8 + k, value.astype(f32), line)
        out_ref[i, :, :width] = query_ref[r]
        out_ref[i, :rows, width:] = line.astype(bf16)
        out_ref[i, rows:, width:] = jnp.zeros((out_ref.shape[1] - rows, lanes), bf16)
        return carry

    lax.fori_loop(0, DP_N, one, 0)


def pack(me, table, query_rows):
    count, rows, width = query_rows.shape
    scalar, vector = (pl.BlockSpec(memory_space=m) for m in (pltpu.SMEM, pltpu.VMEM))
    return pl.pallas_call(
        pack_kernel,
        out_shape=jax.ShapeDtypeStruct((DP_N, rows, width + 64), bf16),
        in_specs=[scalar] * 2 + [vector],
        out_specs=vector,
        scratch_shapes=[pltpu.SMEM((DP_N,), i32)],
        compiler_params=pltpu.CompilerParams(vmem_limit_bytes=32 * 2**20),
        name="pack",
    )(me, table, query_rows)


def attend_kernel(
    me_ref, page_ref, told_ref, query_ref, pool_ref, out_ref,
    which_ref, list_ref, seen_ref, keys_ref, held_pool_ref, sems, own,
):
    me = me_ref[0]
    count, rows, _ = query_ref.shape
    page_rows, width, pages = pool_ref.shape
    chunks = sems.shape[0]
    size = page_rows // chunks
    copies = [
        pltpu.make_async_copy(
            pool_ref.at[pl.ds(n * size, size)], held_pool_ref.at[pl.ds(n * size, size)], sems.at[n]
        )
        for n in range(chunks)
    ]
    for copy in copies:
        copy.start()
    per = page_ref.shape[1] - 1
    slots = count // 2

    def plan(r, at):
        found = page_ref[r, 0] // PAGES == me if own else told_ref[r, 10] > 0
        spot = jnp.minimum(at, slots - 1)

        @pl.when(found)
        def _():
            which_ref[spot] = r
            if own:
                seen_ref[spot] = page_ref[r, per]
            else:
                seen_ref[spot] = told_ref[r, 8] * 2 + told_ref[r, 9]
            for k in range(per):
                list_ref[spot * per + k] = page_ref[r, k] - me * PAGES if own else told_ref[r, k]

        return at + found.astype(i32)

    lax.fori_loop(0, count, plan, jnp.int32(0))
    row = lax.broadcasted_iota(i32, (slots * per, pages), 0)
    lane = lax.broadcasted_iota(i32, (slots * per, pages), 1)
    wanted = jnp.zeros((slots * per, pages), i32)
    for n in range(slots * per):
        wanted = jnp.where(row == n, list_ref[n], wanted)
    order = jnp.where(wanted == lane, 1.0, 0.0).astype(bf16)

    def sort(i, carry):
        sorted_rows = lax.dot_general(
            order, held_pool_ref[i], (((1,), (1,)), ((), ())), preferred_element_type=f32
        ).astype(bf16)
        for pair in range(slots // 2):
            keys_ref[pair, pl.ds(pl.multiple_of(i * 16, 16), 16), :] = sorted_rows[
                pair * 16 : (pair + 1) * 16
            ]
        return carry

    for n in range(chunks):
        copies[n].wait()
        lax.fori_loop(n * size, (n + 1) * size, sort, 0, unroll=True)
    keys_at = lax.broadcasted_iota(i32, (2 * rows, page_rows * 16), 1)
    query_at = lax.broadcasted_iota(i32, (2 * rows, page_rows * 16), 0)
    position = keys_at % 8 * page_rows + keys_at // 16
    second = query_at >= rows
    same = (keys_at // 8 % 2 == 1) == second
    draft = jnp.where(second, query_at - rows, query_at) // (rows // 3)
    offset = jnp.where(same, position - draft, 1 << 20)
    for pair in range(slots // 2):
        queries = jnp.concatenate(
            [query_ref[which_ref[2 * pair + n], :, :width] for n in range(2)], axis=0
        )
        keys = keys_ref[pair]
        scores = (
            lax.dot_general(queries, keys, (((1,), (1,)), ((), ())), preferred_element_type=f32)
            * softmax_scale
        )
        allowed = offset <= jnp.where(second, seen_ref[2 * pair + 1], seen_ref[2 * pair])
        highest = jnp.max(jnp.where(allowed, scores, -1e30), axis=-1, keepdims=True)
        weights = jnp.where(allowed, jnp.exp(jnp.where(allowed, scores - highest, 0.0)), 0.0)
        probs = (weights / jnp.sum(weights, axis=-1, keepdims=True)).astype(bf16)
        latent = lax.dot_general(
            probs, keys[:, :LAT], (((1,), (0,)), ((), ())), preferred_element_type=f32
        ).astype(bf16)
        out_ref[2 * pair] = latent[:rows]
        out_ref[2 * pair + 1] = latent[rows:]


def attend(own, me, table, told, queries, pool):
    count, rows, _ = queries.shape
    page_rows, width, pages = pool.shape
    per, slots = table.shape[1] - 1, count // 2
    scalar, vector = (pl.BlockSpec(memory_space=m) for m in (pltpu.SMEM, pltpu.VMEM))
    return pl.pallas_call(
        functools.partial(attend_kernel, own=own),
        out_shape=jax.ShapeDtypeStruct((slots, rows, LAT), bf16),
        in_specs=[scalar] * 3 + [vector, pl.BlockSpec(memory_space=pl.ANY)],
        out_specs=vector,
        scratch_shapes=[
            pltpu.SMEM((slots,), i32),
            pltpu.SMEM((slots * per,), i32),
            pltpu.SMEM((slots,), i32),
            pltpu.VMEM((slots // 2, page_rows * 16, width), bf16),
            pltpu.VMEM((page_rows, width, pages), bf16),
            pltpu.SemaphoreType.DMA((4,)),
        ],
        compiler_params=pltpu.CompilerParams(vmem_limit_bytes=56 * 2**20),
        cost_estimate=pl.CostEstimate(
            flops=4_000_000_000, bytes_accessed=12_000_000, transcendentals=0
        ),
        name="attend_own" if own else "attend_far",
    )(me, table, told, queries, pool)


def home_kernel(
    spot_ref, here_ref, there_ref, gain_ref, placing_ref, attended_ref, early_ref, late_ref
):
    wide = here_ref.shape[1] // RING
    cut, rest = early_ref.shape[1], late_ref.shape[1] // RING
    here, there = here_ref[...], there_ref[...]
    for k in range(RING):
        for side, block in enumerate((here, there)):
            start = pl.multiple_of(spot_ref[side * RING + k] * wide, 128)
            attended_ref[:, pl.ds(start, wide)] = block[:, k * wide : (k + 1) * wide]
    rows, rows_there = here.astype(f32), there.astype(f32)
    squares = jnp.sum(rows * rows, axis=1, keepdims=True) + jnp.sum(
        rows_there * rows_there, axis=1, keepdims=True
    )
    root = lax.rsqrt(squares / attended_ref.shape[1] + norm_eps)
    normed = (rows * root * gain_ref[...]).astype(bf16)
    placing = placing_ref[...]
    early_ref[...] = jnp.dot(placing, normed[:, :cut], preferred_element_type=f32).astype(bf16)
    for k in range(RING):
        start = pl.multiple_of(spot_ref[k] // 2 * rest, 128)
        late_ref[:, pl.ds(start, rest)] = jnp.dot(
            placing, normed[:, k * wide + cut : (k + 1) * wide], preferred_element_type=f32
        ).astype(bf16)


def home_rows(spots, here, there, gains, placing, cut):
    tokens, half = here.shape
    slots = placing.shape[0]
    vector = pl.BlockSpec(memory_space=pltpu.VMEM)
    return pl.pallas_call(
        home_kernel,
        out_shape=[
            jax.ShapeDtypeStruct((tokens, 2 * half), bf16),
            jax.ShapeDtypeStruct((slots, cut), bf16),
            jax.ShapeDtypeStruct((slots, half - RING * cut), bf16),
        ],
        in_specs=[pl.BlockSpec(memory_space=pltpu.SMEM)] + [vector] * 4,
        out_specs=[vector] * 3,
        compiler_params=pltpu.CompilerParams(vmem_limit_bytes=32 * 2**20),
        name="home_rows",
    )(spots, here, there, gains, placing)


def before(count):
    at = jnp.arange(count, dtype=i32)
    return at[:, None] < at[None, :]


def shards(
    queries,
    kv_pool,
    page_table,
    cache_len,
    accepted,
    w_uv,
    w_o,
    residual,
    norm_gain,
    expert_ids,
    gate_weights,
    w_gate,
    w_up,
    w_down,
):
    at_x, at_y, at_z = lax.axis_index("x"), lax.axis_index("y"), lax.axis_index("z")
    at_core = lax.axis_index("core")
    dp_index = at_y * RING + at_z
    requests = page_table.shape[0]
    tokens, head_group, width = queries.shape
    query_rows = queries.reshape(requests, 3 * head_group, width)
    dps = jnp.arange(DP_N, dtype=i32)
    me = dp_index.astype(i32)[None]

    table = jnp.concatenate([page_table, (cache_len + accepted)[:, None]], axis=1)
    packed = pack(me, table, query_rows)
    arrived = lax.all_to_all(packed, DP, 0, 0, tiled=True)
    told = arrived[:, 0, width:]
    lenders = told[:, 24:40].astype(i32)
    line = told[:, 8:24].astype(i32)
    pool = kv_pool.transpose(1, 2, 0)

    def values_of(own, told, rows):
        latent = attend(own, me, table, told, rows, pool)
        values = jnp.einsum(
            "thc,hcv->thv",
            latent.reshape(tokens // 2, head_group, LAT),
            w_uv,
            preferred_element_type=f32,
        ).astype(bf16)
        return values.reshape(tokens // 2, head_group * w_uv.shape[2])

    values = jnp.concatenate(
        [values_of(True, table, query_rows), values_of(False, line, arrived)], axis=0
    )

    half = values.shape[1] // 2

    def spread(block, first, second):
        line = jnp.concatenate([block] + [hop(block, first, k) for k in (1, 2, 3)], axis=0)
        return [line] + [hop(line, second, k) for k in (1, 2, 3)]

    zy = spread(values[:, :half], "z", "y")
    yz = spread(values[:, half:], "y", "z")
    part_zy = jnp.concatenate(
        [jnp.dot(a, w_o[:half], preferred_element_type=f32) for a in zy], axis=0
    )
    part_yz = jnp.concatenate(
        [jnp.dot(a, w_o[half:], preferred_element_type=f32) for a in yz], axis=0
    )
    columns = w_o.shape[1]
    part_yz = part_yz.reshape(RING, RING, tokens, columns).transpose(1, 0, 2, 3)
    projected = (part_zy + part_yz.reshape(-1, columns)).astype(bf16)

    is_own = (lenders == dps[:, None]).astype(i32)
    own_slot = jnp.sum(is_own[:, :, None] * before(requests)[None], axis=1)
    at_lender = (lenders[:, :, None] == dps[None, None, :]).astype(i32)
    away = at_lender * (dps[:, None, None] != dps[None, None, :])
    lends = jnp.sum(away, axis=1)
    lend_rank = jnp.sum(before(DP_N)[:, :, None] * lends[:, None, :], axis=0)
    far_slot = 8 + jnp.sum(at_lender * lend_rank[:, None, :], axis=2)
    slot = jnp.where(is_own > 0, own_slot, far_slot)
    turned = ((lenders // RING - at_y) % RING) * RING + (lenders % RING - at_z) % RING
    first_row = (turned * requests + slot) * 3
    source = (first_row[:, :, None] + jnp.arange(3, dtype=i32)).reshape(-1)
    rows_all = projected.shape[0]
    moves = (source[:, None] == jnp.arange(rows_all, dtype=i32)[None, :]).astype(bf16)
    homed = jnp.dot(moves, projected, preferred_element_type=f32).astype(bf16)
    wide_piece = w_down.shape[2] // HEAD_N
    cut = 3 * wide_piece // 7
    rest = wide_piece - cut
    away = 1 - at_core
    homed, w_gate, w_up, w_down = lax.optimization_barrier((homed, w_gate, w_up, w_down))

    def spot(k, core):
        return ((at_x + k) % RING * 2 + core) * wide_piece

    def in_first(core):
        return [
            jnp.concatenate(
                [lax.dynamic_slice_in_dim(w[0], spot(k, core), cut, 0) for k in range(RING)], axis=0
            )
            for w in (w_gate, w_up)
        ]

    def in_last(core):
        views = [w[0].reshape(RING, 2, wide_piece, -1) for w in (w_gate, w_up)]
        return [
            lax.dynamic_slice_in_dim(v, core, 1, 1)[:, 0, cut:].reshape(RING * rest, -1)
            for v in views
        ]

    def out_first(core):
        cuts = [lax.dynamic_slice_in_dim(w_down[0], spot(k, core), cut, 1) for k in range(RING)]
        return jnp.concatenate(cuts, axis=1)

    def out_last(core):
        starts = [(2 * k + core) * wide_piece + cut for k in range(RING)]
        cuts = [lax.dynamic_slice_in_dim(w_down[0], start, rest, 1) for start in starts]
        return jnp.concatenate(cuts, axis=1)

    weights = [
        in_first(at_core), in_first(away), in_last(at_core), in_last(away),
        out_first(at_core), out_first(away), out_last(at_core), out_last(away),
    ]
    homed = lax.all_to_all(homed.reshape(DP_N, tokens, columns), DP, 0, 0, tiled=True)
    homed, weights = lax.optimization_barrier((homed, weights))

    homed = homed.reshape(RING, 2, 2, tokens, columns)
    homed = lax.dynamic_slice_in_dim(jnp.concatenate([homed, homed], 0), at_x, RING, 0)
    keep = lax.dynamic_slice_in_dim(homed, at_core, 1, 1)[:, 0]
    give = lax.dynamic_slice_in_dim(homed, 1 - at_core, 1, 1)[:, 0]
    kept = keep.astype(f32) + other_core(give).astype(f32)
    attention = kept[0]
    for k in (2, 1, 3):
        attention = attention + send(kept[k].astype(bf16), "x", k).astype(f32)
    attention = jnp.concatenate([attention[0], attention[1]], axis=1)
    head_index = at_x * 2 + at_core
    near = lax.dynamic_slice_in_dim(residual, head_index * wide_piece, wide_piece, 1)
    piece = (near.astype(f32) + attention).astype(bf16)

    here = jnp.concatenate([piece] + [hop(piece, "x", k) for k in (1, 2, 3)], axis=1)
    there = other_core(here)
    ring_at = (at_x + jnp.arange(RING, dtype=i32)) % RING * 2
    spots_here, spots_there = ring_at + at_core, ring_at + 1 - at_core
    gains = jnp.concatenate([norm_gain, norm_gain]).reshape(2 * RING, 2, wide_piece)
    gains = lax.dynamic_slice(gains, (at_x, at_core, 0), (RING, 1, wide_piece)).reshape(1, -1)

    chosen = (expert_ids[:, :, None] == dps[None, None, :]).astype(i32)
    named = jnp.sum(chosen, axis=1)
    weight = jnp.sum(chosen.astype(f32) * gate_weights[:, :, None], axis=1)
    rank = jnp.sum(before(tokens)[:, :, None] * named[:, None, :], axis=0)
    rank = jnp.where(named > 0, rank, -1)
    ranks = jnp.arange(CAP, dtype=i32)
    placing = (rank.T[:, None, :] == ranks[None, :, None]).astype(bf16)
    placing = placing.reshape(DP_N * CAP, tokens)

    attended, early, late = home_rows(
        jnp.concatenate([spots_here, spots_there]), here, there, gains, placing, cut
    )

    def exchange(block):
        block = lax.all_to_all(block.reshape(DP_N, CAP, -1), DP, 0, 0, tiled=True)
        return block.reshape(DP_N * CAP, -1)

    early = exchange(early)
    early, late = lax.optimization_barrier((early, late))
    late = exchange(late)
    hops = [hop(early, "x", k) for k in (1, 2, 3)]
    late = lax.optimization_barrier((late, hops))[0]
    early = jnp.concatenate([early] + hops, axis=1)

    early_own, early_away, late_own, late_away, out_early, give_early, out_late, give_late = weights

    def product(rows, pair):
        return jnp.dot(rows, jnp.concatenate(pair, axis=1), preferred_element_type=f32)

    units = w_gate.shape[2]
    early_there, late_there = other_core(early), other_core(late)
    sums = product(early, early_own) + product(early_there, early_away)
    sums = sums + product(late, late_own) + product(late_there, late_away)
    hidden = (jax.nn.silu(sums[:, :units]) * sums[:, units:]).astype(bf16)
    hidden = lax.optimization_barrier(hidden)

    def output(keep, give):
        give = jnp.dot(hidden, give, preferred_element_type=f32).astype(bf16)
        return (jnp.dot(hidden, keep, preferred_element_type=f32) + other_core(give).astype(f32)).astype(bf16)

    late = output(out_late, give_late)
    hidden = lax.optimization_barrier((hidden, late))[0]
    early = output(out_early, give_early)

    def ring_sum(block, size):
        total = block[:, :size].astype(f32)
        for k in (2, 1, 3):
            total = total + send(block[:, k * size : (k + 1) * size], "x", k).astype(f32)
        return total

    late = exchange(late)
    early, late = lax.optimization_barrier((ring_sum(early, cut).astype(bf16), late))
    early = exchange(early)

    mix = jnp.where(rank[:, :, None] == ranks[None, None, :], weight[:, :, None], 0.0)
    mix = mix.reshape(tokens, DP_N * CAP)
    coarse = lax.reduce_precision(mix, 8, 7)
    both = jnp.concatenate([coarse.astype(bf16), (mix - coarse).astype(bf16)], axis=0)

    def mixed(block):
        block = jnp.dot(both, block, preferred_element_type=f32)
        return block[:tokens] + block[tokens:]

    late = mixed(late).astype(bf16)
    late = lax.dynamic_slice_in_dim(
        jnp.concatenate([late, late], axis=1), at_x * rest, RING * rest, 1
    )
    late = ring_sum(late, rest)
    routed = jnp.concatenate([mixed(early), late], axis=1).astype(bf16)
    return (attended, routed)


def solution(mesh):
    grid = Mesh(mesh.devices.reshape(RING, RING, RING, 2), ALL)
    return jax.shard_map(
        shards,
        mesh=grid,
        in_specs=(
            P(DP, HEAD, None),
            P(DP, None, None),
            P(DP, None),
            P(DP),
            P(DP),
            P(HEAD, None, None),
            P(HEAD, DP),
            P(DP, None),
            P(),
            P(DP, None),
            P(DP, None),
            P(DP, None, HEAD),
            P(DP, None, HEAD),
            P(DP, HEAD, None),
        ),
        out_specs=(P(DP, None), P(DP, HEAD)),
        check_vma=False,
    )
```

```python
import functools

import jax
import jax.numpy as jnp
from jax import lax
from jax.experimental import pallas as pl
from jax.experimental.pallas import tpu as pltpu
from jax.sharding import Mesh
from jax.sharding import PartitionSpec as P

LAT = 512
DP = ("y", "z")
HEAD = ("x", "core")
ALL = ("y", "z", "x", "core")
RING = 4
DP_N = 16
HEAD_N = 8
PAGES = 128
CAP = 32

softmax_scale = 192.0 ** (-0.5)
norm_eps = 1e-06
bf16 = jnp.bfloat16
f32 = jnp.float32
i32 = jnp.int32


def hop(array, axis, step):
    return lax.ppermute(array, axis, [((i + step) % RING, i) for i in range(RING)])


def send(array, axis, step):
    return lax.ppermute(array, axis, [(i, (i + step) % RING) for i in range(RING)])


def other_core(array):
    return lax.ppermute(array, "core", [(0, 1), (1, 0)])


def pack_kernel(me_ref, page_ref, query_ref, out_ref, who_ref):
    me = me_ref[0]
    width = query_ref.shape[2]
    requests, per = page_ref.shape[0], page_ref.shape[1] - 1
    rows = 16
    lanes = out_ref.shape[2] - width

    row = lax.broadcasted_iota(i32, (rows, lanes), 0)
    lane = lax.broadcasted_iota(i32, (rows, lanes), 1)

    def clear(i, carry):
        who_ref[i] = -1
        return carry

    lax.fori_loop(0, DP_N, clear, 0)
    lane = jnp.where(row == 0, lane, -1)
    base = jnp.zeros((rows, lanes), f32)
    for r in range(requests):
        lender = page_ref[r, 0] // PAGES
        base = jnp.where(lane == 24 + r, lender.astype(f32), base)

        @pl.when(lender != me)
        def _():
            who_ref[lender] = r

    def one(i, carry):
        found = who_ref[i]
        r = jnp.maximum(found, 0)
        seen = page_ref[r, per]
        told = [page_ref[r, k] - page_ref[r, 0] // PAGES * PAGES for k in range(per)]
        told += [seen // 2, seen % 2, jnp.where(found >= 0, 1, 0)]
        line = base
        for k, value in enumerate(told):
            line = jnp.where(lane == 8 + k, value.astype(f32), line)
        out_ref[i, :, :width] = query_ref[r]
        out_ref[i, :rows, width:] = line.astype(bf16)
        out_ref[i, rows:, width:] = jnp.zeros((out_ref.shape[1] - rows, lanes), bf16)
        return carry

    lax.fori_loop(0, DP_N, one, 0)


def pack(me, table, query_rows):
    count, rows, width = query_rows.shape
    scalar, vector = (pl.BlockSpec(memory_space=m) for m in (pltpu.SMEM, pltpu.VMEM))
    return pl.pallas_call(
        pack_kernel,
        out_shape=jax.ShapeDtypeStruct((DP_N, rows, width + 64), bf16),
        in_specs=[scalar] * 2 + [vector],
        out_specs=vector,
        scratch_shapes=[pltpu.SMEM((DP_N,), i32)],
        compiler_params=pltpu.CompilerParams(vmem_limit_bytes=32 * 2**20),
        name="pack",
    )(me, table, query_rows)


def attend_kernel(
    me_ref, page_ref, told_ref, query_ref, pool_ref, out_ref,
    which_ref, list_ref, seen_ref, keys_ref, held_pool_ref, sems, own,
):
    me = me_ref[0]
    count, rows, _ = query_ref.shape
    page_rows, width, pages = pool_ref.shape
    chunks = sems.shape[0]
    size = page_rows // chunks
    copies = [
        pltpu.make_async_copy(
            pool_ref.at[pl.ds(n * size, size)], held_pool_ref.at[pl.ds(n * size, size)], sems.at[n]
        )
        for n in range(chunks)
    ]
    for copy in copies:
        copy.start()
    per = page_ref.shape[1] - 1
    slots = count // 2

    def plan(r, at):
        found = page_ref[r, 0] // PAGES == me if own else told_ref[r, 10] > 0
        spot = jnp.minimum(at, slots - 1)

        @pl.when(found)
        def _():
            which_ref[spot] = r
            if own:
                seen_ref[spot] = page_ref[r, per]
            else:
                seen_ref[spot] = told_ref[r, 8] * 2 + told_ref[r, 9]
            for k in range(per):
                list_ref[spot * per + k] = page_ref[r, k] - me * PAGES if own else told_ref[r, k]

        return at + found.astype(i32)

    lax.fori_loop(0, count, plan, jnp.int32(0))
    row = lax.broadcasted_iota(i32, (slots * per, pages), 0)
    lane = lax.broadcasted_iota(i32, (slots * per, pages), 1)
    wanted = jnp.zeros((slots * per, pages), i32)
    for n in range(slots * per):
        wanted = jnp.where(row == n, list_ref[n], wanted)
    order = jnp.where(wanted == lane, 1.0, 0.0).astype(bf16)

    def sort(i, carry):
        sorted_rows = lax.dot_general(
            order, held_pool_ref[i], (((1,), (1,)), ((), ())), preferred_element_type=f32
        ).astype(bf16)
        for pair in range(slots // 2):
            keys_ref[pair, pl.ds(pl.multiple_of(i * 16, 16), 16), :] = sorted_rows[
                pair * 16 : (pair + 1) * 16
            ]
        return carry

    for n in range(chunks):
        copies[n].wait()
        lax.fori_loop(n * size, (n + 1) * size, sort, 0, unroll=True)
    keys_at = lax.broadcasted_iota(i32, (2 * rows, page_rows * 16), 1)
    query_at = lax.broadcasted_iota(i32, (2 * rows, page_rows * 16), 0)
    position = keys_at % 8 * page_rows + keys_at // 16
    second = query_at >= rows
    same = (keys_at // 8 % 2 == 1) == second
    draft = jnp.where(second, query_at - rows, query_at) // (rows // 3)
    offset = jnp.where(same, position - draft, 1 << 20)
    for pair in range(slots // 2):
        queries = jnp.concatenate(
            [query_ref[which_ref[2 * pair + n], :, :width] for n in range(2)], axis=0
        )
        keys = keys_ref[pair]
        scores = (
            lax.dot_general(queries, keys, (((1,), (1,)), ((), ())), preferred_element_type=f32)
            * softmax_scale
        )
        allowed = offset <= jnp.where(second, seen_ref[2 * pair + 1], seen_ref[2 * pair])
        highest = jnp.max(jnp.where(allowed, scores, -1e30), axis=-1, keepdims=True)
        weights = jnp.where(allowed, jnp.exp(jnp.where(allowed, scores - highest, 0.0)), 0.0)
        probs = (weights / jnp.sum(weights, axis=-1, keepdims=True)).astype(bf16)
        latent = lax.dot_general(
            probs, keys[:, :LAT], (((1,), (0,)), ((), ())), preferred_element_type=f32
        ).astype(bf16)
        out_ref[2 * pair] = latent[:rows]
        out_ref[2 * pair + 1] = latent[rows:]


def attend(own, me, table, told, queries, pool):
    count, rows, _ = queries.shape
    page_rows, width, pages = pool.shape
    per, slots = table.shape[1] - 1, count // 2
    scalar, vector = (pl.BlockSpec(memory_space=m) for m in (pltpu.SMEM, pltpu.VMEM))
    return pl.pallas_call(
        functools.partial(attend_kernel, own=own),
        out_shape=jax.ShapeDtypeStruct((slots, rows, LAT), bf16),
        in_specs=[scalar] * 3 + [vector, pl.BlockSpec(memory_space=pl.ANY)],
        out_specs=vector,
        scratch_shapes=[
            pltpu.SMEM((slots,), i32),
            pltpu.SMEM((slots * per,), i32),
            pltpu.SMEM((slots,), i32),
            pltpu.VMEM((slots // 2, page_rows * 16, width), bf16),
            pltpu.VMEM((page_rows, width, pages), bf16),
            pltpu.SemaphoreType.DMA((4,)),
        ],
        compiler_params=pltpu.CompilerParams(vmem_limit_bytes=56 * 2**20),
        cost_estimate=pl.CostEstimate(
            flops=4_000_000_000, bytes_accessed=12_000_000, transcendentals=0
        ),
        name="attend_own" if own else "attend_far",
    )(me, table, told, queries, pool)


def home_kernel(
    spot_ref, here_ref, there_ref, gain_ref, placing_ref, attended_ref, early_ref, late_ref
):
    wide = here_ref.shape[1] // RING
    cut, rest = early_ref.shape[1], late_ref.shape[1] // RING
    here, there = here_ref[...], there_ref[...]
    for k in range(RING):
        for side, block in enumerate((here, there)):
            start = pl.multiple_of(spot_ref[side * RING + k] * wide, 128)
            attended_ref[:, pl.ds(start, wide)] = block[:, k * wide : (k + 1) * wide]
    rows, rows_there = here.astype(f32), there.astype(f32)
    squares = jnp.sum(rows * rows, axis=1, keepdims=True) + jnp.sum(
        rows_there * rows_there, axis=1, keepdims=True
    )
    root = lax.rsqrt(squares / attended_ref.shape[1] + norm_eps)
    normed = (rows * root * gain_ref[...]).astype(bf16)
    placing = placing_ref[...]
    early_ref[...] = jnp.dot(placing, normed[:, :cut], preferred_element_type=f32).astype(bf16)
    for k in range(RING):
        start = pl.multiple_of(spot_ref[k] // 2 * rest, 128)
        late_ref[:, pl.ds(start, rest)] = jnp.dot(
            placing, normed[:, k * wide + cut : (k + 1) * wide], preferred_element_type=f32
        ).astype(bf16)


def home_rows(spots, here, there, gains, placing, cut):
    tokens, half = here.shape
    slots = placing.shape[0]
    vector = pl.BlockSpec(memory_space=pltpu.VMEM)
    return pl.pallas_call(
        home_kernel,
        out_shape=[
            jax.ShapeDtypeStruct((tokens, 2 * half), bf16),
            jax.ShapeDtypeStruct((slots, cut), bf16),
            jax.ShapeDtypeStruct((slots, half - RING * cut), bf16),
        ],
        in_specs=[pl.BlockSpec(memory_space=pltpu.SMEM)] + [vector] * 4,
        out_specs=[vector] * 3,
        compiler_params=pltpu.CompilerParams(vmem_limit_bytes=32 * 2**20),
        name="home_rows",
    )(spots, here, there, gains, placing)


def before(count):
    at = jnp.arange(count, dtype=i32)
    return at[:, None] < at[None, :]


def shards(
    queries,
    kv_pool,
    page_table,
    cache_len,
    accepted,
    w_uv,
    w_o,
    residual,
    norm_gain,
    expert_ids,
    gate_weights,
    w_gate,
    w_up,
    w_down,
):
    at_x, at_y, at_z = lax.axis_index("x"), lax.axis_index("y"), lax.axis_index("z")
    at_core = lax.axis_index("core")
    dp_index = at_y * RING + at_z
    requests = page_table.shape[0]
    tokens, head_group, width = queries.shape
    query_rows = queries.reshape(requests, 3 * head_group, width)
    dps = jnp.arange(DP_N, dtype=i32)
    me = dp_index.astype(i32)[None]

    table = jnp.concatenate([page_table, (cache_len + accepted)[:, None]], axis=1)
    packed = pack(me, table, query_rows)
    arrived = lax.all_to_all(packed, DP, 0, 0, tiled=True)
    told = arrived[:, 0, width:]
    lenders = told[:, 24:40].astype(i32)
    line = told[:, 8:24].astype(i32)
    pool = kv_pool.transpose(1, 2, 0)

    def values_of(own, told, rows):
        latent = attend(own, me, table, told, rows, pool)
        values = jnp.einsum(
            "thc,hcv->thv",
            latent.reshape(tokens // 2, head_group, LAT),
            w_uv,
            preferred_element_type=f32,
        ).astype(bf16)
        return values.reshape(tokens // 2, head_group * w_uv.shape[2])

    values = jnp.concatenate(
        [values_of(True, table, query_rows), values_of(False, line, arrived)], axis=0
    )

    half = values.shape[1] // 2

    def spread(block, first, second):
        line = jnp.concatenate([block] + [hop(block, first, k) for k in (1, 2, 3)], axis=0)
        return [line] + [hop(line, second, k) for k in (1, 2, 3)]

    zy = spread(values[:, :half], "z", "y")
    yz = spread(values[:, half:], "y", "z")
    part_zy = jnp.concatenate(
        [jnp.dot(a, w_o[:half], preferred_element_type=f32) for a in zy], axis=0
    )
    part_yz = jnp.concatenate(
        [jnp.dot(a, w_o[half:], preferred_element_type=f32) for a in yz], axis=0
    )
    columns = w_o.shape[1]
    part_yz = part_yz.reshape(RING, RING, tokens, columns).transpose(1, 0, 2, 3)
    projected = (part_zy + part_yz.reshape(-1, columns)).astype(bf16)

    is_own = (lenders == dps[:, None]).astype(i32)
    own_slot = jnp.sum(is_own[:, :, None] * before(requests)[None], axis=1)
    at_lender = (lenders[:, :, None] == dps[None, None, :]).astype(i32)
    away = at_lender * (dps[:, None, None] != dps[None, None, :])
    lends = jnp.sum(away, axis=1)
    lend_rank = jnp.sum(before(DP_N)[:, :, None] * lends[:, None, :], axis=0)
    far_slot = 8 + jnp.sum(at_lender * lend_rank[:, None, :], axis=2)
    slot = jnp.where(is_own > 0, own_slot, far_slot)
    turned = ((lenders // RING - at_y) % RING) * RING + (lenders % RING - at_z) % RING
    first_row = (turned * requests + slot) * 3
    source = (first_row[:, :, None] + jnp.arange(3, dtype=i32)).reshape(-1)
    rows_all = projected.shape[0]
    moves = (source[:, None] == jnp.arange(rows_all, dtype=i32)[None, :]).astype(bf16)
    homed = jnp.dot(moves, projected, preferred_element_type=f32).astype(bf16)
    wide_piece = w_down.shape[2] // HEAD_N
    cut = 3 * wide_piece // 7
    rest = wide_piece - cut
    away = 1 - at_core
    homed, w_gate, w_up, w_down = lax.optimization_barrier((homed, w_gate, w_up, w_down))

    def spot(k, core):
        return ((at_x + k) % RING * 2 + core) * wide_piece

    def in_first(core):
        return [
            jnp.concatenate(
                [lax.dynamic_slice_in_dim(w[0], spot(k, core), cut, 0) for k in range(RING)], axis=0
            )
            for w in (w_gate, w_up)
        ]

    def in_last(core):
        views = [w[0].reshape(RING, 2, wide_piece, -1) for w in (w_gate, w_up)]
        return [
            lax.dynamic_slice_in_dim(v, core, 1, 1)[:, 0, cut:].reshape(RING * rest, -1)
            for v in views
        ]

    def out_first(core):
        cuts = [lax.dynamic_slice_in_dim(w_down[0], spot(k, core), cut, 1) for k in range(RING)]
        return jnp.concatenate(cuts, axis=1)

    def out_last(core):
        starts = [(2 * k + core) * wide_piece + cut for k in range(RING)]
        cuts = [lax.dynamic_slice_in_dim(w_down[0], start, rest, 1) for start in starts]
        return jnp.concatenate(cuts, axis=1)

    weights = [
        in_first(at_core), in_first(away), in_last(at_core), in_last(away),
        out_first(at_core), out_first(away), out_last(at_core), out_last(away),
    ]
    homed = lax.all_to_all(homed.reshape(DP_N, tokens, columns), DP, 0, 0, tiled=True)
    homed, weights = lax.optimization_barrier((homed, weights))

    homed = homed.reshape(RING, 2, 2, tokens, columns)
    homed = lax.dynamic_slice_in_dim(jnp.concatenate([homed, homed], 0), at_x, RING, 0)
    keep = lax.dynamic_slice_in_dim(homed, at_core, 1, 1)[:, 0]
    give = lax.dynamic_slice_in_dim(homed, 1 - at_core, 1, 1)[:, 0]
    kept = keep.astype(f32) + other_core(give).astype(f32)
    attention = kept[0]
    for k in (2, 1, 3):
        attention = attention + send(kept[k].astype(bf16), "x", k).astype(f32)
    attention = jnp.concatenate([attention[0], attention[1]], axis=1)
    head_index = at_x * 2 + at_core
    near = lax.dynamic_slice_in_dim(residual, head_index * wide_piece, wide_piece, 1)
    piece = (near.astype(f32) + attention).astype(bf16)

    here = jnp.concatenate([piece] + [hop(piece, "x", k) for k in (1, 2, 3)], axis=1)
    there = other_core(here)
    ring_at = (at_x + jnp.arange(RING, dtype=i32)) % RING * 2
    spots_here, spots_there = ring_at + at_core, ring_at + 1 - at_core
    gains = jnp.concatenate([norm_gain, norm_gain]).reshape(2 * RING, 2, wide_piece)
    gains = lax.dynamic_slice(gains, (at_x, at_core, 0), (RING, 1, wide_piece)).reshape(1, -1)

    chosen = (expert_ids[:, :, None] == dps[None, None, :]).astype(i32)
    named = jnp.sum(chosen, axis=1)
    weight = jnp.sum(chosen.astype(f32) * gate_weights[:, :, None], axis=1)
    rank = jnp.sum(before(tokens)[:, :, None] * named[:, None, :], axis=0)
    rank = jnp.where(named > 0, rank, -1)
    ranks = jnp.arange(CAP, dtype=i32)
    placing = (rank.T[:, None, :] == ranks[None, :, None]).astype(bf16)
    placing = placing.reshape(DP_N * CAP, tokens)

    attended, early, late = home_rows(
        jnp.concatenate([spots_here, spots_there]), here, there, gains, placing, cut
    )

    def exchange(block):
        block = lax.all_to_all(block.reshape(DP_N, CAP, -1), DP, 0, 0, tiled=True)
        return block.reshape(DP_N * CAP, -1)

    early = exchange(early)
    early, late = lax.optimization_barrier((early, late))
    late = exchange(late)
    hops = [hop(early, "x", k) for k in (1, 2, 3)]
    early = jnp.concatenate([early] + hops, axis=1)

    early_own, early_away, late_own, late_away, out_early, give_early, out_late, give_late = weights

    def product(rows, pair):
        return jnp.dot(rows, jnp.concatenate(pair, axis=1), preferred_element_type=f32)

    units = w_gate.shape[2]
    early_there = other_core(early)
    sums = product(early, early_own)
    late, sums = lax.optimization_barrier((late, sums))
    late_there = other_core(late)
    sums = sums + product(early_there, early_away)
    sums = sums + product(late, late_own) + product(late_there, late_away)
    hidden = (jax.nn.silu(sums[:, :units]) * sums[:, units:]).astype(bf16)
    hidden = lax.optimization_barrier(hidden)

    def output(keep, give):
        give = jnp.dot(hidden, give, preferred_element_type=f32).astype(bf16)
        return (jnp.dot(hidden, keep, preferred_element_type=f32) + other_core(give).astype(f32)).astype(bf16)

    late = output(out_late, give_late)
    hidden = lax.optimization_barrier((hidden, late))[0]
    early = output(out_early, give_early)

    def ring_sum(block, size):
        total = block[:, :size].astype(f32)
        for k in (2, 1, 3):
            total = total + send(block[:, k * size : (k + 1) * size], "x", k).astype(f32)
        return total

    late = exchange(late)
    early, late = lax.optimization_barrier((ring_sum(early, cut).astype(bf16), late))
    early = exchange(early)

    mix = jnp.where(rank[:, :, None] == ranks[None, None, :], weight[:, :, None], 0.0)
    mix = mix.reshape(tokens, DP_N * CAP)
    coarse = lax.reduce_precision(mix, 8, 7)
    both = jnp.concatenate([coarse.astype(bf16), (mix - coarse).astype(bf16)], axis=0)

    def mixed(block):
        block = jnp.dot(both, block, preferred_element_type=f32)
        return block[:tokens] + block[tokens:]

    late = mixed(late).astype(bf16)
    late = lax.dynamic_slice_in_dim(
        jnp.concatenate([late, late], axis=1), at_x * rest, RING * rest, 1
    )
    late = ring_sum(late, rest)
    routed = jnp.concatenate([mixed(early), late], axis=1).astype(bf16)
    return (attended, routed)


def solution(mesh):
    grid = Mesh(mesh.devices.reshape(RING, RING, RING, 2), ALL)
    return jax.shard_map(
        shards,
        mesh=grid,
        in_specs=(
            P(DP, HEAD, None),
            P(DP, None, None),
            P(DP, None),
            P(DP),
            P(DP),
            P(HEAD, None, None),
            P(HEAD, DP),
            P(DP, None),
            P(),
            P(DP, None),
            P(DP, None),
            P(DP, None, HEAD),
            P(DP, None, HEAD),
            P(DP, HEAD, None),
        ),
        out_specs=(P(DP, None), P(DP, HEAD)),
        check_vma=False,
    )
```
